256 devices in a mesh: row: 32 (over z_hi, x, core), col: 8 (over z_lo, y).
Axes of the slice: x: 4, y: 4, z: 8 (z_hi: 4, z_lo: 2; z = z_hi * 2 + z_lo), core: 2. Of those that a mesh axis runs over, the one named last changes fastest.
Arguments:
- support: bfloat16 [16384, 256], P(('row', 'col')), may hold values from -1.5 to 1.5
- support_labels: float32 [15, 16384], P(None, ('row', 'col')), may hold values from -6 to 6
- targets: bfloat16 [65536, 256], P('col'), may hold values from -1.5 to 1.5
- target_labels: float32 [15, 65536], P(None, 'col'), may hold values from -6 to 6
Outputs:
- coefficients: float32 [15, 16384], P(None, ('row', 'col'))
- support_grad: float32 [16384, 256], P(('row', 'col'))
The draws below stay inside these ranges and needn't reach their ends.
All inputs are finite; a program needn't handle non-finite values.
Results may differ from the reference program's by a relative error of at most 0.0033.
Values may be sent and summed in bfloat16 or wider, within the bound.
A program may use at most 128 MiB of HBM per device.

```python
import math
import jax
import jax.numpy as jnp
from jax import lax

FEAT = 256
CLASSES = 15
ITERS = 3
SUPPORT = 16384
TARGETS = 65536


def shared_layout(key):
    centre_key, plane_key = jax.random.split(key, 2)
    spread = 1.0 / math.sqrt(FEAT)
    centres = jax.random.normal(centre_key, (16, FEAT), jnp.float32) * (0.85 * spread)
    planes = jax.random.normal(plane_key, (8, FEAT), jnp.float32) * spread
    return (centres, planes)


def place_states(member_key, count, centres, planes, latent, noise):
    member = jax.random.randint(member_key, (count,), 0, 16)
    states = jnp.take(centres, member, axis=0) + noise
    for index in range(8):
        states = states + latent[:, index:index + 1] * planes[index][None, :]
    return jnp.clip(states, -1.5, 1.5).astype(jnp.bfloat16)


def draw_support(key, part):
    centres, planes = shared_layout(key)
    key = jax.random.fold_in(key, 5)
    member_key, latent_key, noise_key = jax.random.split(key, 3)
    latent = jax.random.normal(latent_key, (SUPPORT, 8), jnp.float32) * 0.25
    noise = jax.random.normal(noise_key, (SUPPORT, FEAT), jnp.float32) * 0.05
    return place_states(member_key, SUPPORT, centres, planes, latent, noise)


def draw_targets(key, part):
    centres, planes = shared_layout(key)
    key = jax.random.fold_in(key, 9)
    member_key, latent_key, noise_key = jax.random.split(key, 3)
    latent = jax.random.normal(latent_key, (TARGETS, 8), jnp.float32) * 0.25
    noise = jax.random.normal(noise_key, (TARGETS, FEAT), jnp.float32) * 0.05
    return place_states(member_key, TARGETS, centres, planes, latent, noise)


def block_levels(key, dims, pieces, least, top_value):
    loudness, own = 1.0, jax.random.fold_in(key, 6)
    for axis_at, shards_of in pieces:
        draws = jnp.exp(jax.random.uniform(jax.random.fold_in(own, axis_at), (shards_of,), jnp.float32, least / len(pieces), top_value / len(pieces)))
        loudness = loudness * jnp.repeat(draws, dims[axis_at] // shards_of).reshape([-1 if axis == axis_at else 1 for axis in range(len(dims))])
    return loudness


def scatter_about(stream_key, dims, deviation, most, pieces=(), kind=jnp.bfloat16):
    level = block_levels(stream_key, dims, pieces, -0.22, 0.18) if pieces else 1.0
    array = jax.random.normal(stream_key, dims, jnp.float32) * deviation * level
    return jnp.minimum(jnp.maximum(array, -most), most).astype(kind)


def setup_inputs(seed: int = 0) -> dict:
    streams_of = jax.random.split(jax.random.key(seed), 5)
    support = draw_support(jax.random.fold_in(streams_of[4], 71), 0)
    support_labels = scatter_about(streams_of[1], (CLASSES, SUPPORT), 1.0, 6.0, ((1, 256),), jnp.float32)
    targets = draw_targets(jax.random.fold_in(streams_of[4], 71), 0)
    target_labels = scatter_about(streams_of[3], (CLASSES, TARGETS), 1.0, 6.0, ((1, 8),), jnp.float32)
    return {"support": support, "support_labels": support_labels, "targets": targets, "target_labels": target_labels}


ridge = 0.5

def kernel_block(left, right):
    inner = jnp.dot(left, right.T, preferred_element_type=jnp.float32)
    left_norm = lax.optimization_barrier(jnp.sum(jnp.square(left.astype(jnp.float32)), axis=1))
    right_norm = lax.optimization_barrier(jnp.sum(jnp.square(right.astype(jnp.float32)), axis=1))
    return jnp.exp(inner - 0.5 * left_norm[:, None] - 0.5 * right_norm[None, :])

def contract_last(left, right):
    return lax.dot_general(left, right, (((1,), (1,)), ((), ())), precision=lax.Precision.HIGHEST)

def apply_system(support, direction):
    total = support.shape[0]
    width = math.gcd(total, 1024)
    blocks = support.reshape(total // width, width, support.shape[1])

    def one_block(rows):
        return contract_last(direction, kernel_block(rows, support))
    image = jnp.transpose(lax.map(one_block, blocks), (1, 0, 2)).reshape(direction.shape)
    return image + ridge * direction

def reference(support, support_labels, targets, target_labels):
    solution = jnp.zeros_like(support_labels)
    residual = support_labels
    direction = support_labels
    norm_now = lax.optimization_barrier(jnp.sum(residual * residual, axis=1, keepdims=True))
    for step in range(ITERS):
        image = apply_system(support, direction)
        alpha = norm_now / lax.optimization_barrier(jnp.sum(direction * image, axis=1, keepdims=True))
        solution = solution + alpha * direction
        residual = residual - alpha * image
        norm_next = lax.optimization_barrier(jnp.sum(residual * residual, axis=1, keepdims=True))
        direction = residual + norm_next / norm_now * direction
        norm_now = norm_next
    count = targets.shape[0]
    width = math.gcd(count, 1024)
    target_blocks = targets.reshape(count // width, width, targets.shape[1])

    def predict(rows):
        return contract_last(solution, kernel_block(rows, support))
    predictions = jnp.transpose(lax.map(predict, target_blocks), (1, 0, 2)).reshape(target_labels.shape)
    errors = predictions - target_labels
    error_blocks = jnp.transpose(errors.reshape(errors.shape[0], count // width, width), (1, 0, 2))

    def accumulate(carry, item):
        summed, column_sums = carry
        rows, error_rows = item
        values = kernel_block(rows, support)
        mixing = lax.dot_general(error_rows, solution, (((0,), (0,)), ((), ())), precision=lax.Precision.HIGHEST)
        weights = (mixing * values).astype(jnp.bfloat16)
        summed = summed + lax.dot_general(weights, rows, (((0,), (0,)), ((), ())), preferred_element_type=jnp.float32)
        column_sums = column_sums + lax.optimization_barrier(jnp.sum(weights.astype(jnp.float32), axis=0))
        return ((summed, column_sums), None)
    initial = (jnp.zeros(support.shape, jnp.float32), jnp.zeros((support.shape[0],), jnp.float32))
    (summed, column_sums), unused = lax.scan(accumulate, initial, (target_blocks, error_blocks))
    gradient = (summed - column_sums[:, None] * support.astype(jnp.float32)) / jnp.sqrt(jnp.float32(count))
    return (solution, gradient)
```

```python
import jax
import jax.numpy as jnp
from jax import lax
from jax.experimental import pallas as pl
from jax.experimental.pallas import tpu as pltpu
from jax.sharding import PartitionSpec as P

MESH = pl.DeviceIdType.MESH
F32 = jnp.float32
BF16 = jnp.bfloat16

CHUNK = 64
FEAT = 256
TILE = 256
TILES = 32
GROUP = 16
WIDE = GROUP * CHUNK
HALF = WIDE // 2
RIDGE = 0.5
NN = (((1,), (0,)), ((), ()))
NT = (((1,), (1,)), ((), ()))


def dot(a, b, dims=NN):
    return lax.dot_general(a, b, dims, preferred_element_type=F32)


def split3(v):
    hi = v.astype(BF16)
    rest = v - hi.astype(F32)
    mid = rest.astype(BF16)
    low = (rest - mid.astype(F32)).astype(BF16)
    return hi, mid, low


def row_norms(rows):
    square = jnp.square(rows.astype(F32))
    hi = square.astype(BF16)
    low = (square - hi.astype(F32)).astype(BF16)
    ones = jnp.ones((8, FEAT), BF16)
    return 0.5 * (dot(ones, hi, NT) + dot(ones, low, NT))[0:1, :]


def column_norms(rows):
    return 0.5 * jnp.sum(jnp.square(rows.astype(F32)), axis=1, keepdims=True)


def pack_pair(v):
    left = lax.broadcasted_iota(jnp.int32, (8, 128), 1) < CHUNK
    top, bottom = v[0:8], v[8:16]
    first = jnp.where(left, top, pltpu.roll(bottom, CHUNK, 1))
    second = jnp.where(left, pltpu.roll(top, CHUNK, 1), bottom)
    return first, second


def unpack_pair(a, b):
    left = lax.broadcasted_iota(jnp.int32, (8, 128), 1) < CHUNK
    top = jnp.where(left, a, pltpu.roll(b, CHUNK, 1))
    bottom = jnp.where(left, pltpu.roll(a, CHUNK, 1), b)
    return jnp.concatenate([top, bottom], axis=0)


def unpack(ref):
    wide = jnp.concatenate([unpack_pair(ref[2 * j], ref[2 * j + 1]) for j in range(GROUP // 2)], axis=1)
    return jnp.where(lax.broadcasted_iota(jnp.int32, wide.shape, 0) < 15, wide, 0.0)


def to_lanes(q, shift):
    sub = lax.broadcasted_iota(jnp.int32, (16, 128), 0)
    lane = lax.broadcasted_iota(jnp.int32, (16, 128), 1)
    return jnp.sum(jnp.where(lane == sub + shift, q, 0.0), axis=0, keepdims=True)


def from_lanes(row, shift):
    sub = lax.broadcasted_iota(jnp.int32, (16, 128), 0)
    lane = lax.broadcasted_iota(jnp.int32, (16, 128), 1)
    return jnp.sum(jnp.where(lane == sub + shift, row, 0.0), axis=1, keepdims=True)


def put_scalars(message, row):
    sub = lax.broadcasted_iota(jnp.int32, (8, 128), 0)
    lane = lax.broadcasted_iota(jnp.int32, (8, 128), 1)
    return jnp.where((sub == 7) & (lane >= CHUNK), row, message)


def lane_sum(v):
    return jnp.sum(v, axis=1, keepdims=True)


def ratio(a, b):
    real = lax.broadcasted_iota(jnp.int32, (16, 1), 0) < 15
    return jnp.where(real, a, 0.0) / jnp.where(real, b, 1.0)


def tree(values):
    values = list(values)
    while len(values) > 1:
        values = [values[i] + values[i + 1] if i + 1 < len(values) else values[i] for i in range(0, len(values), 2)]
    return values[0]


def kernel(
    sup_ref, lab_ref, tgt_hbm, tlab_hbm,
    coef_ref, grad_ref,
    tgt, tlab, rf, cf, sup_v, lab_rows, lab_cols,
    kt_hi, kt_lo, kk_hi, kk_lo, sn_ref,
    s1_send, s1_recv, s2_send, s2_rows, s2_cols, s3_send, s3_recv,
    drow, rrow, xrow, dcol, rcol, prev,
    pred_send, pred_recv, err_own, err, xt, gsum, csum, g_send, g_recv,
    local_sems, f_send, f_recv, l_send, l_recv, v_send, v_recv, pred_ss, pred_rs, err_ss, err_rs, g_ss, g_rs,
):
    r = lax.axis_index("row")
    c = lax.axis_index("col")
    chip, core = r // 2, lax.rem(r, 2)
    z, x = chip // 4, lax.rem(chip, 4)
    me = core * 8 + c

    def row_peer(i):
        p = lax.rem(me + i, GROUP)
        return (2 * chip + p // 8, lax.rem(p, 8))

    def col_peer(i):
        return (2 * lax.rem(chip + i, GROUP) + core, c)

    tgt_copy = pltpu.make_async_copy(tgt_hbm, tgt, local_sems.at[0])
    tgt_copy.start()
    start_lane = pl.multiple_of(r * TILE, TILE)
    tlab_copy = pltpu.make_async_copy(tlab_hbm.at[:, pl.ds(start_lane, TILE)], tlab, local_sems.at[1])
    tlab_copy.start()

    barrier = pltpu.get_barrier_semaphore()

    @pl.loop(1, GROUP)
    def _(i):
        pl.semaphore_signal(barrier, inc=1, device_id=row_peer(i), device_id_type=MESH)

    @pl.loop(1, 32)
    def _(i):
        q = lax.rem(r + i, 32)

        @pl.when(q // 2 != chip)
        def _():
            pl.semaphore_signal(barrier, inc=1, device_id=(q, c), device_id_type=MESH)

    sup = sup_ref[...]
    rf[me] = sup
    cf[chip] = sup
    sup_v[...] = sup
    lab = jnp.concatenate([lab_ref[...], jnp.zeros((1, CHUNK), F32)], axis=0)
    packed = jnp.concatenate([lab[0:8], lab[8:16]], axis=1)
    s2_send[0] = packed
    lab_rows[me] = packed
    lab_cols[chip] = packed

    pl.semaphore_wait(barrier, 45)

    def remote(src, dst, ss, rs, to):
        return pltpu.make_async_remote_copy(
            src_ref=src, dst_ref=dst, send_sem=ss, recv_sem=rs, device_id=to, device_id_type=MESH
        )

    def wait_for(ref, sem):
        pltpu.make_async_copy(ref, ref, sem).wait()

    @pl.loop(1, GROUP)
    def _(i):
        remote(sup_v, rf.at[me], f_send.at[0], f_recv.at[0], row_peer(i)).start()

    @pl.loop(1, 4)
    def _(i):
        remote(sup_v, cf.at[chip], f_send.at[1], f_recv.at[1], (2 * (lax.rem(z + i, 4) * 4 + x) + core, c)).start()

    @pl.loop(1, GROUP)
    def _(i):
        remote(s2_send.at[0], lab_rows.at[me], l_send.at[0], l_recv.at[0], row_peer(i)).start()
        remote(s2_send.at[0], lab_cols.at[chip], l_send.at[1], l_recv.at[1], col_peer(i)).start()

    wait_for(cf.at[pl.ds(0, 3)], f_recv.at[1])

    @pl.loop(1, 4)
    def _(i):
        to = (2 * (z * 4 + lax.rem(x + i, 4)) + core, c)

        @pl.loop(0, 4)
        def _(j):
            remote(cf.at[j * 4 + x], cf.at[j * 4 + x], f_send.at[2], f_recv.at[2], to).start()

    wait_for(rf.at[pl.ds(0, 15)], f_recv.at[0])
    tgt_copy.wait()
    rows512 = rf[pl.ds(core * 8, 8)].reshape(HALF, FEAT)
    sn_ref[...] = column_norms(rows512)

    def target_tile(i):
        rows = tgt[i]
        inner = dot(rf[pl.ds(core * 8, 8)].reshape(HALF, FEAT), rows, NT)
        value = jnp.exp(inner - sn_ref[...] - row_norms(rows))
        hi = value.astype(BF16)
        kk_hi[i] = hi
        kk_lo[i] = (value - hi.astype(F32)).astype(BF16)

    done = [0]

    def fill(count):
        stop = min(TILES, done[0] + count)
        if stop > done[0]:
            pl.loop(done[0], stop)(target_tile)
        done[0] = stop

    fill(10)

    wait_for(cf.at[pl.ds(0, 12)], f_recv.at[2])
    rows_all = rf[...].reshape(WIDE, FEAT)
    prev[0:1, :] = row_norms(rows_all)

    @pl.loop(0, 4)
    def _(j):
        part = cf[pl.ds(j * 4, 4)].reshape(TILE, FEAT)
        inner = dot(part, rf[...].reshape(WIDE, FEAT), NT)
        value = jnp.exp(inner - column_norms(part) - prev[0:1, :])
        hi = value.astype(BF16)
        where = pl.ds(pl.multiple_of(j * TILE, TILE), TILE)
        kt_hi[where, :] = hi
        kt_lo[where, :] = (value - hi.astype(F32)).astype(BF16)

    def apply_tile(v):
        hi, mid, low = split3(v)
        big = dot(jnp.concatenate([hi, mid, low], axis=0), kt_hi[...])
        small = dot(jnp.concatenate([hi, mid], axis=0), kt_lo[...])
        return (big[0:16] + small[0:16]) + ((big[16:32] + small[16:32]) + big[32:48])

    wait_for(lab_rows.at[pl.ds(0, 15)], l_recv.at[0])
    wait_for(lab_cols.at[pl.ds(0, 15)], l_recv.at[1])
    b_rows = unpack(lab_rows)
    b_cols = unpack(lab_cols)
    drow[...] = b_rows
    rrow[...] = b_rows
    xrow[...] = jnp.zeros_like(b_rows)
    dcol[...] = b_cols
    rcol[...] = b_cols
    rr = None

    waits = ((4, 4), (4, 4), (3, 3))
    for step in range(3):
        last = step == 2
        applied = apply_tile(rcol[...])
        if step > 0:
            wait_for(s3_recv.at[step - 1, pl.ds(0, 15)], v_recv.at[step - 1, 3])
            new = from_lanes(tree([s3_recv[step - 1, j] for j in range(GROUP)])[7:8], CHUNK)
            beta = ratio(new, rr)
            rr = new
            applied = applied + beta * prev[...]
            drow[...] = rrow[...] + beta * drow[...]
            dcol[...] = rcol[...] + beta * dcol[...]
        prev[...] = applied
        d = drow[...]
        scalars = to_lanes(lane_sum(d * (applied + (RIDGE / GROUP) * d)), CHUNK)
        if step == 0:
            scalars = scalars + to_lanes(lane_sum(d * d) * (1.0 / GROUP), CHUNK + 16)
        if last:
            s1_send[step, 0] = put_scalars(jnp.zeros((8, 128), F32), scalars)
            s1_recv[step, me] = s1_send[step, 0]

            @pl.loop(1, GROUP)
            def _(i):
                remote(s1_send.at[step, 0], s1_recv.at[step, me], v_send.at[step, 0], v_recv.at[step, 0], row_peer(i)).start()
        else:
            for j in range(GROUP // 2):
                first, second = pack_pair(applied[:, 128 * j:128 * (j + 1)])
                s1_send[step, 2 * j] = put_scalars(first, scalars)
                s1_send[step, 2 * j + 1] = put_scalars(second, scalars)
            s1_recv[step, me] = s1_send[step, me]

            @pl.loop(1, GROUP)
            def _(i):
                p = lax.rem(me + i, GROUP)
                remote(s1_send.at[step, p], s1_recv.at[step, me], v_send.at[step, 0], v_recv.at[step, 0], row_peer(i)).start()

        fill(waits[step][0])
        wait_for(s1_recv.at[step, pl.ds(0, 15)], v_recv.at[step, 0])
        own = tree([s1_recv[step, j] for j in range(GROUP)])
        s2_send[1 + step] = own
        s2_cols[step, chip] = own
        if not last:
            s2_rows[step, me] = own

        @pl.loop(1, GROUP)
        def _(i):
            remote(s2_send.at[1 + step], s2_cols.at[step, chip], v_send.at[step, 1], v_recv.at[step, 1], col_peer(i)).start()
            if not last:
                remote(s2_send.at[1 + step], s2_rows.at[step, me], v_send.at[step, 2], v_recv.at[step, 2], row_peer(i)).start()

        fill(waits[step][1])
        wait_for(s2_cols.at[step, pl.ds(0, 15)], v_recv.at[step, 1])
        total = tree([s2_cols[step, j] for j in range(GROUP)])[7:8]
        if step == 0:
            rr = from_lanes(total, CHUNK + 16)
        alpha = ratio(rr, from_lanes(total, CHUNK))
        xrow[...] = xrow[...] + alpha * drow[...]
        if not last:
            y_cols = unpack(s2_cols.at[step]) + RIDGE * dcol[...]
            left = rcol[...] - alpha * y_cols
            rcol[...] = left
            s3_send[step] = put_scalars(jnp.zeros((8, 128), F32), to_lanes(lane_sum(left * left), CHUNK))
            s3_recv[step, me] = s3_send[step]

            @pl.loop(1, GROUP)
            def _(i):
                remote(s3_send.at[step], s3_recv.at[step, me], v_send.at[step, 3], v_recv.at[step, 3], row_peer(i)).start()

            wait_for(s2_rows.at[step, pl.ds(0, 15)], v_recv.at[step, 2])
            rrow[...] = rrow[...] - alpha * (unpack(s2_rows.at[step]) + RIDGE * drow[...])

    fill(TILES)

    pair = xrow[:, pl.ds(pl.multiple_of((me // 2) * 128, 128), 128)]
    own_x = jnp.where(lax.rem(me, 2) == 0, pair, pltpu.roll(pair, CHUNK, 1))
    coef_ref[...] = own_x[0:15, 0:CHUNK]

    x512 = xrow[:, pl.ds(pl.multiple_of(core * HALF, HALF), HALF)]
    hi, mid, low = split3(x512)
    x48 = jnp.concatenate([hi, mid, low], axis=0)
    x32 = jnp.concatenate([hi, mid], axis=0)
    wide = jnp.concatenate([hi.astype(F32), mid.astype(F32), jnp.zeros((96, HALF), F32)], axis=0)
    xt[...] = wide.T[:, 0:32].astype(BF16)

    def predict(i):
        big = dot(x48, kk_hi[i])
        small = dot(x32, kk_lo[i])
        return (big[0:16] + small[0:16]) + ((big[16:32] + small[16:32]) + big[32:48])

    @pl.loop(1, TILES)
    def _(i):
        t = lax.rem(r + i, TILES)
        pred_send[t] = predict(t)
        remote(pred_send.at[t], pred_recv.at[r], pred_ss, pred_rs, (t, c)).start()

    pred_recv[r] = predict(r)
    tlab_copy.wait()
    wait_for(pred_recv.at[pl.ds(0, 31)], pred_rs)
    labels = jnp.concatenate([tlab[...], jnp.zeros((1, TILE), F32)], axis=0)
    own_err = (tree([pred_recv[j] for j in range(TILES)]) - labels).astype(BF16)
    err_own[...] = own_err
    err[r] = own_err

    @pl.loop(1, TILES)
    def _(i):
        t = lax.rem(r + i, TILES)
        remote(err_own, err.at[r], err_ss, err_rs.at[r], (t, c)).start()

    gsum[...] = jnp.zeros_like(gsum)
    csum[...] = jnp.zeros_like(csum)

    def accumulate(t):
        e = err[t]
        mix = dot(xt[...], jnp.concatenate([e, e], axis=0))
        weights = (mix * kk_hi[t].astype(F32)).astype(BF16)
        gsum[...] += dot(weights, tgt[t])
        back = weights.astype(F32)
        csum[...] += back[:, 0:128] + back[:, 128:256]

    accumulate(r)

    @pl.loop(1, TILES)
    def _(i):
        t = lax.rem(r + TILES - i, TILES)
        wait_for(err.at[t], err_rs.at[t])
        accumulate(t)

    scale = 1.0 / 256.0
    sums = lane_sum(csum[...])
    term = (gsum[...] - sums * rf[pl.ds(core * 8, 8)].reshape(HALF, FEAT).astype(F32)) * scale
    g_send[...] = term.reshape(8, CHUNK, FEAT)
    g_recv[c] = g_send[c]

    @pl.loop(1, 8)
    def _(i):
        p = lax.rem(c + i, 8)
        remote(g_send.at[p], g_recv.at[c], g_ss, g_rs, (r, p)).start()

    wait_for(g_recv.at[pl.ds(0, 7)], g_rs)
    grad_ref[...] = tree([g_recv[j] for j in range(8)])

    wait_for(rf.at[pl.ds(0, 15)], f_send.at[0])
    wait_for(cf.at[pl.ds(0, 3)], f_send.at[1])
    wait_for(cf.at[pl.ds(0, 12)], f_send.at[2])
    wait_for(lab_rows.at[pl.ds(0, 15)], l_send.at[0])
    wait_for(lab_cols.at[pl.ds(0, 15)], l_send.at[1])
    for step in range(3):
        wait_for(s1_recv.at[step, pl.ds(0, 15)], v_send.at[step, 0])
        wait_for(s2_cols.at[step, pl.ds(0, 15)], v_send.at[step, 1])
        if step < 2:
            wait_for(s2_rows.at[step, pl.ds(0, 15)], v_send.at[step, 2])
            wait_for(s3_recv.at[step, pl.ds(0, 15)], v_send.at[step, 3])
    wait_for(pred_recv.at[pl.ds(0, 31)], pred_ss)
    wait_for(err.at[pl.ds(0, 31)], err_ss)
    wait_for(g_recv.at[pl.ds(0, 7)], g_ss)


def body(support, support_labels, targets, target_labels):
    classes = support_labels.shape[0]
    vmem = pl.BlockSpec(memory_space=pltpu.VMEM)
    anywhere = pl.BlockSpec(memory_space=pl.ANY)
    dma = pltpu.SemaphoreType.DMA
    return pl.pallas_call(
        kernel,
        out_shape=(
            jax.ShapeDtypeStruct((classes, CHUNK), F32),
            jax.ShapeDtypeStruct((CHUNK, FEAT), F32),
        ),
        in_specs=[vmem, vmem, anywhere, anywhere],
        out_specs=(vmem, vmem),
        scratch_shapes=[
            pltpu.VMEM((TILES, TILE, FEAT), BF16),
            pltpu.VMEM((classes, TILE), F32),
            pltpu.VMEM((GROUP, CHUNK, FEAT), BF16),
            pltpu.VMEM((GROUP, CHUNK, FEAT), BF16),
            pltpu.VMEM((CHUNK, FEAT), BF16),
            pltpu.VMEM((GROUP, 8, 128), F32),
            pltpu.VMEM((GROUP, 8, 128), F32),
            pltpu.VMEM((WIDE, WIDE), BF16),
            pltpu.VMEM((WIDE, WIDE), BF16),
            pltpu.VMEM((TILES, HALF, TILE), BF16),
            pltpu.VMEM((TILES, HALF, TILE), BF16),
            pltpu.VMEM((HALF, 1), F32),
            pltpu.VMEM((3, GROUP, 8, 128), F32),
            pltpu.VMEM((3, GROUP, 8, 128), F32),
            pltpu.VMEM((4, 8, 128), F32),
            pltpu.VMEM((2, GROUP, 8, 128), F32),
            pltpu.VMEM((3, GROUP, 8, 128), F32),
            pltpu.VMEM((2, 8, 128), F32),
            pltpu.VMEM((2, GROUP, 8, 128), F32),
            pltpu.VMEM((GROUP, WIDE), F32),
            pltpu.VMEM((GROUP, WIDE), F32),
            pltpu.VMEM((GROUP, WIDE), F32),
            pltpu.VMEM((GROUP, WIDE), F32),
            pltpu.VMEM((GROUP, WIDE), F32),
            pltpu.VMEM((GROUP, WIDE), F32),
            pltpu.VMEM((TILES, GROUP, TILE), F32),
            pltpu.VMEM((TILES, GROUP, TILE), F32),
            pltpu.VMEM((GROUP, TILE), BF16),
            pltpu.VMEM((TILES, GROUP, TILE), BF16),
            pltpu.VMEM((HALF, 32), BF16),
            pltpu.VMEM((HALF, FEAT), F32),
            pltpu.VMEM((HALF, 128), F32),
            pltpu.VMEM((8, CHUNK, FEAT), F32),
            pltpu.VMEM((8, CHUNK, FEAT), F32),
            dma((2,)),
            dma((3,)),
            dma((3,)),
            dma((2,)),
            dma((2,)),
            dma((3, 4)),
            dma((3, 4)),
            dma,
            dma,
            dma,
            dma((TILES,)),
            dma,
            dma,
        ],
        compiler_params=pltpu.CompilerParams(
            collective_id=0, has_side_effects=True, vmem_limit_bytes=58 * 1024 * 1024
        ),
    )(support, support_labels, targets.reshape(TILES, TILE, FEAT), target_labels)


def solution(mesh):
    in_specs = (P(("row", "col"), None), P(None, ("row", "col")), P("col", None), P(None, "col"))
    out_specs = (P(None, ("row", "col")), P(("row", "col"), None))
    return jax.shard_map(body, mesh=mesh, in_specs=in_specs, out_specs=out_specs, check_vma=False)
```

```python
import jax
import jax.numpy as jnp
from jax import lax
from jax.experimental import pallas as pl
from jax.experimental.pallas import tpu as pltpu
from jax.sharding import PartitionSpec as P

MESH = pl.DeviceIdType.MESH
F32 = jnp.float32
BF16 = jnp.bfloat16

CHUNK = 64
FEAT = 256
TILE = 256
TILES = 32
GROUP = 16
WIDE = GROUP * CHUNK
HALF = WIDE // 2
RIDGE = 0.5
UNIT = CHUNK + 16
NN = (((1,), (0,)), ((), ()))
NT = (((1,), (1,)), ((), ()))


def dot(a, b, dims=NN):
    return lax.dot_general(a, b, dims, preferred_element_type=F32)


def split3(v):
    hi = v.astype(BF16)
    rest = v - hi.astype(F32)
    mid = rest.astype(BF16)
    low = (rest - mid.astype(F32)).astype(BF16)
    return hi, mid, low


def row_norms(rows):
    square = jnp.square(rows.astype(F32))
    hi = square.astype(BF16)
    low = (square - hi.astype(F32)).astype(BF16)
    ones = jnp.ones((8, FEAT), BF16)
    return 0.5 * (dot(ones, hi, NT) + dot(ones, low, NT))[0:1, :]


def column_norms(rows):
    return 0.5 * jnp.sum(jnp.square(rows.astype(F32)), axis=1, keepdims=True)


def pack_pair(v):
    left = lax.broadcasted_iota(jnp.int32, (8, 128), 1) < CHUNK
    top, bottom = v[0:8], v[8:16]
    first = jnp.where(left, top, pltpu.roll(bottom, CHUNK, 1))
    second = jnp.where(left, pltpu.roll(top, CHUNK, 1), bottom)
    return first, second


def unpack_pair(a, b):
    left = lax.broadcasted_iota(jnp.int32, (8, 128), 1) < CHUNK
    top = jnp.where(left, a, pltpu.roll(b, CHUNK, 1))
    bottom = jnp.where(left, pltpu.roll(a, CHUNK, 1), b)
    return jnp.concatenate([top, bottom], axis=0)


def unpack(ref):
    wide = jnp.concatenate([unpack_pair(ref[2 * j], ref[2 * j + 1]) for j in range(GROUP // 2)], axis=1)
    return jnp.where(lax.broadcasted_iota(jnp.int32, wide.shape, 0) < 15, wide, 0.0)


def label_rows(labels):
    hi, mid, low = split3(labels)
    parts = [hi.astype(F32), mid.astype(F32), low.astype(F32), jnp.zeros((16, CHUNK), F32)]
    return jnp.concatenate(parts, axis=1).astype(BF16)


def labels_of(ref):
    left = lax.broadcasted_iota(jnp.int32, (16, 128), 1) < CHUNK
    whole = []
    for j in range(GROUP):
        block = ref[j, CHUNK:UNIT, :].astype(F32)
        a, b = block[:, 0:128], block[:, 128:256]
        whole.append((a + pltpu.roll(a, CHUNK, 1)) + (b + pltpu.roll(b, CHUNK, 1)))
    return jnp.concatenate([jnp.where(left, whole[2 * j], whole[2 * j + 1]) for j in range(GROUP // 2)], axis=1)


def gray(j):
    return j + (j // 2) * (5 - 2 * j)


def to_lanes(q, shift):
    sub = lax.broadcasted_iota(jnp.int32, (16, 128), 0)
    lane = lax.broadcasted_iota(jnp.int32, (16, 128), 1)
    return jnp.sum(jnp.where(lane == sub + shift, q, 0.0), axis=0, keepdims=True)


def from_lanes(row, shift):
    sub = lax.broadcasted_iota(jnp.int32, (16, 128), 0)
    lane = lax.broadcasted_iota(jnp.int32, (16, 128), 1)
    return jnp.sum(jnp.where(lane == sub + shift, row, 0.0), axis=1, keepdims=True)


def put_scalars(message, row):
    sub = lax.broadcasted_iota(jnp.int32, (8, 128), 0)
    lane = lax.broadcasted_iota(jnp.int32, (8, 128), 1)
    return jnp.where((sub == 7) & (lane >= CHUNK), row, message)


def lane_sum(v):
    return jnp.sum(v, axis=1, keepdims=True)


def ratio(a, b):
    real = lax.broadcasted_iota(jnp.int32, (16, 1), 0) < 15
    return jnp.where(real, a, 0.0) / jnp.where(real, b, 1.0)


def tree(values):
    values = list(values)
    while len(values) > 1:
        values = [values[i] + values[i + 1] if i + 1 < len(values) else values[i] for i in range(0, len(values), 2)]
    return values[0]


def kernel(
    sup_ref, lab_ref, tgt_hbm, tlab_hbm,
    coef_ref, grad_ref,
    tgt, tlab, unit, rf, cf, rows_all, rn_ref, sn_ref,
    kt_hi, kt_lo, kk_hi, kk_lo,
    s1_send, s1_recv, s2_send, s2_rows, s2_cols, s3_send, s3_recv,
    drow, rrow, xrow, dcol, rcol, prev,
    both, sib_send, sib_recv, pred_send, pred_recv, err_own, err, xt, gsum, csum, g_send, g_recv,
    local_sems, f_send, z_recv, x_recv, r_recv, b_recv, v_send, v_recv,
    sib_ss, sib_rs, pred_ss, pred_rs, err_ss, err_rs, g_ss, g_rs,
):
    r = lax.axis_index("row")
    c = lax.axis_index("col")
    chip, core = r // 2, lax.rem(r, 2)
    z, x = chip // 4, lax.rem(chip, 4)
    zl, y = c // 4, lax.rem(c, 4)
    me = core * 8 + c
    here = x * 4 + z

    def row_peer(j):
        k = lax.rem(core + j % 2, 2)
        p = lax.rem(zl + j // 8, 2) * 4 + lax.rem(y + gray((j // 2) % 4), 4)
        return k * 8 + p, (2 * chip + k, p)

    def chip_at(j):
        return lax.rem(z + gray(j // 4), 4), lax.rem(x + gray(j % 4), 4)

    def col_peer(j):
        pz, px = chip_at(j)
        return (2 * (pz * 4 + px) + core, c)

    def tile_at(j):
        pz, px = chip_at(j // 2)
        return 2 * (pz * 4 + px) + lax.rem(core + j % 2, 2)

    def far_first(count, act):
        @pl.loop(0, count - 1)
        def _(i):
            act(count - 1 - i)

    tgt_copy = pltpu.make_async_copy(tgt_hbm, tgt, local_sems.at[0])
    tgt_copy.start()
    start_lane = pl.multiple_of(r * TILE, TILE)
    tlab_copy = pltpu.make_async_copy(tlab_hbm.at[:, pl.ds(start_lane, TILE)], tlab, local_sems.at[1])
    tlab_copy.start()

    barrier = pltpu.get_barrier_semaphore()

    def greet_row(j):
        pl.semaphore_signal(barrier, inc=1, device_id=row_peer(j)[1], device_id_type=MESH)

    def greet_col(j):
        pl.semaphore_signal(barrier, inc=1, device_id=(tile_at(j), c), device_id_type=MESH)

    far_first(32, lambda j: pl.when(j > 1)(lambda: greet_col(j)))
    far_first(GROUP, greet_row)

    lab = jnp.concatenate([lab_ref[...], jnp.zeros((1, CHUNK), F32)], axis=0)
    unit[0:CHUNK, :] = sup_ref[...]
    unit[CHUNK:UNIT, :] = label_rows(lab)
    rf[me] = unit[...]
    cf[here] = unit[...]

    pl.semaphore_wait(barrier, 45)

    drains = []

    def remote(src, dst, ss, rs, to):
        return pltpu.make_async_remote_copy(
            src_ref=src, dst_ref=dst, send_sem=ss, recv_sem=rs, device_id=to, device_id_type=MESH
        )

    def wait_for(ref, sem):
        pltpu.make_async_copy(ref, ref, sem).wait()

    def device(pz, px):
        return (2 * (pz * 4 + px) + core, c)

    @pl.loop(0, 3)
    def _(i):
        to = device(lax.rem(z + gray(3 - i), 4), x)
        remote(unit, cf.at[here], f_send.at[0], z_recv.at[z], to).start()

    @pl.loop(0, 7)
    def _(i):
        j = 7 - i
        p = lax.rem(zl + j // 4, 2) * 4 + lax.rem(y + gray(j % 4), 4)
        remote(unit, rf.at[me], f_send.at[1], r_recv, (r, p)).start()

    def to_x(pz):
        @pl.loop(0, 3)
        def _(i):
            slot = x * 4 + pz
            remote(cf.at[slot], cf.at[slot], f_send.at[2], x_recv.at[x], device(z, lax.rem(x + gray(3 - i), 4))).start()

    to_x(z)

    @pl.loop(1, 4)
    def _(i):
        pz = lax.rem(z + gray(i), 4)
        wait_for(cf.at[0], z_recv.at[pz])
        to_x(pz)

    wait_for(rf.at[pl.ds(0, 7)], r_recv)
    block = pl.ds(core * 8, 8)
    other = 2 * chip + 1 - core
    remote(rf.at[block], rf.at[block], f_send.at[3], b_recv, (other, c)).start()
    drains.append((cf.at[pl.ds(0, 3)], f_send.at[0]))
    drains.append((rf.at[pl.ds(0, 7)], f_send.at[1]))
    drains.append((cf.at[pl.ds(0, 12)], f_send.at[2]))
    drains.append((rf.at[pl.ds(0, 8)], f_send.at[3]))

    half = pl.ds(pl.multiple_of(core * HALF, HALF), HALF)
    mine = rf[block][:, 0:CHUNK, :].reshape(HALF, FEAT)
    rows_all[half, :] = mine
    sn_ref[...] = column_norms(mine)
    tgt_copy.wait()

    def target_tile(i):
        rows = tgt[i]
        inner = dot(rows_all[half, :], rows, NT)
        value = jnp.exp(inner - sn_ref[...] - row_norms(rows))
        hi = value.astype(BF16)
        kk_hi[i] = hi
        kk_lo[i] = (value - hi.astype(F32)).astype(BF16)

    done = [0]

    def fill(count):
        stop = min(TILES, done[0] + count)
        if stop > done[0]:
            pl.loop(done[0], stop)(target_tile)
        done[0] = stop

    fill(10)

    wait_for(rf.at[pl.ds(0, 8)], b_recv)
    theirs = rf[pl.ds(8 - core * 8, 8)][:, 0:CHUNK, :].reshape(HALF, FEAT)
    rows_all[pl.ds(pl.multiple_of(HALF - core * HALF, HALF), HALF), :] = theirs
    rn_ref[...] = row_norms(rows_all[...])

    @pl.loop(0, 4)
    def _(i):
        px = lax.rem(x + gray(i), 4)

        @pl.when(i > 0)
        def _():
            wait_for(cf.at[pl.ds(0, 4)], x_recv.at[px])

        part = cf[pl.ds(px * 4, 4)][:, 0:CHUNK, :].reshape(TILE, FEAT)
        inner = dot(part, rows_all[...], NT)
        value = jnp.exp(inner - column_norms(part) - rn_ref[...])
        hi = value.astype(BF16)
        where = pl.ds(pl.multiple_of(px * TILE, TILE), TILE)
        kt_hi[where, :] = hi
        kt_lo[where, :] = (value - hi.astype(F32)).astype(BF16)

    def apply_tile(v):
        hi, mid, low = split3(v)
        big = dot(jnp.concatenate([hi, mid, low], axis=0), kt_hi[...])
        small = dot(jnp.concatenate([hi, mid], axis=0), kt_lo[...])
        return (big[0:16] + small[0:16]) + ((big[16:32] + small[16:32]) + big[32:48])

    b_rows = labels_of(rf)
    b_cols = labels_of(cf)
    drow[...] = b_rows
    rrow[...] = b_rows
    xrow[...] = jnp.zeros_like(b_rows)
    dcol[...] = b_cols
    rcol[...] = b_cols
    rr = None

    def predict_tiles(first, last):
        hi, mid, low = split3(xrow[:, half])
        hi2, mid2, low2 = split3(drow[:, half])
        three = jnp.concatenate([hi, hi2, mid, mid2, low, low2], axis=0)
        two = jnp.concatenate([hi, hi2, mid, mid2], axis=0)

        @pl.loop(first, last)
        def _(i):
            big = dot(three, kk_hi[i])
            small = dot(two, kk_lo[i])
            both[i] = (big[0:32] + small[0:32]) + ((big[32:64] + small[32:64]) + big[64:96])

    waits = ((5, 8), (5, 4))
    for step in range(3):
        last = step == 2
        applied = apply_tile(rcol[...])
        if step > 0:
            wait_for(s3_recv.at[step - 1, pl.ds(0, 15)], v_recv.at[step - 1, 3])
            new = from_lanes(tree([s3_recv[step - 1, j] for j in range(GROUP)])[7:8], CHUNK)
            beta = ratio(new, rr)
            rr = new
            applied = applied + beta * prev[...]
            drow[...] = rrow[...] + beta * drow[...]
            dcol[...] = rcol[...] + beta * dcol[...]
        prev[...] = applied
        d = drow[...]
        scalars = to_lanes(lane_sum(d * (applied + (RIDGE / GROUP) * d)), CHUNK)
        if step == 0:
            scalars = scalars + to_lanes(lane_sum(d * d) * (1.0 / GROUP), CHUNK + 16)
        if last:
            s1_send[step, 0] = put_scalars(jnp.zeros((8, 128), F32), scalars)
            s1_recv[step, me] = s1_send[step, 0]
        else:
            for j in range(GROUP // 2):
                first, second = pack_pair(applied[:, 128 * j:128 * (j + 1)])
                s1_send[step, 2 * j] = put_scalars(first, scalars)
                s1_send[step, 2 * j + 1] = put_scalars(second, scalars)
            s1_recv[step, me] = s1_send[step, me]

        def send1(j):
            p, to = row_peer(j)
            src = s1_send.at[step, 0] if last else s1_send.at[step, p]
            remote(src, s1_recv.at[step, me], v_send.at[step, 0], v_recv.at[step, 0], to).start()

        far_first(GROUP, send1)
        drains.append((s1_recv.at[step, pl.ds(0, 15)], v_send.at[step, 0]))
        if last:
            fill(TILES)
            predict_tiles(0, 12)
        else:
            fill(waits[step][0])
        wait_for(s1_recv.at[step, pl.ds(0, 15)], v_recv.at[step, 0])
        own = tree([s1_recv[step, j] for j in range(GROUP)])
        s2_send[step] = own
        s2_cols[step, here] = own

        def send2(j):
            remote(s2_send.at[step], s2_cols.at[step, here], v_send.at[step, 1], v_recv.at[step, 1], col_peer(j)).start()

        far_first(GROUP, send2)
        drains.append((s2_cols.at[step, pl.ds(0, 15)], v_send.at[step, 1]))
        if last:
            predict_tiles(12, TILES)
        else:
            s2_rows[step, me] = own

            def send_rows(j):
                remote(
                    s2_send.at[step], s2_rows.at[step, me], v_send.at[step, 2], v_recv.at[step, 2], row_peer(j)[1]
                ).start()

            far_first(GROUP, send_rows)
            drains.append((s2_rows.at[step, pl.ds(0, 15)], v_send.at[step, 2]))
            fill(waits[step][1])
        wait_for(s2_cols.at[step, pl.ds(0, 15)], v_recv.at[step, 1])
        total = tree([s2_cols[step, j] for j in range(GROUP)])[7:8]
        if step == 0:
            rr = from_lanes(total, CHUNK + 16)
        alpha = ratio(rr, from_lanes(total, CHUNK))
        if not last:
            left = rcol[...] - alpha * (unpack(s2_cols.at[step]) + RIDGE * dcol[...])
            rcol[...] = left
            s3_send[step] = put_scalars(jnp.zeros((8, 128), F32), to_lanes(lane_sum(left * left), CHUNK))
            s3_recv[step, me] = s3_send[step]

            def send3(j):
                remote(
                    s3_send.at[step], s3_recv.at[step, me], v_send.at[step, 3], v_recv.at[step, 3], row_peer(j)[1]
                ).start()

            far_first(GROUP, send3)
            drains.append((s3_recv.at[step, pl.ds(0, 15)], v_send.at[step, 3]))
            xrow[...] = xrow[...] + alpha * drow[...]
            wait_for(s2_rows.at[step, pl.ds(0, 15)], v_recv.at[step, 2])
            rrow[...] = rrow[...] - alpha * (unpack(s2_rows.at[step]) + RIDGE * drow[...])

    def combined(t):
        return both[t, 0:16, :] + alpha * both[t, 16:32, :]

    @pl.loop(0, 4)
    def _(g):
        quarter = pl.ds(12 - 4 * g, 4)
        for k in range(4):
            j = 12 - 4 * g + k
            sib_send[j] = combined(tile_at(2 * j + 1))
        remote(sib_send.at[quarter], sib_recv.at[quarter], sib_ss, sib_rs.at[3 - g], (other, c)).start()

    @pl.loop(0, 4)
    def _(g):
        wait_for(sib_recv.at[pl.ds(0, 4)], sib_rs.at[3 - g])
        for k in range(4):
            j = 15 - 4 * g - k
            t = tile_at(2 * j)
            value = combined(t) + sib_recv[j]

            @pl.when(j > 0)
            def _():
                pred_send[j] = value
                remote(pred_send.at[j], pred_recv.at[chip], pred_ss, pred_rs, (t, c)).start()

            @pl.when(j == 0)
            def _():
                pred_recv[chip] = value

    drains.append((sib_recv, sib_ss))
    drains.append((pred_recv.at[pl.ds(0, 15)], pred_ss))

    xrow[...] = xrow[...] + alpha * drow[...]
    pair = xrow[:, pl.ds(pl.multiple_of((me // 2) * 128, 128), 128)]
    own_x = jnp.where(lax.rem(me, 2) == 0, pair, pltpu.roll(pair, CHUNK, 1))
    coef_ref[...] = own_x[0:15, 0:CHUNK]
    hi, mid, low = split3(xrow[:, half])
    wide = jnp.concatenate([hi.astype(F32), mid.astype(F32), jnp.zeros((96, HALF), F32)], axis=0)
    xt[...] = wide.T[:, 0:32].astype(BF16)
    gsum[...] = jnp.zeros_like(gsum)
    csum[...] = jnp.zeros_like(csum)
    tlab_copy.wait()
    labels = jnp.concatenate([tlab[...], jnp.zeros((1, TILE), F32)], axis=0)

    wait_for(pred_recv.at[pl.ds(0, 15)], pred_rs)
    own_err = (tree([pred_recv[j] for j in range(GROUP)]) - labels).astype(BF16)
    err_own[...] = own_err
    err[r] = own_err

    def send_err(j):
        remote(err_own, err.at[r], err_ss, err_rs.at[r], (tile_at(j), c)).start()

    far_first(32, send_err)
    drains.append((err.at[pl.ds(0, 31)], err_ss))

    @pl.loop(0, 8)
    def _(s):
        part, sums = None, None
        for k in range(4):
            j = s * 4 + k
            t = tile_at(j)

            @pl.when(j > 0)
            def _():
                wait_for(err.at[0], err_rs.at[t])

            e = err[t]
            mix = dot(xt[...], jnp.concatenate([e, e], axis=0))
            weights = mix.astype(BF16) * kk_hi[t]
            product = dot(weights, tgt[t])
            back = weights.astype(F32)
            back = back[:, 0:128] + back[:, 128:256]
            part = product if part is None else part + product
            sums = back if sums is None else sums + back
        gsum[...] += part
        csum[...] += sums

    scale = 1.0 / 256.0
    term = (gsum[...] - lane_sum(csum[...]) * rows_all[half, :].astype(F32)) * scale
    g_send[...] = term.reshape(8, CHUNK, FEAT)
    g_recv[c] = g_send[c]

    @pl.loop(0, 7)
    def _(i):
        j = 7 - i
        p = lax.rem(zl + j // 4, 2) * 4 + lax.rem(y + gray(j % 4), 4)
        remote(g_send.at[p], g_recv.at[c], g_ss, g_rs, (r, p)).start()

    drains.append((g_recv.at[pl.ds(0, 7)], g_ss))
    wait_for(g_recv.at[pl.ds(0, 7)], g_rs)
    grad_ref[...] = tree([g_recv[j] for j in range(8)])

    for ref, sem in drains:
        wait_for(ref, sem)


def body(support, support_labels, targets, target_labels):
    classes = support_labels.shape[0]
    vmem = pl.BlockSpec(memory_space=pltpu.VMEM)
    anywhere = pl.BlockSpec(memory_space=pl.ANY)
    dma = pltpu.SemaphoreType.DMA
    return pl.pallas_call(
        kernel,
        out_shape=(
            jax.ShapeDtypeStruct((classes, CHUNK), F32),
            jax.ShapeDtypeStruct((CHUNK, FEAT), F32),
        ),
        in_specs=[vmem, vmem, anywhere, anywhere],
        out_specs=(vmem, vmem),
        scratch_shapes=[
            pltpu.VMEM((TILES, TILE, FEAT), BF16),
            pltpu.VMEM((classes, TILE), F32),
            pltpu.VMEM((UNIT, FEAT), BF16),
            pltpu.VMEM((GROUP, UNIT, FEAT), BF16),
            pltpu.VMEM((GROUP, UNIT, FEAT), BF16),
            pltpu.VMEM((WIDE, FEAT), BF16),
            pltpu.VMEM((1, WIDE), F32),
            pltpu.VMEM((HALF, 1), F32),
            pltpu.VMEM((WIDE, WIDE), BF16),
            pltpu.VMEM((WIDE, WIDE), BF16),
            pltpu.VMEM((TILES, HALF, TILE), BF16),
            pltpu.VMEM((TILES, HALF, TILE), BF16),
            pltpu.VMEM((3, GROUP, 8, 128), F32),
            pltpu.VMEM((3, GROUP, 8, 128), F32),
            pltpu.VMEM((3, 8, 128), F32),
            pltpu.VMEM((2, GROUP, 8, 128), F32),
            pltpu.VMEM((3, GROUP, 8, 128), F32),
            pltpu.VMEM((2, 8, 128), F32),
            pltpu.VMEM((2, GROUP, 8, 128), F32),
            pltpu.VMEM((GROUP, WIDE), F32),
            pltpu.VMEM((GROUP, WIDE), F32),
            pltpu.VMEM((GROUP, WIDE), F32),
            pltpu.VMEM((GROUP, WIDE), F32),
            pltpu.VMEM((GROUP, WIDE), F32),
            pltpu.VMEM((GROUP, WIDE), F32),
            pltpu.VMEM((TILES, 32, TILE), F32),
            pltpu.VMEM((GROUP, 16, TILE), F32),
            pltpu.VMEM((GROUP, 16, TILE), F32),
            pltpu.VMEM((GROUP, 16, TILE), F32),
            pltpu.VMEM((GROUP, 16, TILE), F32),
            pltpu.VMEM((16, TILE), BF16),
            pltpu.VMEM((TILES, 16, TILE), BF16),
            pltpu.VMEM((HALF, 32), BF16),
            pltpu.VMEM((HALF, FEAT), F32),
            pltpu.VMEM((HALF, 128), F32),
            pltpu.VMEM((8, CHUNK, FEAT), F32),
            pltpu.VMEM((8, CHUNK, FEAT), F32),
            dma((2,)),
            dma((4,)),
            dma((4,)),
            dma((4,)),
            dma,
            dma,
            dma((3, 4)),
            dma((3, 4)),
            dma,
            dma((4,)),
            dma,
            dma,
            dma,
            dma((TILES,)),
            dma,
            dma,
        ],
        compiler_params=pltpu.CompilerParams(
            collective_id=0, has_side_effects=True, vmem_limit_bytes=58 * 1024 * 1024
        ),
    )(support, support_labels, targets.reshape(TILES, TILE, FEAT), target_labels)


def solution(mesh):
    in_specs = (P(("row", "col"), None), P(None, ("row", "col")), P("col", None), P(None, "col"))
    out_specs = (P(None, ("row", "col")), P(("row", "col"), None))
    return jax.shard_map(body, mesh=mesh, in_specs=in_specs, out_specs=out_specs, check_vma=False)
```

```python
import jax
import jax.numpy as jnp
from jax import lax
from jax.experimental import pallas as pl
from jax.experimental.pallas import tpu as pltpu
from jax.sharding import PartitionSpec as P

MESH = pl.DeviceIdType.MESH
F32 = jnp.float32
BF16 = jnp.bfloat16

CHUNK = 64
FEAT = 256
TILE = 256
TILES = 32
GROUP = 16
WIDE = GROUP * CHUNK
HALF = WIDE // 2
RIDGE = 0.5
UNIT = CHUNK + 16
NN = (((1,), (0,)), ((), ()))
NT = (((1,), (1,)), ((), ()))


def dot(a, b, dims=NN):
    return lax.dot_general(a, b, dims, preferred_element_type=F32)


def split3(v):
    hi = v.astype(BF16)
    rest = v - hi.astype(F32)
    mid = rest.astype(BF16)
    low = (rest - mid.astype(F32)).astype(BF16)
    return hi, mid, low


def row_norms(rows):
    square = jnp.square(rows.astype(F32))
    hi = square.astype(BF16)
    low = (square - hi.astype(F32)).astype(BF16)
    ones = jnp.ones((8, FEAT), BF16)
    return 0.5 * (dot(ones, hi, NT) + dot(ones, low, NT))[0:1, :]


def column_norms(rows):
    return 0.5 * jnp.sum(jnp.square(rows.astype(F32)), axis=1, keepdims=True)


def pack_pair(v):
    left = lax.broadcasted_iota(jnp.int32, (8, 128), 1) < CHUNK
    top, bottom = v[0:8], v[8:16]
    first = jnp.where(left, top, pltpu.roll(bottom, CHUNK, 1))
    second = jnp.where(left, pltpu.roll(top, CHUNK, 1), bottom)
    return first, second


def unpack_pair(a, b):
    left = lax.broadcasted_iota(jnp.int32, (8, 128), 1) < CHUNK
    top = jnp.where(left, a, pltpu.roll(b, CHUNK, 1))
    bottom = jnp.where(left, pltpu.roll(a, CHUNK, 1), b)
    return jnp.concatenate([top, bottom], axis=0)


def unpack(ref):
    wide = jnp.concatenate([unpack_pair(ref[2 * j], ref[2 * j + 1]) for j in range(GROUP // 2)], axis=1)
    return jnp.where(lax.broadcasted_iota(jnp.int32, wide.shape, 0) < 15, wide, 0.0)


def label_rows(labels):
    hi, mid, low = split3(labels)
    parts = [hi.astype(F32), mid.astype(F32), low.astype(F32), jnp.zeros((16, CHUNK), F32)]
    return jnp.concatenate(parts, axis=1).astype(BF16)


def labels_of(ref):
    left = lax.broadcasted_iota(jnp.int32, (16, 128), 1) < CHUNK
    whole = []
    for j in range(GROUP):
        block = ref[j, CHUNK:UNIT, :].astype(F32)
        a, b = block[:, 0:128], block[:, 128:256]
        whole.append((a + pltpu.roll(a, CHUNK, 1)) + (b + pltpu.roll(b, CHUNK, 1)))
    return jnp.concatenate([jnp.where(left, whole[2 * j], whole[2 * j + 1]) for j in range(GROUP // 2)], axis=1)


def gray(j):
    return j + (j // 2) * (5 - 2 * j)


def to_lanes(q, shift):
    sub = lax.broadcasted_iota(jnp.int32, (16, 128), 0)
    lane = lax.broadcasted_iota(jnp.int32, (16, 128), 1)
    return jnp.sum(jnp.where(lane == sub + shift, q, 0.0), axis=0, keepdims=True)


def from_lanes(row, shift):
    sub = lax.broadcasted_iota(jnp.int32, (16, 128), 0)
    lane = lax.broadcasted_iota(jnp.int32, (16, 128), 1)
    return jnp.sum(jnp.where(lane == sub + shift, row, 0.0), axis=1, keepdims=True)


def put_scalars(message, row):
    sub = lax.broadcasted_iota(jnp.int32, (8, 128), 0)
    lane = lax.broadcasted_iota(jnp.int32, (8, 128), 1)
    return jnp.where((sub == 7) & (lane >= CHUNK), row, message)


def lane_sum(v):
    return jnp.sum(v, axis=1, keepdims=True)


def ratio(a, b):
    real = lax.broadcasted_iota(jnp.int32, (16, 1), 0) < 15
    return jnp.where(real, a, 0.0) / jnp.where(real, b, 1.0)


def tree(values):
    values = list(values)
    while len(values) > 1:
        values = [values[i] + values[i + 1] if i + 1 < len(values) else values[i] for i in range(0, len(values), 2)]
    return values[0]


def kernel(
    sup_ref, lab_ref, tgt_hbm, tlab_hbm,
    out_ref,
    tgt, tlab, unit, rf, cf, rows_all, rn_ref, sn_ref,
    kt_hi, kt_lo, kk_hi, kk_lo,
    s1_send, s1_recv, s2_send, s2_rows, s2_cols, s3_send, s3_recv, t_send, t_rows, t_cols,
    drow, rrow, xrow, dcol, rcol, prev,
    both, sib_send, sib_recv, pred_send, pred_recv, err_own, err, xt, gsum, csum, g_send, g_recv,
    local_sems, f_send, z_recv, x_recv, r_recv, b_recv, v_send, v_recv,
    sib_ss, sib_rs, pred_ss, pred_rs, err_ss, err_rs, g_ss, g_rs,
):
    r = lax.axis_index("row")
    c = lax.axis_index("col")
    chip, core = r // 2, lax.rem(r, 2)
    z, x = chip // 4, lax.rem(chip, 4)
    zl, y = c // 4, lax.rem(c, 4)
    me = core * 8 + c
    here = x * 4 + z

    def device(pz, px):
        return (2 * (pz * 4 + px) + core, c)

    xs = [lax.rem(x + d, 4) for d in range(4)]
    zs = [lax.rem(z + d, 4) for d in range(4)]
    ys = [lax.rem(y + d, 4) for d in range(4)]
    ls = [zl, 1 - zl]
    ks = [core, 1 - core]

    def row_peer(j):
        k, p = ks[j % 2], ls[j // 8] * 4 + ys[gray((j // 2) % 4)]
        return k * 8 + p, (2 * chip + k, p)

    def col_peer(j):
        return (2 * (zs[gray(j // 4)] * 4 + xs[gray(j % 4)]) + core, c)

    def tile_at(j):
        j = jnp.int32(j)
        chip_there = lax.rem(z + gray(j // 8), 4) * 4 + lax.rem(x + gray((j // 2) % 4), 4)
        return 2 * chip_there + lax.rem(core + j % 2, 2)

    def far_first(count, act):
        for j in range(count - 1, 0, -1):
            act(j)

    tgt_copy = pltpu.make_async_copy(tgt_hbm, tgt, local_sems.at[0])
    tgt_copy.start()
    start_lane = pl.multiple_of(r * TILE, TILE)
    tlab_copy = pltpu.make_async_copy(tlab_hbm.at[:, pl.ds(start_lane, TILE)], tlab, local_sems.at[1])
    tlab_copy.start()

    barrier = pltpu.get_barrier_semaphore()
    far_first(4, lambda j: pl.semaphore_signal(barrier, inc=1, device_id=device(zs[j], x), device_id_type=MESH))
    far_first(4, lambda j: pl.semaphore_signal(barrier, inc=1, device_id=device(z, xs[j]), device_id_type=MESH))
    far_first(
        GROUP, lambda j: pl.semaphore_signal(barrier, inc=1, device_id=row_peer(j)[1], device_id_type=MESH)
    )

    lab = jnp.concatenate([lab_ref[...], jnp.zeros((1, CHUNK), F32)], axis=0)
    unit[0:CHUNK, :] = sup_ref[...]
    unit[CHUNK:UNIT, :] = label_rows(lab)
    rf[me] = unit[...]
    cf[here] = unit[...]

    pl.semaphore_wait(barrier, 21)

    drains = []

    def remote(src, dst, ss, rs, to):
        return pltpu.make_async_remote_copy(
            src_ref=src, dst_ref=dst, send_sem=ss, recv_sem=rs, device_id=to, device_id_type=MESH
        )

    def wait_for(ref, sem):
        pltpu.make_async_copy(ref, ref, sem).wait()

    for d in (2, 3, 1):
        remote(unit, cf.at[here], f_send.at[0], z_recv.at[z], device(zs[d], x)).start()
    for j in range(7, 0, -1):
        to = (r, ls[j // 4] * 4 + ys[gray(j % 4)])
        remote(unit, rf.at[me], f_send.at[1], r_recv, to).start()

    def to_x(pz):
        for d in (2, 3, 1):
            slot = x * 4 + pz
            remote(cf.at[slot], cf.at[slot], f_send.at[2], x_recv.at[x], device(z, xs[d])).start()

    to_x(z)

    for d in (1, 3, 2):
        wait_for(cf.at[0], z_recv.at[zs[d]])
        to_x(zs[d])

    wait_for(rf.at[pl.ds(0, 7)], r_recv)
    block = pl.ds(core * 8, 8)
    other = 2 * chip + 1 - core
    remote(rf.at[block], rf.at[block], f_send.at[3], b_recv, (other, c)).start()
    drains.append((cf.at[pl.ds(0, 3)], f_send.at[0]))
    drains.append((rf.at[pl.ds(0, 7)], f_send.at[1]))
    drains.append((cf.at[pl.ds(0, 12)], f_send.at[2]))
    drains.append((rf.at[pl.ds(0, 8)], f_send.at[3]))

    half = pl.ds(pl.multiple_of(core * HALF, HALF), HALF)
    mine = rf[block][:, 0:CHUNK, :].reshape(HALF, FEAT)
    rows_all[half, :] = mine
    sn_ref[...] = column_norms(mine)
    tgt_copy.wait()

    def target_tile(i):
        rows = tgt[i]
        inner = dot(rows_all[half, :], rows, NT)
        value = jnp.exp(inner - sn_ref[...] - row_norms(rows))
        hi = value.astype(BF16)
        kk_hi[i] = hi
        kk_lo[i] = (value - hi.astype(F32)).astype(BF16)

    done = [0]

    def fill(count):
        stop = min(TILES, done[0] + count)
        if stop > done[0]:
            pl.loop(done[0], stop)(target_tile)
        done[0] = stop

    fill(10)

    wait_for(rf.at[pl.ds(0, 8)], b_recv)
    theirs = rf[pl.ds(8 - core * 8, 8)][:, 0:CHUNK, :].reshape(HALF, FEAT)
    rows_all[pl.ds(pl.multiple_of(HALF - core * HALF, HALF), HALF), :] = theirs
    rn_ref[...] = row_norms(rows_all[...])

    @pl.loop(0, 4)
    def _(i):
        px = lax.rem(x + gray(i), 4)

        @pl.when(i > 0)
        def _():
            wait_for(cf.at[pl.ds(0, 4)], x_recv.at[px])

        part = cf[pl.ds(px * 4, 4)][:, 0:CHUNK, :].reshape(TILE, FEAT)
        inner = dot(part, rows_all[...], NT)
        value = jnp.exp(inner - column_norms(part) - rn_ref[...])
        hi = value.astype(BF16)
        where = pl.ds(pl.multiple_of(px * TILE, TILE), TILE)
        kt_hi[where, :] = hi
        kt_lo[where, :] = (value - hi.astype(F32)).astype(BF16)

    def apply_tile(v):
        hi, mid, low = split3(v)
        big = dot(jnp.concatenate([hi, mid, low], axis=0), kt_hi[...])
        small = dot(jnp.concatenate([hi, mid], axis=0), kt_lo[...])
        return (big[0:16] + small[0:16]) + ((big[16:32] + small[16:32]) + big[32:48])

    b_rows = labels_of(rf)
    b_cols = labels_of(cf)
    drow[...] = b_rows
    rrow[...] = b_rows
    xrow[...] = jnp.zeros_like(b_rows)
    dcol[...] = b_cols
    rcol[...] = b_cols
    rr = None

    def predict_tile(t):
        hi, mid, low = split3(xrow[:, half])
        hi2, mid2, low2 = split3(drow[:, half])
        three = jnp.concatenate([hi, hi2, mid, mid2, low, low2], axis=0)
        two = jnp.concatenate([hi, hi2, mid, mid2], axis=0)
        big = dot(three, kk_hi[t])
        small = dot(two, kk_lo[t])
        return (big[0:32] + small[0:32]) + ((big[32:64] + small[32:64]) + big[64:96])

    def predict_theirs():
        @pl.loop(0, 4)
        def _(g):
            for k in range(4):
                j = 12 - 4 * g + k
                sib_send[j] = predict_tile(tile_at(2 * j + 1))
            quarter = pl.ds(12 - 4 * g, 4)
            remote(sib_send.at[quarter], sib_recv.at[quarter], sib_ss, sib_rs.at[3 - g], (other, c)).start()

    def predict_own():
        @pl.loop(0, 4)
        def _(g):
            wait_for(sib_recv.at[pl.ds(0, 4)], sib_rs.at[3 - g])
            for k in range(4):
                j = 12 - 4 * g + k
                both[j] = predict_tile(tile_at(2 * j)) + sib_recv[j]

    waits = ((5, 8), (5, 4))
    for step in range(3):
        last = step == 2
        applied = apply_tile(rcol[...])
        if step > 0:
            wait_for(s3_recv.at[step - 1, pl.ds(0, 15)], v_recv.at[step - 1, 3])
            new = from_lanes(tree([s3_recv[step - 1, j] for j in range(GROUP)]), CHUNK)
            beta = ratio(new, rr)
            rr = new
            applied = applied + beta * prev[...]
            drow[...] = rrow[...] + beta * drow[...]
            dcol[...] = rcol[...] + beta * dcol[...]
        prev[...] = applied
        d = drow[...]
        scalars = to_lanes(lane_sum(d * (applied + (RIDGE / GROUP) * d)), CHUNK)
        if step == 0:
            scalars = scalars + to_lanes(lane_sum(d * d) * (1.0 / GROUP), CHUNK + 16)
        if last:
            t_send[0] = scalars
            t_rows[me] = scalars
        else:
            for j in range(GROUP // 2):
                first, second = pack_pair(applied[:, 128 * j:128 * (j + 1)])
                s1_send[step, 2 * j] = put_scalars(first, scalars)
                s1_send[step, 2 * j + 1] = put_scalars(second, scalars)
            s1_recv[step, me] = s1_send[step, me]

        def send1(j):
            p, to = row_peer(j)
            src = t_send.at[0] if last else s1_send.at[step, p]
            dst = t_rows.at[me] if last else s1_recv.at[step, me]
            remote(src, dst, v_send.at[step, 0], v_recv.at[step, 0], to).start()

        far_first(GROUP, send1)
        landed = t_rows.at[pl.ds(0, 15)] if last else s1_recv.at[step, pl.ds(0, 15)]
        drains.append((landed, v_send.at[step, 0]))
        if last:
            fill(TILES)
            predict_theirs()
        else:
            fill(waits[step][0])
        wait_for(landed, v_recv.at[step, 0])
        if last:
            own = tree([t_rows[j] for j in range(GROUP)])
            t_send[1] = own
            t_cols[here] = own
        else:
            own = tree([s1_recv[step, j] for j in range(GROUP)])
            s2_send[step] = own
            s2_cols[step, here] = own

        def send2(j):
            src = t_send.at[1] if last else s2_send.at[step]
            dst = t_cols.at[here] if last else s2_cols.at[step, here]
            remote(src, dst, v_send.at[step, 1], v_recv.at[step, 1], col_peer(j)).start()

        far_first(GROUP, send2)
        landed = t_cols.at[pl.ds(0, 15)] if last else s2_cols.at[step, pl.ds(0, 15)]
        drains.append((landed, v_send.at[step, 1]))
        if last:
            predict_own()
        else:
            s2_rows[step, me] = own

            def send_rows(j):
                remote(
                    s2_send.at[step], s2_rows.at[step, me], v_send.at[step, 2], v_recv.at[step, 2], row_peer(j)[1]
                ).start()

            far_first(GROUP, send_rows)
            drains.append((s2_rows.at[step, pl.ds(0, 15)], v_send.at[step, 2]))
            fill(waits[step][1])
        wait_for(landed, v_recv.at[step, 1])
        if last:
            total = tree([t_cols[j] for j in range(GROUP)])
        else:
            total = tree([s2_cols[step, j] for j in range(GROUP)])[7:8]
        if step == 0:
            rr = from_lanes(total, CHUNK + 16)
        alpha = ratio(rr, from_lanes(total, CHUNK))
        if not last:
            left = rcol[...] - alpha * (unpack(s2_cols.at[step]) + RIDGE * dcol[...])
            rcol[...] = left
            norms = to_lanes(lane_sum(left * left), CHUNK)
            s3_send[step] = norms
            s3_recv[step, me] = norms

            def send3(j):
                remote(
                    s3_send.at[step], s3_recv.at[step, me], v_send.at[step, 3], v_recv.at[step, 3], row_peer(j)[1]
                ).start()

            far_first(GROUP, send3)
            drains.append((s3_recv.at[step, pl.ds(0, 15)], v_send.at[step, 3]))
            xrow[...] = xrow[...] + alpha * drow[...]
            wait_for(s2_rows.at[step, pl.ds(0, 15)], v_recv.at[step, 2])
            rrow[...] = rrow[...] - alpha * (unpack(s2_rows.at[step]) + RIDGE * drow[...])

    for j in range(GROUP - 1, -1, -1):
        value = both[j, 0:16, :] + alpha * both[j, 16:32, :]
        if j > 0:
            pred_send[j] = value
            remote(pred_send.at[j], pred_recv.at[chip], pred_ss, pred_rs, col_peer(j)).start()
        else:
            pred_recv[chip] = value

    drains.append((sib_recv, sib_ss))
    drains.append((pred_recv.at[pl.ds(0, 15)], pred_ss))

    xrow[...] = xrow[...] + alpha * drow[...]
    pair = xrow[:, pl.ds(pl.multiple_of((me // 2) * 128, 128), 128)]
    own_x = jnp.where(lax.rem(me, 2) == 0, pair, pltpu.roll(pair, CHUNK, 1))
    out_ref[CHUNK:UNIT, 0:128] = own_x
    out_ref[CHUNK:UNIT, 128:FEAT] = jnp.zeros((16, 128), F32)
    hi, mid, low = split3(xrow[:, half])
    wide = jnp.concatenate([hi.astype(F32), mid.astype(F32), jnp.zeros((96, HALF), F32)], axis=0)
    xt[...] = wide.T[:, 0:32].astype(BF16)
    gsum[...] = jnp.zeros_like(gsum)
    csum[...] = jnp.zeros_like(csum)
    tlab_copy.wait()
    labels = jnp.concatenate([tlab[...], jnp.zeros((1, TILE), F32)], axis=0)

    wait_for(pred_recv.at[pl.ds(0, 15)], pred_rs)
    own_err = (tree([pred_recv[j] for j in range(GROUP)]) - labels).astype(BF16)
    err_own[...] = own_err
    err[r] = own_err

    @pl.loop(1, 32)
    def _(j):
        remote(err_own, err.at[r], err_ss, err_rs.at[r], (tile_at(j), c)).start()

    drains.append((err.at[pl.ds(0, 31)], err_ss))

    @pl.loop(0, 8)
    def _(s):
        part, sums = None, None
        for k in range(4):
            j = s * 4 + k
            t = tile_at(j)

            @pl.when(j > 0)
            def _():
                wait_for(err.at[0], err_rs.at[t])

            e = err[t]
            mix = dot(xt[...], jnp.concatenate([e, e], axis=0))
            weights = mix.astype(BF16) * kk_hi[t]
            product = dot(weights, tgt[t])
            back = weights.astype(F32)
            back = back[:, 0:128] + back[:, 128:256]
            part = product if part is None else part + product
            sums = back if sums is None else sums + back
        gsum[...] += part
        csum[...] += sums

    scale = 1.0 / 256.0
    term = (gsum[...] - lane_sum(csum[...]) * rows_all[half, :].astype(F32)) * scale
    g_send[...] = term.reshape(8, CHUNK, FEAT)
    g_recv[c] = g_send[c]

    for j in range(7, 0, -1):
        p = ls[j // 4] * 4 + ys[gray(j % 4)]
        remote(g_send.at[p], g_recv.at[c], g_ss, g_rs, (r, p)).start()

    drains.append((g_recv.at[pl.ds(0, 7)], g_ss))
    wait_for(g_recv.at[pl.ds(0, 7)], g_rs)
    out_ref[0:CHUNK, :] = tree([g_recv[j] for j in range(8)])

    for ref, sem in drains:
        wait_for(ref, sem)


def part_outputs(joint_ref, coef_ref, grad_ref):
    coef_ref[...] = joint_ref[CHUNK:CHUNK + 15, 0:CHUNK]
    grad_ref[...] = joint_ref[0:CHUNK, :]


def body(support, support_labels, targets, target_labels):
    classes = support_labels.shape[0]
    vmem = pl.BlockSpec(memory_space=pltpu.VMEM)
    anywhere = pl.BlockSpec(memory_space=pl.ANY)
    dma = pltpu.SemaphoreType.DMA
    joint = pl.pallas_call(
        kernel,
        out_shape=jax.ShapeDtypeStruct((UNIT, FEAT), F32),
        in_specs=[vmem, vmem, anywhere, anywhere],
        out_specs=vmem,
        scratch_shapes=[
            pltpu.VMEM((TILES, TILE, FEAT), BF16),
            pltpu.VMEM((classes, TILE), F32),
            pltpu.VMEM((UNIT, FEAT), BF16),
            pltpu.VMEM((GROUP, UNIT, FEAT), BF16),
            pltpu.VMEM((GROUP, UNIT, FEAT), BF16),
            pltpu.VMEM((WIDE, FEAT), BF16),
            pltpu.VMEM((1, WIDE), F32),
            pltpu.VMEM((HALF, 1), F32),
            pltpu.VMEM((WIDE, WIDE), BF16),
            pltpu.VMEM((WIDE, WIDE), BF16),
            pltpu.VMEM((TILES, HALF, TILE), BF16),
            pltpu.VMEM((TILES, HALF, TILE), BF16),
            pltpu.VMEM((2, GROUP, 8, 128), F32),
            pltpu.VMEM((2, GROUP, 8, 128), F32),
            pltpu.VMEM((2, 8, 128), F32),
            pltpu.VMEM((2, GROUP, 8, 128), F32),
            pltpu.VMEM((2, GROUP, 8, 128), F32),
            pltpu.VMEM((2, 1, 128), F32),
            pltpu.VMEM((2, GROUP, 1, 128), F32),
            pltpu.VMEM((2, 1, 128), F32),
            pltpu.VMEM((GROUP, 1, 128), F32),
            pltpu.VMEM((GROUP, 1, 128), F32),
            pltpu.VMEM((GROUP, WIDE), F32),
            pltpu.VMEM((GROUP, WIDE), F32),
            pltpu.VMEM((GROUP, WIDE), F32),
            pltpu.VMEM((GROUP, WIDE), F32),
            pltpu.VMEM((GROUP, WIDE), F32),
            pltpu.VMEM((GROUP, WIDE), F32),
            pltpu.VMEM((GROUP, 32, TILE), F32),
            pltpu.VMEM((GROUP, 32, TILE), F32),
            pltpu.VMEM((GROUP, 32, TILE), F32),
            pltpu.VMEM((GROUP, 16, TILE), F32),
            pltpu.VMEM((GROUP, 16, TILE), F32),
            pltpu.VMEM((16, TILE), BF16),
            pltpu.VMEM((TILES, 16, TILE), BF16),
            pltpu.VMEM((HALF, 32), BF16),
            pltpu.VMEM((HALF, FEAT), F32),
            pltpu.VMEM((HALF, 128), F32),
            pltpu.VMEM((8, CHUNK, FEAT), F32),
            pltpu.VMEM((8, CHUNK, FEAT), F32),
            dma((2,)),
            dma((4,)),
            dma((4,)),
            dma((4,)),
            dma,
            dma,
            dma((3, 4)),
            dma((3, 4)),
            dma,
            dma((4,)),
            dma,
            dma,
            dma,
            dma((TILES,)),
            dma,
            dma,
        ],
        compiler_params=pltpu.CompilerParams(
            collective_id=0, has_side_effects=True, vmem_limit_bytes=58 * 1024 * 1024
        ),
    )(support, support_labels, targets.reshape(TILES, TILE, FEAT), target_labels)
    return pl.pallas_call(
        part_outputs,
        out_shape=(
            jax.ShapeDtypeStruct((classes, CHUNK), F32),
            jax.ShapeDtypeStruct((CHUNK, FEAT), F32),
        ),
        in_specs=[vmem],
        out_specs=(vmem, vmem),
    )(joint)


def solution(mesh):
    in_specs = (P(("row", "col"), None), P(None, ("row", "col")), P("col", None), P(None, "col"))
    out_specs = (P(None, ("row", "col")), P(("row", "col"), None))
    return jax.shard_map(body, mesh=mesh, in_specs=in_specs, out_specs=out_specs, check_vma=False)
```

```python
import jax
import jax.numpy as jnp
from jax import lax
from jax.experimental import pallas as pl
from jax.experimental.pallas import tpu as pltpu
from jax.sharding import PartitionSpec as P

MESH = pl.DeviceIdType.MESH
F32 = jnp.float32
BF16 = jnp.bfloat16

CHUNK = 64
FEAT = 256
TILE = 256
TILES = 32
GROUP = 16
WIDE = GROUP * CHUNK
HALF = WIDE // 2
RIDGE = 0.5
NN = (((1,), (0,)), ((), ()))
NT = (((1,), (1,)), ((), ()))


def dot(a, b, dims=NN):
    return lax.dot_general(a, b, dims, preferred_element_type=F32)


def split3(v):
    hi = v.astype(BF16)
    rest = v - hi.astype(F32)
    mid = rest.astype(BF16)
    low = (rest - mid.astype(F32)).astype(BF16)
    return hi, mid, low


def row_norms(rows):
    square = jnp.square(rows.astype(F32))
    hi = square.astype(BF16)
    low = (square - hi.astype(F32)).astype(BF16)
    ones = jnp.ones((8, FEAT), BF16)
    return 0.5 * (dot(ones, hi, NT) + dot(ones, low, NT))[0:1, :]


def column_norms(rows):
    return 0.5 * jnp.sum(jnp.square(rows.astype(F32)), axis=1, keepdims=True)


def pack_pair(v):
    left = lax.broadcasted_iota(jnp.int32, (8, 128), 1) < CHUNK
    top, bottom = v[0:8], v[8:16]
    first = jnp.where(left, top, pltpu.roll(bottom, CHUNK, 1))
    second = jnp.where(left, pltpu.roll(top, CHUNK, 1), bottom)
    return first, second


def unpack_pair(a, b):
    left = lax.broadcasted_iota(jnp.int32, (8, 128), 1) < CHUNK
    top = jnp.where(left, a, pltpu.roll(b, CHUNK, 1))
    bottom = jnp.where(left, pltpu.roll(a, CHUNK, 1), b)
    return jnp.concatenate([top, bottom], axis=0)


def unpack(ref):
    wide = jnp.concatenate([unpack_pair(ref[2 * j], ref[2 * j + 1]) for j in range(GROUP // 2)], axis=1)
    return jnp.where(lax.broadcasted_iota(jnp.int32, wide.shape, 0) < 15, wide, 0.0)


def gray(j):
    return j + (j // 2) * (5 - 2 * j)


def to_lanes(q, shift):
    sub = lax.broadcasted_iota(jnp.int32, (16, 128), 0)
    lane = lax.broadcasted_iota(jnp.int32, (16, 128), 1)
    return jnp.sum(jnp.where(lane == sub + shift, q, 0.0), axis=0, keepdims=True)


def from_lanes(row, shift):
    sub = lax.broadcasted_iota(jnp.int32, (16, 128), 0)
    lane = lax.broadcasted_iota(jnp.int32, (16, 128), 1)
    return jnp.sum(jnp.where(lane == sub + shift, row, 0.0), axis=1, keepdims=True)


def put_scalars(message, row):
    sub = lax.broadcasted_iota(jnp.int32, (8, 128), 0)
    lane = lax.broadcasted_iota(jnp.int32, (8, 128), 1)
    return jnp.where((sub == 7) & (lane >= CHUNK), row, message)


def lane_sum(v):
    return jnp.sum(v, axis=1, keepdims=True)


def ratio(a, b):
    real = lax.broadcasted_iota(jnp.int32, (16, 1), 0) < 15
    return jnp.where(real, a, 0.0) / jnp.where(real, b, 1.0)


def tree(values):
    values = list(values)
    while len(values) > 1:
        values = [values[i] + values[i + 1] if i + 1 < len(values) else values[i] for i in range(0, len(values), 2)]
    return values[0]


def kernel(
    sup_ref, lab_ref, tgt_hbm, tlab_hbm,
    out_ref,
    tgt, tlab, sup_v, lab_v, rf, cf, lab_rows, lab_cols, rn_ref, sn_ref,
    kt_hi, kt_lo, kk_hi, kk_lo,
    s1_send, s1_recv, s2_send, s2_rows, s2_cols, t_send, t_rows, t_cols,
    drow, rrow, xrow, dcol, rcol, prev,
    three, both, sib_send, sib_recv, pred_send, pred_recv, err_own, err, xt, gsum, csum, g_send, g_recv,
    local_sems, f_send, z_recv, x_recv, r_recv, l_send, l_recv, v_send, v_recv,
    sib_ss, sib_rs, pred_ss, pred_rs, err_ss, err_rs, pass_ss, g_ss, g_rs,
):
    r = lax.axis_index("row")
    c = lax.axis_index("col")
    chip, core = r // 2, lax.rem(r, 2)
    z, x = chip // 4, lax.rem(chip, 4)
    zl, y = c // 4, lax.rem(c, 4)
    me = core * 8 + c
    here = x * 4 + z

    def device(pz, px):
        return (2 * (pz * 4 + px) + core, c)

    xs = [lax.rem(x + d, 4) for d in range(4)]
    zs = [lax.rem(z + d, 4) for d in range(4)]
    ys = [lax.rem(y + d, 4) for d in range(4)]
    ls = [zl, 1 - zl]
    ks = [core, 1 - core]

    def row_peer(j):
        k, p = ks[j % 2], ls[j // 8] * 4 + ys[gray((j // 2) % 4)]
        return k * 8 + p, (2 * chip + k, p)

    def col_peer(j):
        return (2 * (zs[gray(j // 4)] * 4 + xs[gray(j % 4)]) + core, c)

    def tile_at(j):
        j = jnp.int32(j)
        chip_there = lax.rem(z + gray(j // 8), 4) * 4 + lax.rem(x + gray((j // 2) % 4), 4)
        return 2 * chip_there + lax.rem(core + j % 2, 2)

    def far_first(count, act):
        for j in range(count - 1, 0, -1):
            act(j)

    tgt_copy = pltpu.make_async_copy(tgt_hbm, tgt, local_sems.at[0])
    tgt_copy.start()
    start_lane = pl.multiple_of(r * TILE, TILE)
    tlab_copy = pltpu.make_async_copy(tlab_hbm.at[:, pl.ds(start_lane, TILE)], tlab, local_sems.at[1])
    tlab_copy.start()

    barrier = pltpu.get_barrier_semaphore()
    far_first(4, lambda j: pl.semaphore_signal(barrier, inc=1, device_id=device(zs[j], x), device_id_type=MESH))
    far_first(4, lambda j: pl.semaphore_signal(barrier, inc=1, device_id=device(z, xs[j]), device_id_type=MESH))
    far_first(
        GROUP, lambda j: pl.semaphore_signal(barrier, inc=1, device_id=row_peer(j)[1], device_id_type=MESH)
    )

    lab = jnp.concatenate([lab_ref[...], jnp.zeros((1, CHUNK), F32)], axis=0)
    lab_v[...] = jnp.concatenate([lab[0:8], lab[8:16]], axis=1)
    sup = sup_ref[...]
    sup_v[...] = sup
    rf[me] = sup
    cf[here] = sup
    lab_rows[me] = lab_v[...]
    lab_cols[here] = lab_v[...]

    pl.semaphore_wait(barrier, 21)

    drains = []

    def remote(src, dst, ss, rs, to):
        return pltpu.make_async_remote_copy(
            src_ref=src, dst_ref=dst, send_sem=ss, recv_sem=rs, device_id=to, device_id_type=MESH
        )

    def wait_for(ref, sem):
        pltpu.make_async_copy(ref, ref, sem).wait()

    def to_x(dz, steps):
        slot = xs[0] * 4 + zs[dz]
        for d in steps:
            remote(cf.at[slot], cf.at[slot], f_send.at[2], x_recv.at[slot], device(z, xs[d])).start()

    def from_x(dx, dz):
        slot = xs[dx] * 4 + zs[dz]
        wait_for(cf.at[0], x_recv.at[slot])
        return slot

    def pass_on(dx, dz):
        slot = from_x(dx, dz)
        remote(cf.at[slot], cf.at[slot], f_send.at[2], x_recv.at[slot], device(z, xs[4 - dx])).start()

    col_peers = [(r, ls[j // 4] * 4 + ys[gray(j % 4)]) for j in range(8)]
    for d in (2, 3, 1):
        remote(sup_v, cf.at[here], f_send.at[0], z_recv.at[z], device(zs[d], x)).start()
    to_x(0, (1, 3))
    for j in range(7, 0, -1):
        remote(sup_v, rf.at[me], f_send.at[1], r_recv.at[0], col_peers[j]).start()
    for d in (2, 3, 1):
        remote(lab_v, lab_cols.at[here], l_send.at[0], l_recv.at[0], device(zs[d], x)).start()
    for j in range(7, 0, -1):
        remote(lab_v, lab_rows.at[me], l_send.at[1], l_recv.at[1], col_peers[j]).start()

    for d in (1, 3):
        wait_for(cf.at[0], z_recv.at[zs[d]])
        to_x(d, (1, 3))
    pass_on(1, 0)
    wait_for(cf.at[0], z_recv.at[zs[2]])
    to_x(2, (1, 3))

    block = pl.ds(core * 8, 8)
    other = 2 * chip + 1 - core
    wait_for(rf.at[pl.ds(0, 7)], r_recv.at[0])
    remote(rf.at[block], rf.at[block], f_send.at[3], r_recv.at[1], (other, c)).start()
    wait_for(lab_cols.at[pl.ds(0, 3)], l_recv.at[0])
    for d in (2, 3, 1):
        four = lab_cols.at[pl.ds(x * 4, 4)]
        remote(four, four, l_send.at[2], l_recv.at[2], device(z, xs[d])).start()
    wait_for(lab_rows.at[pl.ds(0, 7)], l_recv.at[1])
    remote(lab_rows.at[block], lab_rows.at[block], l_send.at[3], l_recv.at[3], (other, c)).start()

    drains.append((cf.at[pl.ds(0, 3)], f_send.at[0]))
    drains.append((rf.at[pl.ds(0, 7)], f_send.at[1]))
    drains.append((cf.at[pl.ds(0, 12)], f_send.at[2]))
    drains.append((rf.at[pl.ds(0, 8)], f_send.at[3]))
    drains.append((lab_cols.at[pl.ds(0, 3)], l_send.at[0]))
    drains.append((lab_rows.at[pl.ds(0, 7)], l_send.at[1]))
    drains.append((lab_cols.at[pl.ds(0, 12)], l_send.at[2]))
    drains.append((lab_rows.at[pl.ds(0, 8)], l_send.at[3]))

    half = pl.ds(pl.multiple_of(core * HALF, HALF), HALF)
    sn_ref[...] = column_norms(rf[block].reshape(HALF, FEAT))
    tgt_copy.wait()

    def target_tile(i):
        rows = tgt[i]
        inner = dot(rf[block].reshape(HALF, FEAT), rows, NT)
        value = jnp.exp(inner - sn_ref[...] - row_norms(rows))
        hi = value.astype(BF16)
        kk_hi[i] = hi
        kk_lo[i] = (value - hi.astype(F32)).astype(BF16)

    done = [0]

    def fill(count):
        stop = min(TILES, done[0] + count)
        if stop > done[0]:

            @pl.loop(done[0] // 2, stop // 2)
            def _(i):
                target_tile(2 * i)
                target_tile(2 * i + 1)

        done[0] = stop

    fill(4)
    pass_on(3, 1)
    pass_on(3, 3)
    pass_on(1, 2)
    fill(4)

    wait_for(rf.at[pl.ds(0, 8)], r_recv.at[1])
    rn_ref[...] = row_norms(rf[...].reshape(WIDE, FEAT))

    @pl.loop(0, 4)
    def _(i):
        @pl.when(i == 1)
        def _():
            from_x(1, 1)
            from_x(1, 3)

        @pl.when(i == 2)
        def _():
            from_x(3, 0)
            from_x(3, 2)

        @pl.when(i == 3)
        def _():
            for d in range(4):
                from_x(2, d)

        px = lax.rem(x + gray(i), 4)
        part = cf[pl.ds(px * 4, 4)].reshape(TILE, FEAT)
        inner = dot(part, rf[...].reshape(WIDE, FEAT), NT)
        value = jnp.exp(inner - column_norms(part) - rn_ref[...])
        hi = value.astype(BF16)
        where = pl.ds(pl.multiple_of(px * TILE, TILE), TILE)
        kt_hi[where, :] = hi
        kt_lo[where, :] = (value - hi.astype(F32)).astype(BF16)

    def apply_tile(v):
        hi, mid, low = split3(v)
        big = dot(jnp.concatenate([hi, mid, low], axis=0), kt_hi[...])
        small = dot(jnp.concatenate([hi, mid], axis=0), kt_lo[...])
        return (big[0:16] + small[0:16]) + ((big[16:32] + small[16:32]) + big[32:48])

    wait_for(lab_cols.at[pl.ds(0, 12)], l_recv.at[2])
    b_cols = unpack(lab_cols)
    wait_for(lab_rows.at[pl.ds(0, 8)], l_recv.at[3])
    b_rows = unpack(lab_rows)
    drow[...] = b_rows
    rrow[...] = b_rows
    xrow[...] = jnp.zeros_like(b_rows)
    dcol[...] = b_cols
    rcol[...] = b_cols
    rr = None

    def predict_tile(t):
        big = dot(three[...], kk_hi[t])
        small = dot(three[0:64, :], kk_lo[t])
        return (big[0:32] + small[0:32]) + ((big[32:64] + small[32:64]) + big[64:96])

    def predict_theirs():
        @pl.loop(0, 4)
        def _(g):
            for k in range(4):
                j = 12 - 4 * g + k
                sib_send[j] = predict_tile(tile_at(2 * j + 1))
            quarter = pl.ds(12 - 4 * g, 4)
            remote(sib_send.at[quarter], sib_recv.at[quarter], sib_ss, sib_rs.at[3 - g], (other, c)).start()

    def predict_own():
        @pl.loop(0, 4)
        def _(g):
            wait_for(sib_recv.at[pl.ds(0, 4)], sib_rs.at[3 - g])
            for k in range(4):
                j = 12 - 4 * g + k
                both[j] = predict_tile(tile_at(2 * j)) + sib_recv[j]

    lane = lax.broadcasted_iota(jnp.int32, (1, 128), 1)
    left_half = lax.broadcasted_iota(jnp.int32, (8, 128), 1) < CHUNK
    waits = ((8, 8), (4, 4))
    for step in range(3):
        first, last = step == 0, step == 2
        norm = lane_sum(rcol[...] * rcol[...])
        applied = apply_tile(rcol[...])
        small_ridge = RIDGE / GROUP
        if first:
            d = drow[...]
            guess = applied
            scalars = to_lanes(lane_sum(d * (applied + small_ridge * d)), CHUNK) + to_lanes(norm, CHUNK + 48)
        else:
            near = ratio(norm * float(GROUP), rr)
            old = drow[...]
            d = rrow[...] + near * old
            guess = applied + near * prev[...]
            by_d = guess + small_ridge * d
            by_old = prev[...] + small_ridge * old
            scalars = to_lanes(lane_sum(d * by_d), CHUNK) + to_lanes(lane_sum(d * by_old + old * by_d), CHUNK + 16)
            scalars = scalars + to_lanes(lane_sum(old * by_old), CHUNK + 32) + to_lanes(norm, CHUNK + 48)
        if last:
            t_send[0] = scalars
            t_rows[me] = scalars
        else:
            for j in range(GROUP // 2):
                a, b = pack_pair(applied[:, 128 * j:128 * (j + 1)])
                s1_send[step, 2 * j] = put_scalars(a, scalars)
                s1_send[step, 2 * j + 1] = put_scalars(b, scalars)
            s1_recv[step, me] = s1_send[step, me]

        def send1(j):
            p, to = row_peer(j)
            src = t_send.at[0] if last else s1_send.at[step, p]
            dst = t_rows.at[me] if last else s1_recv.at[step, me]
            remote(src, dst, v_send.at[step, 0], v_recv.at[step, 0], to).start()

        far_first(GROUP, send1)
        landed = t_rows.at[pl.ds(0, 15)] if last else s1_recv.at[step, pl.ds(0, 15)]
        drains.append((landed, v_send.at[step, 0]))
        if last:
            fill(TILES)
        else:
            fill(waits[step][0])
        wait_for(landed, v_recv.at[step, 0])
        if last:
            scalar_rows = [t_rows[j] for j in range(GROUP)]
        else:
            scalar_rows = [s1_recv[step, j][7:8] for j in range(GROUP)]
        sums = tree(scalar_rows)
        if first:
            rr = from_lanes(sums, CHUNK + 48)
            share = sums
        else:
            held = (lane >= CHUNK + 48) & (lane < CHUNK + 63)
            under = jnp.where(held, to_lanes(rr, CHUNK + 48), 1.0)
            senders = jnp.concatenate(scalar_rows, axis=0)
            true = jnp.where(held, sums, 0.0) / under
            off = true - jnp.where(held, senders * float(GROUP), 0.0) / under
            off = pltpu.roll(off, 80, 1)
            share = senders + off * (pltpu.roll(senders, 112, 1) + off * pltpu.roll(senders, 96, 1))
            share = jnp.sum(share, axis=0, keepdims=True)
            new = from_lanes(sums, CHUNK + 48)
            beta = ratio(new, rr)
            rr = new
        if last:
            t_send[1] = share
            t_cols[here] = share
        else:
            own = tree([s1_recv[step, j] for j in range(GROUP)])
            if not first:
                own = own + jnp.where(left_half, beta[0:8], beta[8:16]) * s2_send[step - 1]
            own = put_scalars(own, share)
            s2_send[step] = own
            s2_cols[step, here] = own

        def send2(j):
            src = t_send.at[1] if last else s2_send.at[step]
            dst = t_cols.at[here] if last else s2_cols.at[step, here]
            remote(src, dst, v_send.at[step, 1], v_recv.at[step, 1], col_peer(j)).start()

        far_first(GROUP, send2)
        landed = t_cols.at[pl.ds(0, 15)] if last else s2_cols.at[step, pl.ds(0, 15)]
        drains.append((landed, v_send.at[step, 1]))
        if not last:
            s2_rows[step, me] = own

            def send_rows(j):
                remote(
                    s2_send.at[step], s2_rows.at[step, me], v_send.at[step, 2], v_recv.at[step, 2], row_peer(j)[1]
                ).start()

            far_first(GROUP, send_rows)
            drains.append((s2_rows.at[step, pl.ds(0, 15)], v_send.at[step, 2]))
        if first:
            prev[...] = applied
        else:
            drow[...] = rrow[...] + beta * drow[...]
            if not last:
                prev[...] = applied + beta * prev[...]
                dcol[...] = rcol[...] + beta * dcol[...]
        if last:
            hi, mid, low = split3(xrow[:, half])
            hi2, mid2, low2 = split3(drow[:, half])
            three[...] = jnp.concatenate([hi, hi2, mid, mid2, low, low2], axis=0)
            predict_theirs()
            predict_own()
        else:
            fill(waits[step][1])
        wait_for(landed, v_recv.at[step, 1])
        if last:
            total = tree([t_cols[j] for j in range(GROUP)])
        else:
            total = tree([s2_cols[step, j][7:8] for j in range(GROUP)])
        alpha = ratio(rr, from_lanes(total, CHUNK))
        if not last:
            rcol[...] = rcol[...] - alpha * (unpack(s2_cols.at[step]) + RIDGE * dcol[...])
            xrow[...] = xrow[...] + alpha * drow[...]
            wait_for(s2_rows.at[step, pl.ds(0, 15)], v_recv.at[step, 2])
            rrow[...] = rrow[...] - alpha * (unpack(s2_rows.at[step]) + RIDGE * drow[...])

    for j in range(GROUP - 1, -1, -1):
        value = both[j, 0:16, :] + alpha * both[j, 16:32, :]
        if j > 0:
            pred_send[j] = value
            remote(pred_send.at[j], pred_recv.at[chip], pred_ss, pred_rs, col_peer(j)).start()
        else:
            pred_recv[chip] = value

    drains.append((sib_recv, sib_ss))
    drains.append((pred_recv.at[pl.ds(0, 15)], pred_ss))

    xrow[...] = xrow[...] + alpha * drow[...]
    pair = xrow[:, pl.ds(pl.multiple_of((me // 2) * 128, 128), 128)]
    own_x = jnp.where(lax.rem(me, 2) == 0, pair, pltpu.roll(pair, CHUNK, 1))
    out_ref[CHUNK:CHUNK + 16, 0:128] = own_x
    out_ref[CHUNK:CHUNK + 16, 128:FEAT] = jnp.zeros((16, 128), F32)
    hi, mid, low = split3(xrow[:, half])
    wide = jnp.concatenate([hi.astype(F32), mid.astype(F32), jnp.zeros((96, HALF), F32)], axis=0)
    xt[...] = wide.T[:, 0:32].astype(BF16)
    gsum[...] = jnp.zeros_like(gsum)
    csum[...] = jnp.zeros_like(csum)
    tlab_copy.wait()
    labels = jnp.concatenate([tlab[...], jnp.zeros((1, TILE), F32)], axis=0)

    wait_for(pred_recv.at[pl.ds(0, 15)], pred_rs)
    own_err = (tree([pred_recv[j] for j in range(GROUP)]) - labels).astype(BF16)
    err_own[...] = own_err
    err[r] = own_err

    for j in range(1, GROUP):
        remote(err_own, err.at[r], err_ss, err_rs.at[r], col_peer(j)).start()
    drains.append((err.at[pl.ds(0, 15)], err_ss))

    def add_tiles(tiles):
        part, sums = None, None
        for t in tiles:
            e = err[t]
            mix = dot(xt[...], jnp.concatenate([e, e], axis=0))
            weights = mix.astype(BF16) * kk_hi[t]
            product = dot(weights, tgt[t])
            back = weights.astype(F32)
            back = back[:, 0:128] + back[:, 128:256]
            part = product if part is None else part + product
            sums = back if sums is None else sums + back
        gsum[...] += part
        csum[...] += sums

    def take_own(j):
        t = tile_at(2 * j)

        @pl.when(j > 0)
        def _():
            wait_for(err.at[0], err_rs.at[t])

        remote(err.at[t], err.at[t], pass_ss, err_rs.at[t], (other, c)).start()
        return t

    def take_theirs(j):
        t = tile_at(2 * j + 1)
        wait_for(err.at[0], err_rs.at[t])
        return t

    zero = jnp.int32(0)
    add_tiles([take_own(zero), take_own(zero + 1)])

    @pl.loop(1, 8)
    def _(s):
        mine = [take_own(2 * s), take_own(2 * s + 1)]
        add_tiles([take_theirs(2 * s - 2), take_theirs(2 * s - 1)] + mine)

    add_tiles([take_theirs(zero + 14), take_theirs(zero + 15)])
    drains.append((err.at[pl.ds(0, 16)], pass_ss))

    scale = 1.0 / 256.0
    term = (gsum[...] - lane_sum(csum[...]) * rf[block].reshape(HALF, FEAT).astype(F32)) * scale
    g_send[...] = term.reshape(8, CHUNK, FEAT)
    g_recv[c] = g_send[c]

    for j in range(7, 0, -1):
        remote(g_send.at[col_peers[j][1]], g_recv.at[c], g_ss, g_rs, col_peers[j]).start()

    drains.append((g_recv.at[pl.ds(0, 7)], g_ss))
    wait_for(g_recv.at[pl.ds(0, 7)], g_rs)
    out_ref[0:CHUNK, :] = tree([g_recv[j] for j in range(8)])

    for ref, sem in drains:
        wait_for(ref, sem)


def part_outputs(joint_ref, coef_ref, grad_ref):
    coef_ref[...] = joint_ref[CHUNK:CHUNK + 15, 0:CHUNK]
    grad_ref[...] = joint_ref[0:CHUNK, :]


def body(support, support_labels, targets, target_labels):
    classes = support_labels.shape[0]
    vmem = pl.BlockSpec(memory_space=pltpu.VMEM)
    anywhere = pl.BlockSpec(memory_space=pl.ANY)
    dma = pltpu.SemaphoreType.DMA
    joint = pl.pallas_call(
        kernel,
        out_shape=jax.ShapeDtypeStruct((CHUNK + 16, FEAT), F32),
        in_specs=[vmem, vmem, anywhere, anywhere],
        out_specs=vmem,
        scratch_shapes=[
            pltpu.VMEM((TILES, TILE, FEAT), BF16),
            pltpu.VMEM((classes, TILE), F32),
            pltpu.VMEM((CHUNK, FEAT), BF16),
            pltpu.VMEM((8, 128), F32),
            pltpu.VMEM((GROUP, CHUNK, FEAT), BF16),
            pltpu.VMEM((GROUP, CHUNK, FEAT), BF16),
            pltpu.VMEM((GROUP, 8, 128), F32),
            pltpu.VMEM((GROUP, 8, 128), F32),
            pltpu.VMEM((1, WIDE), F32),
            pltpu.VMEM((HALF, 1), F32),
            pltpu.VMEM((WIDE, WIDE), BF16),
            pltpu.VMEM((WIDE, WIDE), BF16),
            pltpu.VMEM((TILES, HALF, TILE), BF16),
            pltpu.VMEM((TILES, HALF, TILE), BF16),
            pltpu.VMEM((2, GROUP, 8, 128), F32),
            pltpu.VMEM((2, GROUP, 8, 128), F32),
            pltpu.VMEM((2, 8, 128), F32),
            pltpu.VMEM((2, GROUP, 8, 128), F32),
            pltpu.VMEM((2, GROUP, 8, 128), F32),
            pltpu.VMEM((2, 1, 128), F32),
            pltpu.VMEM((GROUP, 1, 128), F32),
            pltpu.VMEM((GROUP, 1, 128), F32),
            pltpu.VMEM((GROUP, WIDE), F32),
            pltpu.VMEM((GROUP, WIDE), F32),
            pltpu.VMEM((GROUP, WIDE), F32),
            pltpu.VMEM((GROUP, WIDE), F32),
            pltpu.VMEM((GROUP, WIDE), F32),
            pltpu.VMEM((GROUP, WIDE), F32),
            pltpu.VMEM((96, HALF), BF16),
            pltpu.VMEM((GROUP, 32, TILE), F32),
            pltpu.VMEM((GROUP, 32, TILE), F32),
            pltpu.VMEM((GROUP, 32, TILE), F32),
            pltpu.VMEM((GROUP, 16, TILE), F32),
            pltpu.VMEM((GROUP, 16, TILE), F32),
            pltpu.VMEM((16, TILE), BF16),
            pltpu.VMEM((TILES, 16, TILE), BF16),
            pltpu.VMEM((HALF, 32), BF16),
            pltpu.VMEM((HALF, FEAT), F32),
            pltpu.VMEM((HALF, 128), F32),
            pltpu.VMEM((8, CHUNK, FEAT), F32),
            pltpu.VMEM((8, CHUNK, FEAT), F32),
            dma((2,)),
            dma((4,)),
            dma((4,)),
            dma((GROUP,)),
            dma((2,)),
            dma((4,)),
            dma((4,)),
            dma((3, 3)),
            dma((3, 3)),
            dma,
            dma((4,)),
            dma,
            dma,
            dma,
            dma((TILES,)),
            dma,
            dma,
            dma,
        ],
        compiler_params=pltpu.CompilerParams(
            collective_id=0, has_side_effects=True, vmem_limit_bytes=58 * 1024 * 1024
        ),
    )(support, support_labels, targets.reshape(TILES, TILE, FEAT), target_labels)
    return pl.pallas_call(
        part_outputs,
        out_shape=(
            jax.ShapeDtypeStruct((classes, CHUNK), F32),
            jax.ShapeDtypeStruct((CHUNK, FEAT), F32),
        ),
        in_specs=[vmem],
        out_specs=(vmem, vmem),
    )(joint)


def solution(mesh):
    in_specs = (P(("row", "col"), None), P(None, ("row", "col")), P("col", None), P(None, "col"))
    out_specs = (P(None, ("row", "col")), P(("row", "col"), None))
    return jax.shard_map(body, mesh=mesh, in_specs=in_specs, out_specs=out_specs, check_vma=False)
```

```python
import jax
import jax.numpy as jnp
from jax import lax
from jax.experimental import pallas as pl
from jax.experimental.pallas import tpu as pltpu
from jax.sharding import PartitionSpec as P

MESH = pl.DeviceIdType.MESH
F32 = jnp.float32
BF16 = jnp.bfloat16

CHUNK = 64
FEAT = 256
TILE = 256
TILES = 32
GROUP = 16
WIDE = GROUP * CHUNK
HALF = WIDE // 2
RIDGE = 0.5
NN = (((1,), (0,)), ((), ()))
NT = (((1,), (1,)), ((), ()))


def dot(a, b, dims=NN):
    return lax.dot_general(a, b, dims, preferred_element_type=F32)


def split3(v):
    hi = v.astype(BF16)
    rest = v - hi.astype(F32)
    mid = rest.astype(BF16)
    low = (rest - mid.astype(F32)).astype(BF16)
    return hi, mid, low


def row_norms(rows):
    square = jnp.square(rows.astype(F32))
    hi = square.astype(BF16)
    low = (square - hi.astype(F32)).astype(BF16)
    ones = jnp.ones((8, FEAT), BF16)
    return 0.5 * (dot(ones, hi, NT) + dot(ones, low, NT))[0:1, :]


def column_norms(rows):
    return 0.5 * jnp.sum(jnp.square(rows.astype(F32)), axis=1, keepdims=True)


def pack_pair(v):
    left = lax.broadcasted_iota(jnp.int32, (8, 128), 1) < CHUNK
    top, bottom = v[0:8], v[8:16]
    first = jnp.where(left, top, pltpu.roll(bottom, CHUNK, 1))
    second = jnp.where(left, pltpu.roll(top, CHUNK, 1), bottom)
    return first, second


def unpack_pair(a, b):
    left = lax.broadcasted_iota(jnp.int32, (8, 128), 1) < CHUNK
    top = jnp.where(left, a, pltpu.roll(b, CHUNK, 1))
    bottom = jnp.where(left, pltpu.roll(a, CHUNK, 1), b)
    return jnp.concatenate([top, bottom], axis=0)


def unpack(ref):
    wide = jnp.concatenate([unpack_pair(ref[2 * j], ref[2 * j + 1]) for j in range(GROUP // 2)], axis=1)
    return jnp.where(lax.broadcasted_iota(jnp.int32, wide.shape, 0) < 15, wide, 0.0)


def gray(j):
    return j + (j // 2) * (5 - 2 * j)


def to_lanes(q, shift):
    sub = lax.broadcasted_iota(jnp.int32, (16, 128), 0)
    lane = lax.broadcasted_iota(jnp.int32, (16, 128), 1)
    return jnp.sum(jnp.where(lane == sub + shift, q, 0.0), axis=0, keepdims=True)


def from_lanes(row, shift):
    sub = lax.broadcasted_iota(jnp.int32, (16, 128), 0)
    lane = lax.broadcasted_iota(jnp.int32, (16, 128), 1)
    return jnp.sum(jnp.where(lane == sub + shift, row, 0.0), axis=1, keepdims=True)


def put_scalars(message, row):
    sub = lax.broadcasted_iota(jnp.int32, (8, 128), 0)
    lane = lax.broadcasted_iota(jnp.int32, (8, 128), 1)
    return jnp.where((sub == 7) & (lane >= CHUNK), row, message)


def lane_sum(v):
    return jnp.sum(v, axis=1, keepdims=True)


def ratio(a, b):
    real = lax.broadcasted_iota(jnp.int32, (16, 1), 0) < 15
    return jnp.where(real, a, 0.0) / jnp.where(real, b, 1.0)


def tree(values):
    values = list(values)
    while len(values) > 1:
        values = [values[i] + values[i + 1] if i + 1 < len(values) else values[i] for i in range(0, len(values), 2)]
    return values[0]


def kernel(
    sup_ref, lab_ref, tgt_hbm, tlab_hbm,
    out_ref,
    tgt, tlab, sup_v, lab_v, rf, cf, lab_rows, lab_cols, rn_ref, sn_ref,
    kt_hi, kt_lo, kk_hi, kk_lo,
    s1_send, s1_recv, s2_send, s2_rows, s2_cols, t_send, t_rows, t_cols,
    drow, rrow, xrow, dcol, rcol, prev,
    three, both, sib_send, sib_recv, pred_send, pred_recv, err_own, err, xt, gsum, csum, g_send, g_recv,
    local_sems, f_send, z_recv, x_recv, r_recv, l_send, lz_recv, l_recv, v_send, v_recv,
    sib_ss, sib_rs, pred_ss, pred_rs, err_ss, err_rs, pass_ss, g_ss, g_rs,
):
    r = lax.axis_index("row")
    c = lax.axis_index("col")
    chip, core = r // 2, lax.rem(r, 2)
    z, x = chip // 4, lax.rem(chip, 4)
    zl, y = c // 4, lax.rem(c, 4)
    me = core * 8 + c
    here = x * 4 + z

    def device(pz, px):
        return (2 * (pz * 4 + px) + core, c)

    xs = [lax.rem(x + d, 4) for d in range(4)]
    zs = [lax.rem(z + d, 4) for d in range(4)]
    ys = [lax.rem(y + d, 4) for d in range(4)]
    ls = [zl, 1 - zl]
    ks = [core, 1 - core]

    def row_peer(j):
        k, p = ks[j % 2], ls[j // 8] * 4 + ys[gray((j // 2) % 4)]
        return k * 8 + p, (2 * chip + k, p)

    def col_peer(j):
        return (2 * (zs[gray(j // 4)] * 4 + xs[gray(j % 4)]) + core, c)

    def tile_at(j):
        j = jnp.int32(j)
        chip_there = lax.rem(z + gray(j // 8), 4) * 4 + lax.rem(x + gray((j // 2) % 4), 4)
        return 2 * chip_there + lax.rem(core + j % 2, 2)

    def far_first(count, act):
        for j in range(count - 1, 0, -1):
            act(j)

    tgt_copy = pltpu.make_async_copy(tgt_hbm, tgt, local_sems.at[0])
    tgt_copy.start()
    start_lane = pl.multiple_of(r * TILE, TILE)
    tlab_copy = pltpu.make_async_copy(tlab_hbm.at[:, pl.ds(start_lane, TILE)], tlab, local_sems.at[1])
    tlab_copy.start()

    barrier = pltpu.get_barrier_semaphore()
    for d in (1, 3):
        pl.semaphore_signal(barrier, inc=1, device_id=device(zs[d], x), device_id_type=MESH)
    far_first(4, lambda j: pl.semaphore_signal(barrier, inc=1, device_id=device(z, xs[j]), device_id_type=MESH))
    far_first(
        GROUP, lambda j: pl.semaphore_signal(barrier, inc=1, device_id=row_peer(j)[1], device_id_type=MESH)
    )

    lab = jnp.concatenate([lab_ref[...], jnp.zeros((1, CHUNK), F32)], axis=0)
    lab_v[...] = jnp.concatenate([lab[0:8], lab[8:16]], axis=1)
    sup = sup_ref[...]
    sup_v[...] = sup
    rf[me] = sup
    cf[here] = sup
    lab_rows[me] = lab_v[...]
    lab_cols[here] = lab_v[...]

    pl.semaphore_wait(barrier, 20)

    drains = []

    def remote(src, dst, ss, rs, to):
        return pltpu.make_async_remote_copy(
            src_ref=src, dst_ref=dst, send_sem=ss, recv_sem=rs, device_id=to, device_id_type=MESH
        )

    def wait_for(ref, sem):
        pltpu.make_async_copy(ref, ref, sem).wait()

    def to_x(dz, steps):
        slot = xs[0] * 4 + zs[dz]
        for d in steps:
            remote(cf.at[slot], cf.at[slot], f_send.at[2], x_recv.at[slot], device(z, xs[d])).start()

    def from_x(dx, dz):
        slot = xs[dx] * 4 + zs[dz]
        wait_for(cf.at[0], x_recv.at[slot])
        return slot

    def pass_on(dx, dz):
        slot = from_x(dx, dz)
        remote(cf.at[slot], cf.at[slot], f_send.at[2], x_recv.at[slot], device(z, xs[4 - dx])).start()

    col_peers = [(r, ls[j // 4] * 4 + ys[gray(j % 4)]) for j in range(8)]
    for d in (1, 3):
        remote(sup_v, cf.at[here], f_send.at[0], z_recv.at[z], device(zs[d], x)).start()
    to_x(0, (1, 3))
    for j in range(7, 0, -1):
        remote(sup_v, rf.at[me], f_send.at[1], r_recv.at[0], col_peers[j]).start()
    for d in (1, 3):
        remote(lab_v, lab_cols.at[here], l_send.at[0], lz_recv.at[z], device(zs[d], x)).start()
    for j in range(7, 0, -1):
        remote(lab_v, lab_rows.at[me], l_send.at[1], l_recv.at[1], col_peers[j]).start()

    beside = x * 4 + zs[1]
    wait_for(cf.at[0], z_recv.at[zs[1]])
    remote(cf.at[beside], cf.at[beside], f_send.at[0], z_recv.at[zs[1]], device(zs[3], x)).start()
    to_x(1, (1, 3))
    wait_for(cf.at[0], z_recv.at[zs[3]])
    to_x(3, (1, 3))
    pass_on(1, 0)
    wait_for(cf.at[0], z_recv.at[zs[2]])
    to_x(2, (1, 3))
    wait_for(lab_cols.at[0], lz_recv.at[zs[1]])
    remote(lab_cols.at[beside], lab_cols.at[beside], l_send.at[0], lz_recv.at[zs[1]], device(zs[3], x)).start()

    block = pl.ds(core * 8, 8)
    other = 2 * chip + 1 - core
    wait_for(rf.at[pl.ds(0, 7)], r_recv.at[0])
    remote(rf.at[block], rf.at[block], f_send.at[3], r_recv.at[1], (other, c)).start()
    pass_on(3, 1)
    pass_on(3, 3)
    wait_for(lab_cols.at[0], lz_recv.at[zs[3]])
    wait_for(lab_cols.at[0], lz_recv.at[zs[2]])
    for d in (2, 3, 1):
        four = lab_cols.at[pl.ds(x * 4, 4)]
        remote(four, four, l_send.at[2], l_recv.at[2], device(z, xs[d])).start()
    pass_on(1, 2)
    wait_for(lab_rows.at[pl.ds(0, 7)], l_recv.at[1])
    remote(lab_rows.at[block], lab_rows.at[block], l_send.at[3], l_recv.at[3], (other, c)).start()

    drains.append((cf.at[pl.ds(0, 3)], f_send.at[0]))
    drains.append((rf.at[pl.ds(0, 7)], f_send.at[1]))
    drains.append((cf.at[pl.ds(0, 12)], f_send.at[2]))
    drains.append((rf.at[pl.ds(0, 8)], f_send.at[3]))
    drains.append((lab_cols.at[pl.ds(0, 3)], l_send.at[0]))
    drains.append((lab_rows.at[pl.ds(0, 7)], l_send.at[1]))
    drains.append((lab_cols.at[pl.ds(0, 12)], l_send.at[2]))
    drains.append((lab_rows.at[pl.ds(0, 8)], l_send.at[3]))

    half = pl.ds(pl.multiple_of(core * HALF, HALF), HALF)
    sn_ref[...] = column_norms(rf[block].reshape(HALF, FEAT))
    tgt_copy.wait()

    def target_tile(i):
        rows = tgt[i]
        inner = dot(rf[block].reshape(HALF, FEAT), rows, NT)
        value = jnp.exp(inner - sn_ref[...] - row_norms(rows))
        hi = value.astype(BF16)
        kk_hi[i] = hi
        kk_lo[i] = (value - hi.astype(F32)).astype(BF16)

    done = [0]

    def fill(count):
        stop = min(TILES, done[0] + count)
        if stop > done[0]:

            @pl.loop(done[0] // 2, stop // 2)
            def _(i):
                target_tile(2 * i)
                target_tile(2 * i + 1)

        done[0] = stop

    wait_for(rf.at[pl.ds(0, 8)], r_recv.at[1])
    rn_ref[...] = row_norms(rf[...].reshape(WIDE, FEAT))

    @pl.loop(0, 4)
    def _(i):
        @pl.when(i == 1)
        def _():
            from_x(1, 1)
            from_x(1, 3)

        @pl.when(i == 2)
        def _():
            from_x(3, 0)
            from_x(3, 2)

        @pl.when(i == 3)
        def _():
            for d in range(4):
                from_x(2, d)

        px = lax.rem(x + gray(i), 4)
        part = cf[pl.ds(px * 4, 4)].reshape(TILE, FEAT)
        inner = dot(part, rf[...].reshape(WIDE, FEAT), NT)
        value = jnp.exp(inner - column_norms(part) - rn_ref[...])
        hi = value.astype(BF16)
        where = pl.ds(pl.multiple_of(px * TILE, TILE), TILE)
        kt_hi[where, :] = hi
        kt_lo[where, :] = (value - hi.astype(F32)).astype(BF16)

    def apply_tile(v):
        hi, mid, low = split3(v)
        big = dot(jnp.concatenate([hi, mid, low], axis=0), kt_hi[...])
        small = dot(jnp.concatenate([hi, mid], axis=0), kt_lo[...])
        return (big[0:16] + small[0:16]) + ((big[16:32] + small[16:32]) + big[32:48])

    wait_for(lab_cols.at[pl.ds(0, 12)], l_recv.at[2])
    b_cols = unpack(lab_cols)
    wait_for(lab_rows.at[pl.ds(0, 8)], l_recv.at[3])
    b_rows = unpack(lab_rows)
    drow[...] = b_rows
    rrow[...] = b_rows
    xrow[...] = jnp.zeros_like(b_rows)
    dcol[...] = b_cols
    rcol[...] = b_cols
    rr = None

    def predict_tile(t):
        big = dot(three[...], kk_hi[t])
        small = dot(three[0:64, :], kk_lo[t])
        return (big[0:32] + small[0:32]) + ((big[32:64] + small[32:64]) + big[64:96])

    def predict_theirs():
        @pl.loop(0, 4)
        def _(g):
            for k in range(4):
                j = 12 - 4 * g + k
                sib_send[j] = predict_tile(tile_at(2 * j + 1))
            quarter = pl.ds(12 - 4 * g, 4)
            remote(sib_send.at[quarter], sib_recv.at[quarter], sib_ss, sib_rs.at[3 - g], (other, c)).start()

    def predict_own():
        @pl.loop(0, 4)
        def _(g):
            wait_for(sib_recv.at[pl.ds(0, 4)], sib_rs.at[3 - g])
            for k in range(4):
                j = 12 - 4 * g + k
                both[j] = predict_tile(tile_at(2 * j)) + sib_recv[j]

    lane = lax.broadcasted_iota(jnp.int32, (1, 128), 1)
    left_half = lax.broadcasted_iota(jnp.int32, (8, 128), 1) < CHUNK
    waits = ((0, 12), (6, 14))
    for step in range(3):
        first, last = step == 0, step == 2
        norm = lane_sum(rcol[...] * rcol[...])
        applied = apply_tile(rcol[...])
        small_ridge = RIDGE / GROUP
        if first:
            d = drow[...]
            guess = applied
            scalars = to_lanes(lane_sum(d * (applied + small_ridge * d)), CHUNK) + to_lanes(norm, CHUNK + 48)
        else:
            near = ratio(norm * float(GROUP), rr)
            old = drow[...]
            d = rrow[...] + near * old
            guess = applied + near * prev[...]
            by_d = guess + small_ridge * d
            by_old = prev[...] + small_ridge * old
            scalars = to_lanes(lane_sum(d * by_d), CHUNK) + to_lanes(lane_sum(d * by_old + old * by_d), CHUNK + 16)
            scalars = scalars + to_lanes(lane_sum(old * by_old), CHUNK + 32) + to_lanes(norm, CHUNK + 48)
        if last:
            t_send[0] = scalars
            t_rows[me] = scalars
        else:
            for j in range(GROUP // 2):
                a, b = pack_pair(applied[:, 128 * j:128 * (j + 1)])
                s1_send[step, 2 * j] = put_scalars(a, scalars)
                s1_send[step, 2 * j + 1] = put_scalars(b, scalars)
            s1_recv[step, me] = s1_send[step, me]

        def send1(j):
            p, to = row_peer(j)
            src = t_send.at[0] if last else s1_send.at[step, p]
            dst = t_rows.at[me] if last else s1_recv.at[step, me]
            remote(src, dst, v_send.at[step, 0], v_recv.at[step, 0], to).start()

        far_first(GROUP, send1)
        landed = t_rows.at[pl.ds(0, 15)] if last else s1_recv.at[step, pl.ds(0, 15)]
        drains.append((landed, v_send.at[step, 0]))
        if last:
            fill(TILES)
        else:
            fill(waits[step][0])
        wait_for(landed, v_recv.at[step, 0])
        if last:
            scalar_rows = [t_rows[j] for j in range(GROUP)]
        else:
            scalar_rows = [s1_recv[step, j][7:8] for j in range(GROUP)]
        sums = tree(scalar_rows)
        if first:
            rr = from_lanes(sums, CHUNK + 48)
            share = sums
        else:
            held = (lane >= CHUNK + 48) & (lane < CHUNK + 63)
            under = jnp.where(held, to_lanes(rr, CHUNK + 48), 1.0)
            senders = jnp.concatenate(scalar_rows, axis=0)
            true = jnp.where(held, sums, 0.0) / under
            off = true - jnp.where(held, senders * float(GROUP), 0.0) / under
            off = pltpu.roll(off, 80, 1)
            share = senders + off * (pltpu.roll(senders, 112, 1) + off * pltpu.roll(senders, 96, 1))
            share = jnp.sum(share, axis=0, keepdims=True)
            new = from_lanes(sums, CHUNK + 48)
            beta = ratio(new, rr)
            rr = new
        if last:
            t_send[1] = share
            t_cols[here] = share
        else:
            own = tree([s1_recv[step, j] for j in range(GROUP)])
            if not first:
                own = own + jnp.where(left_half, beta[0:8], beta[8:16]) * s2_send[step - 1]
            own = put_scalars(own, share)
            s2_send[step] = own
            s2_cols[step, here] = own

        def send2(j):
            src = t_send.at[1] if last else s2_send.at[step]
            dst = t_cols.at[here] if last else s2_cols.at[step, here]
            remote(src, dst, v_send.at[step, 1], v_recv.at[step, 1], col_peer(j)).start()

        far_first(GROUP, send2)
        landed = t_cols.at[pl.ds(0, 15)] if last else s2_cols.at[step, pl.ds(0, 15)]
        drains.append((landed, v_send.at[step, 1]))
        if not last:
            s2_rows[step, me] = own

            def send_rows(j):
                remote(
                    s2_send.at[step], s2_rows.at[step, me], v_send.at[step, 2], v_recv.at[step, 2], row_peer(j)[1]
                ).start()

            far_first(GROUP, send_rows)
            drains.append((s2_rows.at[step, pl.ds(0, 15)], v_send.at[step, 2]))
        if first:
            prev[...] = applied
        else:
            drow[...] = rrow[...] + beta * drow[...]
            if not last:
                prev[...] = applied + beta * prev[...]
                dcol[...] = rcol[...] + beta * dcol[...]
        if last:
            hi, mid, low = split3(xrow[:, half])
            hi2, mid2, low2 = split3(drow[:, half])
            three[...] = jnp.concatenate([hi, hi2, mid, mid2, low, low2], axis=0)
            predict_theirs()
            drains.append((sib_recv, sib_ss))
            predict_own()
        else:
            fill(waits[step][1])
        wait_for(landed, v_recv.at[step, 1])
        if last:
            total = tree([t_cols[j] for j in range(GROUP)])
        else:
            total = tree([s2_cols[step, j][7:8] for j in range(GROUP)])
        alpha = ratio(rr, from_lanes(total, CHUNK))
        if not last:
            rcol[...] = rcol[...] - alpha * (unpack(s2_cols.at[step]) + RIDGE * dcol[...])
            xrow[...] = xrow[...] + alpha * drow[...]
            wait_for(s2_rows.at[step, pl.ds(0, 15)], v_recv.at[step, 2])
            rrow[...] = rrow[...] - alpha * (unpack(s2_rows.at[step]) + RIDGE * drow[...])

    for j in range(GROUP - 1, -1, -1):
        value = both[j, 0:16, :] + alpha * both[j, 16:32, :]
        if j > 0:
            pred_send[j] = value
            remote(pred_send.at[j], pred_recv.at[chip], pred_ss, pred_rs, col_peer(j)).start()
        else:
            pred_recv[chip] = value

    drains.append((pred_recv.at[pl.ds(0, 15)], pred_ss))

    xrow[...] = xrow[...] + alpha * drow[...]
    pair = xrow[:, pl.ds(pl.multiple_of((me // 2) * 128, 128), 128)]
    own_x = jnp.where(lax.rem(me, 2) == 0, pair, pltpu.roll(pair, CHUNK, 1))
    out_ref[CHUNK:CHUNK + 16, 0:128] = own_x
    out_ref[CHUNK:CHUNK + 16, 128:FEAT] = jnp.zeros((16, 128), F32)
    hi, mid, low = split3(xrow[:, half])
    wide = jnp.concatenate([hi.astype(F32), mid.astype(F32), jnp.zeros((96, HALF), F32)], axis=0)
    xt[...] = wide.T[:, 0:32].astype(BF16)
    gsum[...] = jnp.zeros_like(gsum)
    csum[...] = jnp.zeros_like(csum)
    tlab_copy.wait()
    labels = jnp.concatenate([tlab[...], jnp.zeros((1, TILE), F32)], axis=0)

    wait_for(pred_recv.at[pl.ds(0, 15)], pred_rs)
    own_err = (tree([pred_recv[j] for j in range(GROUP)]) - labels).astype(BF16)
    err_own[...] = own_err
    err[r] = own_err

    for j in range(1, GROUP):
        remote(err_own, err.at[r], err_ss, err_rs.at[r], col_peer(j)).start()
    drains.append((err.at[pl.ds(0, 15)], err_ss))

    def add_tiles(tiles):
        part, sums = None, None
        for t in tiles:
            e = err[t]
            mix = dot(xt[...], jnp.concatenate([e, e], axis=0))
            weights = mix.astype(BF16) * kk_hi[t]
            product = dot(weights, tgt[t])
            back = weights.astype(F32)
            back = back[:, 0:128] + back[:, 128:256]
            part = product if part is None else part + product
            sums = back if sums is None else sums + back
        gsum[...] += part
        csum[...] += sums

    def take_own(j):
        t = tile_at(2 * j)

        @pl.when(j > 0)
        def _():
            wait_for(err.at[0], err_rs.at[t])

        remote(err.at[t], err.at[t], pass_ss, err_rs.at[t], (other, c)).start()
        return t

    def take_theirs(j):
        t = tile_at(2 * j + 1)
        wait_for(err.at[0], err_rs.at[t])
        return t

    zero = jnp.int32(0)
    add_tiles([take_own(zero), take_own(zero + 1)])

    @pl.loop(1, 8)
    def _(s):
        mine = [take_own(2 * s), take_own(2 * s + 1)]
        add_tiles([take_theirs(2 * s - 2), take_theirs(2 * s - 1)] + mine)

    add_tiles([take_theirs(zero + 14), take_theirs(zero + 15)])
    drains.append((err.at[pl.ds(0, 16)], pass_ss))

    scale = 1.0 / 256.0
    term = (gsum[...] - lane_sum(csum[...]) * rf[block].reshape(HALF, FEAT).astype(F32)) * scale
    g_send[...] = term.reshape(8, CHUNK, FEAT)
    g_recv[c] = g_send[c]

    for j in range(7, 0, -1):
        remote(g_send.at[col_peers[j][1]], g_recv.at[c], g_ss, g_rs, col_peers[j]).start()

    drains.append((g_recv.at[pl.ds(0, 7)], g_ss))
    wait_for(g_recv.at[pl.ds(0, 7)], g_rs)
    out_ref[0:CHUNK, :] = tree([g_recv[j] for j in range(8)])

    for ref, sem in drains:
        wait_for(ref, sem)


def part_outputs(joint_ref, coef_ref, grad_ref, rows, sems):
    first = pltpu.make_async_copy(joint_ref.at[pl.ds(0, CHUNK)], grad_ref, sems.at[0])
    second = pltpu.make_async_copy(joint_ref.at[pl.ds(CHUNK, 16)], rows, sems.at[1])
    first.start()
    second.start()
    second.wait()
    coef_ref[...] = rows[0:15, 0:CHUNK]
    first.wait()


def body(support, support_labels, targets, target_labels):
    classes = support_labels.shape[0]
    vmem = pl.BlockSpec(memory_space=pltpu.VMEM)
    anywhere = pl.BlockSpec(memory_space=pl.ANY)
    dma = pltpu.SemaphoreType.DMA
    joint = pl.pallas_call(
        kernel,
        out_shape=jax.ShapeDtypeStruct((CHUNK + 16, FEAT), F32),
        in_specs=[vmem, vmem, anywhere, anywhere],
        out_specs=vmem,
        scratch_shapes=[
            pltpu.VMEM((TILES, TILE, FEAT), BF16),
            pltpu.VMEM((classes, TILE), F32),
            pltpu.VMEM((CHUNK, FEAT), BF16),
            pltpu.VMEM((8, 128), F32),
            pltpu.VMEM((GROUP, CHUNK, FEAT), BF16),
            pltpu.VMEM((GROUP, CHUNK, FEAT), BF16),
            pltpu.VMEM((GROUP, 8, 128), F32),
            pltpu.VMEM((GROUP, 8, 128), F32),
            pltpu.VMEM((1, WIDE), F32),
            pltpu.VMEM((HALF, 1), F32),
            pltpu.VMEM((WIDE, WIDE), BF16),
            pltpu.VMEM((WIDE, WIDE), BF16),
            pltpu.VMEM((TILES, HALF, TILE), BF16),
            pltpu.VMEM((TILES, HALF, TILE), BF16),
            pltpu.VMEM((2, GROUP, 8, 128), F32),
            pltpu.VMEM((2, GROUP, 8, 128), F32),
            pltpu.VMEM((2, 8, 128), F32),
            pltpu.VMEM((2, GROUP, 8, 128), F32),
            pltpu.VMEM((2, GROUP, 8, 128), F32),
            pltpu.VMEM((2, 1, 128), F32),
            pltpu.VMEM((GROUP, 1, 128), F32),
            pltpu.VMEM((GROUP, 1, 128), F32),
            pltpu.VMEM((GROUP, WIDE), F32),
            pltpu.VMEM((GROUP, WIDE), F32),
            pltpu.VMEM((GROUP, WIDE), F32),
            pltpu.VMEM((GROUP, WIDE), F32),
            pltpu.VMEM((GROUP, WIDE), F32),
            pltpu.VMEM((GROUP, WIDE), F32),
            pltpu.VMEM((96, HALF), BF16),
            pltpu.VMEM((GROUP, 32, TILE), F32),
            pltpu.VMEM((GROUP, 32, TILE), F32),
            pltpu.VMEM((GROUP, 32, TILE), F32),
            pltpu.VMEM((GROUP, 16, TILE), F32),
            pltpu.VMEM((GROUP, 16, TILE), F32),
            pltpu.VMEM((16, TILE), BF16),
            pltpu.VMEM((TILES, 16, TILE), BF16),
            pltpu.VMEM((HALF, 32), BF16),
            pltpu.VMEM((HALF, FEAT), F32),
            pltpu.VMEM((HALF, 128), F32),
            pltpu.VMEM((8, CHUNK, FEAT), F32),
            pltpu.VMEM((8, CHUNK, FEAT), F32),
            dma((2,)),
            dma((4,)),
            dma((4,)),
            dma((GROUP,)),
            dma((2,)),
            dma((4,)),
            dma((4,)),
            dma((4,)),
            dma((3, 3)),
            dma((3, 3)),
            dma,
            dma((4,)),
            dma,
            dma,
            dma,
            dma((TILES,)),
            dma,
            dma,
            dma,
        ],
        compiler_params=pltpu.CompilerParams(
            collective_id=0, has_side_effects=True, vmem_limit_bytes=58 * 1024 * 1024
        ),
    )(support, support_labels, targets.reshape(TILES, TILE, FEAT), target_labels)
    return pl.pallas_call(
        part_outputs,
        out_shape=(
            jax.ShapeDtypeStruct((classes, CHUNK), F32),
            jax.ShapeDtypeStruct((CHUNK, FEAT), F32),
        ),
        in_specs=[anywhere],
        out_specs=(vmem, anywhere),
        scratch_shapes=[pltpu.VMEM((16, FEAT), F32), dma((2,))],
        compiler_params=pltpu.CompilerParams(vmem_limit_bytes=58 * 1024 * 1024),
    )(joint)


def solution(mesh):
    in_specs = (P(("row", "col"), None), P(None, ("row", "col")), P("col", None), P(None, "col"))
    out_specs = (P(None, ("row", "col")), P(("row", "col"), None))
    return jax.shard_map(body, mesh=mesh, in_specs=in_specs, out_specs=out_specs, check_vma=False)
```

```python
import jax
import jax.numpy as jnp
from jax import lax
from jax.experimental import pallas as pl
from jax.experimental.pallas import tpu as pltpu
from jax.sharding import PartitionSpec as P

MESH = pl.DeviceIdType.MESH
F32 = jnp.float32
BF16 = jnp.bfloat16

CHUNK = 64
FEAT = 256
TILE = 256
TILES = 32
GROUP = 16
WIDE = GROUP * CHUNK
HALF = WIDE // 2
RIDGE = 0.5
FILL = (12, 8, 8)
NN = (((1,), (0,)), ((), ()))
NT = (((1,), (1,)), ((), ()))


def dot(a, b, dims=NN):
    return lax.dot_general(a, b, dims, preferred_element_type=F32)


def split3(v):
    hi = v.astype(BF16)
    rest = v - hi.astype(F32)
    mid = rest.astype(BF16)
    low = (rest - mid.astype(F32)).astype(BF16)
    return hi, mid, low


def row_norms(rows):
    square = jnp.square(rows.astype(F32))
    hi = square.astype(BF16)
    low = (square - hi.astype(F32)).astype(BF16)
    ones = jnp.ones((8, FEAT), BF16)
    return 0.5 * (dot(ones, hi, NT) + dot(ones, low, NT))[0:1, :]


def column_norms(rows):
    return 0.5 * jnp.sum(jnp.square(rows.astype(F32)), axis=1, keepdims=True)


def pack_pair(v):
    left = lax.broadcasted_iota(jnp.int32, (8, 128), 1) < CHUNK
    top, bottom = v[0:8], v[8:16]
    first = jnp.where(left, top, pltpu.roll(bottom, CHUNK, 1))
    second = jnp.where(left, pltpu.roll(top, CHUNK, 1), bottom)
    return first, second


def unpack_pair(a, b):
    left = lax.broadcasted_iota(jnp.int32, (8, 128), 1) < CHUNK
    top = jnp.where(left, a, pltpu.roll(b, CHUNK, 1))
    bottom = jnp.where(left, pltpu.roll(a, CHUNK, 1), b)
    return jnp.concatenate([top, bottom], axis=0)


def unpack(ref):
    wide = jnp.concatenate([unpack_pair(ref[2 * j], ref[2 * j + 1]) for j in range(GROUP // 2)], axis=1)
    return jnp.where(lax.broadcasted_iota(jnp.int32, wide.shape, 0) < 15, wide, 0.0)


def gray(j):
    return j + (j // 2) * (5 - 2 * j)


def to_lanes(q, shift):
    sub = lax.broadcasted_iota(jnp.int32, (16, 128), 0)
    lane = lax.broadcasted_iota(jnp.int32, (16, 128), 1)
    return jnp.sum(jnp.where(lane == sub + shift, q, 0.0), axis=0, keepdims=True)


def from_lanes(row, shift):
    sub = lax.broadcasted_iota(jnp.int32, (16, 128), 0)
    lane = lax.broadcasted_iota(jnp.int32, (16, 128), 1)
    return jnp.sum(jnp.where(lane == sub + shift, row, 0.0), axis=1, keepdims=True)


def put_scalars(message, row):
    sub = lax.broadcasted_iota(jnp.int32, (8, 128), 0)
    lane = lax.broadcasted_iota(jnp.int32, (8, 128), 1)
    return jnp.where((sub == 7) & (lane >= CHUNK), row, message)


def lane_sum(v):
    return jnp.sum(v, axis=1, keepdims=True)


def ratio(a, b):
    real = lax.broadcasted_iota(jnp.int32, (16, 1), 0) < 15
    return jnp.where(real, a, 0.0) / jnp.where(real, b, 1.0)


def tree(values):
    values = list(values)
    while len(values) > 1:
        values = [values[i] + values[i + 1] if i + 1 < len(values) else values[i] for i in range(0, len(values), 2)]
    return values[0]


def kernel(
    sup_ref, lab_ref, tgt_hbm, tlab_hbm,
    out_ref,
    tgt, tlab, sup_v, lab_v, rf, cf, lab_rows, lab_cols, rn_ref, sn_ref,
    kt_hi, kt_lo, kk_hi, kk_lo,
    s1_send, s1_recv, s2_send, s2_rows, s2_cols, t_send, t_rows, t_cols,
    drow, rrow, xrow, dcol, rcol, prev,
    three, one, both, own2, sib_send, sib_recv, sib_send2, sib_recv2, pred_send, pred_recv, err_own, err, xt, gsum, csum, g_send, g_recv,
    local_sems, f_send, z_recv, x_recv, r_recv, l_send, l_recv, v_send, v_recv,
    sib_ss, sib_rs, pred_ss, pred_rs, err_ss, err_rs, pass_ss, g_ss, g_rs,
):
    r = lax.axis_index("row")
    c = lax.axis_index("col")
    chip, core = r // 2, lax.rem(r, 2)
    z, x = chip // 4, lax.rem(chip, 4)
    zl, y = c // 4, lax.rem(c, 4)
    me = core * 8 + c
    here = x * 4 + z

    def device(pz, px):
        return (2 * (pz * 4 + px) + core, c)

    xs = [lax.rem(x + d, 4) for d in range(4)]
    zs = [lax.rem(z + d, 4) for d in range(4)]
    ys = [lax.rem(y + d, 4) for d in range(4)]
    ls = [zl, 1 - zl]
    ks = [core, 1 - core]

    def row_peer(j):
        k, p = ks[j % 2], ls[j // 8] * 4 + ys[gray((j // 2) % 4)]
        return k * 8 + p, (2 * chip + k, p)

    def col_peer(j):
        return (2 * (zs[gray(j // 4)] * 4 + xs[gray(j % 4)]) + core, c)

    def tile_at(j):
        j = jnp.int32(j)
        chip_there = lax.rem(z + gray(j // 8), 4) * 4 + lax.rem(x + gray((j // 2) % 4), 4)
        return 2 * chip_there + lax.rem(core + j % 2, 2)

    def far_first(count, act):
        for j in range(count - 1, 0, -1):
            act(j)

    tgt_copy = pltpu.make_async_copy(tgt_hbm, tgt, local_sems.at[0])
    tgt_copy.start()
    start_lane = pl.multiple_of(r * TILE, TILE)
    tlab_copy = pltpu.make_async_copy(tlab_hbm.at[:, pl.ds(start_lane, TILE)], tlab, local_sems.at[1])
    tlab_copy.start()

    barrier = pltpu.get_barrier_semaphore()
    far_first(4, lambda j: pl.semaphore_signal(barrier, inc=1, device_id=device(zs[j], x), device_id_type=MESH))
    far_first(4, lambda j: pl.semaphore_signal(barrier, inc=1, device_id=device(z, xs[j]), device_id_type=MESH))
    far_first(
        GROUP, lambda j: pl.semaphore_signal(barrier, inc=1, device_id=row_peer(j)[1], device_id_type=MESH)
    )

    lab = jnp.concatenate([lab_ref[...], jnp.zeros((1, CHUNK), F32)], axis=0)
    lab_v[...] = jnp.concatenate([lab[0:8], lab[8:16]], axis=1)
    sup = sup_ref[...]
    sup_v[...] = sup
    rf[me] = sup
    cf[here] = sup
    lab_rows[me] = lab_v[...]
    lab_cols[here] = lab_v[...]

    pl.semaphore_wait(barrier, 21)

    drains = []

    def remote(src, dst, ss, rs, to):
        return pltpu.make_async_remote_copy(
            src_ref=src, dst_ref=dst, send_sem=ss, recv_sem=rs, device_id=to, device_id_type=MESH
        )

    def wait_for(ref, sem):
        pltpu.make_async_copy(ref, ref, sem).wait()

    def to_x(dz):
        slot = xs[0] * 4 + zs[dz]
        for d in (2, 1, 3):
            remote(cf.at[slot], cf.at[slot], f_send.at[2], x_recv.at[x], device(z, xs[d])).start()

    col_peers = [(r, ls[j // 4] * 4 + ys[gray(j % 4)]) for j in range(8)]
    for d in (2, 3, 1):
        remote(sup_v, cf.at[here], f_send.at[0], z_recv.at[z], device(zs[d], x)).start()
    to_x(0)
    for j in range(7, 0, -1):
        remote(sup_v, rf.at[me], f_send.at[1], r_recv.at[0], col_peers[j]).start()
    for d in (2, 3, 1):
        remote(lab_v, lab_cols.at[here], l_send.at[0], l_recv.at[0], device(zs[d], x)).start()
    for j in range(7, 0, -1):
        remote(lab_v, lab_rows.at[me], l_send.at[1], l_recv.at[1], col_peers[j]).start()

    for d in (1, 3):
        wait_for(cf.at[0], z_recv.at[zs[d]])
        to_x(d)
    wait_for(cf.at[0], z_recv.at[zs[2]])
    to_x(2)

    block = pl.ds(core * 8, 8)
    other = 2 * chip + 1 - core
    wait_for(rf.at[pl.ds(0, 7)], r_recv.at[0])
    remote(rf.at[block], rf.at[block], f_send.at[3], r_recv.at[1], (other, c)).start()
    wait_for(lab_cols.at[pl.ds(0, 3)], l_recv.at[0])
    for d in (2, 3, 1):
        four = lab_cols.at[pl.ds(x * 4, 4)]
        remote(four, four, l_send.at[2], l_recv.at[2], device(z, xs[d])).start()
    wait_for(lab_rows.at[pl.ds(0, 7)], l_recv.at[1])
    remote(lab_rows.at[block], lab_rows.at[block], l_send.at[3], l_recv.at[3], (other, c)).start()

    drains.append((cf.at[pl.ds(0, 3)], f_send.at[0]))
    drains.append((rf.at[pl.ds(0, 7)], f_send.at[1]))
    drains.append((cf.at[pl.ds(0, 12)], f_send.at[2]))
    drains.append((rf.at[pl.ds(0, 8)], f_send.at[3]))
    drains.append((lab_cols.at[pl.ds(0, 3)], l_send.at[0]))
    drains.append((lab_rows.at[pl.ds(0, 7)], l_send.at[1]))
    drains.append((lab_cols.at[pl.ds(0, 12)], l_send.at[2]))
    drains.append((lab_rows.at[pl.ds(0, 8)], l_send.at[3]))

    half = pl.ds(pl.multiple_of(core * HALF, HALF), HALF)
    sn_ref[...] = column_norms(rf[block].reshape(HALF, FEAT))
    tgt_copy.wait()

    def target_tile(i):
        rows = tgt[i]
        inner = dot(rf[block].reshape(HALF, FEAT), rows, NT)
        value = jnp.exp(inner - sn_ref[...] - row_norms(rows))
        hi = value.astype(BF16)
        kk_hi[i] = hi
        kk_lo[i] = (value - hi.astype(F32)).astype(BF16)

    done = [0]

    def fill(count):
        stop = min(TILES, done[0] + count)
        if stop > done[0]:

            @pl.loop(done[0] // 2, stop // 2)
            def _(i):
                target_tile(2 * i)
                target_tile(2 * i + 1)

        done[0] = stop

    fill(FILL[0])

    wait_for(rf.at[pl.ds(0, 8)], r_recv.at[1])
    rn_ref[...] = row_norms(rf[...].reshape(WIDE, FEAT))

    @pl.loop(0, 4)
    def _(i):
        px = lax.rem(x + gray(i), 4)

        @pl.when(i > 0)
        def _():
            wait_for(cf.at[pl.ds(0, 4)], x_recv.at[px])

        part = cf[pl.ds(px * 4, 4)].reshape(TILE, FEAT)
        inner = dot(part, rf[...].reshape(WIDE, FEAT), NT)
        value = jnp.exp(inner - column_norms(part) - rn_ref[...])
        hi = value.astype(BF16)
        where = pl.ds(pl.multiple_of(px * TILE, TILE), TILE)
        kt_hi[where, :] = hi
        kt_lo[where, :] = (value - hi.astype(F32)).astype(BF16)

    def apply_tile(v):
        hi, mid, low = split3(v)
        big = dot(jnp.concatenate([hi, mid, low], axis=0), kt_hi[...])
        small = dot(jnp.concatenate([hi, mid], axis=0), kt_lo[...])
        return (big[0:16] + small[0:16]) + ((big[16:32] + small[16:32]) + big[32:48])

    wait_for(lab_cols.at[pl.ds(0, 12)], l_recv.at[2])
    b_cols = unpack(lab_cols)
    wait_for(lab_rows.at[pl.ds(0, 8)], l_recv.at[3])
    b_rows = unpack(lab_rows)
    drow[...] = b_rows
    rrow[...] = b_rows
    xrow[...] = jnp.zeros_like(b_rows)
    dcol[...] = b_cols
    rcol[...] = b_cols
    rr = None

    def predict_tile(t, parts, count):
        m = 16 * count
        big = dot(parts[...], kk_hi[t])
        small = dot(parts[0:2 * m, :], kk_lo[t])
        return (big[0:m] + small[0:m]) + ((big[m:2 * m] + small[m:2 * m]) + big[2 * m:3 * m])

    def predict_theirs(parts, count, send, recv, which):
        @pl.loop(0, 4)
        def _(g):
            for k in range(4):
                j = 12 - 4 * g + k
                send[j] = predict_tile(tile_at(2 * j + 1), parts, count)
            quarter = pl.ds(12 - 4 * g, 4)
            remote(send.at[quarter], recv.at[quarter], sib_ss.at[which], sib_rs.at[which, 3 - g], (other, c)).start()

        drains.append((recv, sib_ss.at[which]))

    def predict_own(parts, count, recv, which, store):
        @pl.loop(0, 4)
        def _(g):
            wait_for(recv.at[pl.ds(0, 4)], sib_rs.at[which, 3 - g])
            for k in range(4):
                j = 12 - 4 * g + k
                store[j] = predict_tile(tile_at(2 * j), parts, count) + recv[j]

    def reduce_predictions(which, value):
        for j in range(GROUP - 1, 0, -1):
            pred_send[which, j] = value(j)
            remote(
                pred_send.at[which, j], pred_recv.at[which, chip], pred_ss.at[which], pred_rs.at[which], col_peer(j)
            ).start()
        pred_recv[which, chip] = value(0)
        drains.append((pred_recv.at[which, pl.ds(0, 15)], pred_ss.at[which]))

    lane = lax.broadcasted_iota(jnp.int32, (1, 128), 1)
    left_half = lax.broadcasted_iota(jnp.int32, (8, 128), 1) < CHUNK
    for step in range(3):
        first, last = step == 0, step == 2
        norm = lane_sum(rcol[...] * rcol[...])
        applied = apply_tile(rcol[...])
        small_ridge = RIDGE / GROUP
        if first:
            d = drow[...]
            guess = applied
            scalars = to_lanes(lane_sum(d * (applied + small_ridge * d)), CHUNK) + to_lanes(norm, CHUNK + 48)
        else:
            near = ratio(norm * float(GROUP), rr)
            old = drow[...]
            d = rrow[...] + near * old
            guess = applied + near * prev[...]
            by_d = guess + small_ridge * d
            by_old = prev[...] + small_ridge * old
            scalars = to_lanes(lane_sum(d * by_d), CHUNK) + to_lanes(lane_sum(d * by_old + old * by_d), CHUNK + 16)
            scalars = scalars + to_lanes(lane_sum(old * by_old), CHUNK + 32) + to_lanes(norm, CHUNK + 48)
        if last:
            t_send[0] = scalars
            t_rows[me] = scalars
        else:
            for j in range(GROUP // 2):
                a, b = pack_pair(applied[:, 128 * j:128 * (j + 1)])
                s1_send[step, 2 * j] = put_scalars(a, scalars)
                s1_send[step, 2 * j + 1] = put_scalars(b, scalars)
            s1_recv[step, me] = s1_send[step, me]

        def send1(j):
            p, to = row_peer(j)
            src = t_send.at[0] if last else s1_send.at[step, p]
            dst = t_rows.at[me] if last else s1_recv.at[step, me]
            remote(src, dst, v_send.at[step, 0], v_recv.at[step, 0], to).start()

        far_first(GROUP, send1)
        landed = t_rows.at[pl.ds(0, 15)] if last else s1_recv.at[step, pl.ds(0, 15)]
        drains.append((landed, v_send.at[step, 0]))
        if first:
            fill(FILL[1])
        elif not last:
            fill(TILES)
        else:
            hi, mid, low = split3(rrow[:, half])
            one[...] = jnp.concatenate([hi, mid, low], axis=0)
            predict_theirs(one, 1, sib_send2, sib_recv2, 1)
            reduce_predictions(0, lambda j: both[j, 0:16, :] + alpha * both[j, 16:32, :])
            predict_own(one, 1, sib_recv2, 1, own2)
        wait_for(landed, v_recv.at[step, 0])
        if last:
            scalar_rows = [t_rows[j] for j in range(GROUP)]
        else:
            scalar_rows = [s1_recv[step, j][7:8] for j in range(GROUP)]
        sums = tree(scalar_rows)
        if first:
            rr = from_lanes(sums, CHUNK + 48)
            share = sums
        else:
            held = (lane >= CHUNK + 48) & (lane < CHUNK + 63)
            under = jnp.where(held, to_lanes(rr, CHUNK + 48), 1.0)
            senders = jnp.concatenate(scalar_rows, axis=0)
            true = jnp.where(held, sums, 0.0) / under
            off = true - jnp.where(held, senders * float(GROUP), 0.0) / under
            off = pltpu.roll(off, 80, 1)
            share = senders + off * (pltpu.roll(senders, 112, 1) + off * pltpu.roll(senders, 96, 1))
            share = jnp.sum(share, axis=0, keepdims=True)
            new = from_lanes(sums, CHUNK + 48)
            beta = ratio(new, rr)
            rr = new
        if last:
            t_send[1] = share
            t_cols[here] = share
        else:
            own = tree([s1_recv[step, j] for j in range(GROUP)])
            if not first:
                own = own + jnp.where(left_half, beta[0:8], beta[8:16]) * s2_send[step - 1]
            own = put_scalars(own, share)
            s2_send[step] = own
            s2_cols[step, here] = own

        def send2(j):
            src = t_send.at[1] if last else s2_send.at[step]
            dst = t_cols.at[here] if last else s2_cols.at[step, here]
            remote(src, dst, v_send.at[step, 1], v_recv.at[step, 1], col_peer(j)).start()

        far_first(GROUP, send2)
        landed = t_cols.at[pl.ds(0, 15)] if last else s2_cols.at[step, pl.ds(0, 15)]
        drains.append((landed, v_send.at[step, 1]))
        if not last:
            s2_rows[step, me] = own

            def send_rows(j):
                remote(
                    s2_send.at[step], s2_rows.at[step, me], v_send.at[step, 2], v_recv.at[step, 2], row_peer(j)[1]
                ).start()

            far_first(GROUP, send_rows)
            drains.append((s2_rows.at[step, pl.ds(0, 15)], v_send.at[step, 2]))
        if last:
            reduce_predictions(1, lambda j: own2[j] + beta * both[j, 16:32, :])
        if first:
            prev[...] = applied
        else:
            drow[...] = rrow[...] + beta * drow[...]
            if not last:
                prev[...] = applied + beta * prev[...]
                dcol[...] = rcol[...] + beta * dcol[...]
        if first:
            fill(FILL[2])
        elif not last:
            hi, mid, low = split3(xrow[:, half])
            hi2, mid2, low2 = split3(drow[:, half])
            three[...] = jnp.concatenate([hi, hi2, mid, mid2, low, low2], axis=0)
            predict_theirs(three, 2, sib_send, sib_recv, 0)
            predict_own(three, 2, sib_recv, 0, both)
        wait_for(landed, v_recv.at[step, 1])
        if last:
            total = tree([t_cols[j] for j in range(GROUP)])
        else:
            total = tree([s2_cols[step, j][7:8] for j in range(GROUP)])
        alpha = ratio(rr, from_lanes(total, CHUNK))
        if not last:
            rcol[...] = rcol[...] - alpha * (unpack(s2_cols.at[step]) + RIDGE * dcol[...])
            xrow[...] = xrow[...] + alpha * drow[...]
            wait_for(s2_rows.at[step, pl.ds(0, 15)], v_recv.at[step, 2])
            rrow[...] = rrow[...] - alpha * (unpack(s2_rows.at[step]) + RIDGE * drow[...])

    xrow[...] = xrow[...] + alpha * drow[...]
    pair = xrow[:, pl.ds(pl.multiple_of((me // 2) * 128, 128), 128)]
    own_x = jnp.where(lax.rem(me, 2) == 0, pair, pltpu.roll(pair, CHUNK, 1))
    out_ref[CHUNK:CHUNK + 16, 0:128] = own_x
    out_ref[CHUNK:CHUNK + 16, 128:FEAT] = jnp.zeros((16, 128), F32)
    hi, mid, low = split3(xrow[:, half])
    wide = jnp.concatenate([hi.astype(F32), mid.astype(F32), jnp.zeros((96, HALF), F32)], axis=0)
    xt[...] = wide.T[:, 0:32].astype(BF16)
    gsum[...] = jnp.zeros_like(gsum)
    csum[...] = jnp.zeros_like(csum)
    tlab_copy.wait()
    labels = jnp.concatenate([tlab[...], jnp.zeros((1, TILE), F32)], axis=0)

    for which in range(2):
        wait_for(pred_recv.at[which, pl.ds(0, 15)], pred_rs.at[which])
    predictions = tree([pred_recv[0, j] for j in range(GROUP)]) + alpha * tree([pred_recv[1, j] for j in range(GROUP)])
    own_err = (predictions - labels).astype(BF16)
    err_own[...] = own_err
    err[r] = own_err

    for j in range(1, GROUP):
        remote(err_own, err.at[r], err_ss, err_rs.at[r], col_peer(j)).start()
    drains.append((err.at[pl.ds(0, 15)], err_ss))

    def add_tiles(tiles):
        part, sums = None, None
        for t in tiles:
            e = err[t]
            mix = dot(xt[...], jnp.concatenate([e, e], axis=0))
            weights = mix.astype(BF16) * kk_hi[t]
            product = dot(weights, tgt[t])
            back = weights.astype(F32)
            back = back[:, 0:128] + back[:, 128:256]
            part = product if part is None else part + product
            sums = back if sums is None else sums + back
        gsum[...] += part
        csum[...] += sums

    def take_own(j):
        t = tile_at(2 * j)

        @pl.when(j > 0)
        def _():
            wait_for(err.at[0], err_rs.at[t])

        remote(err.at[t], err.at[t], pass_ss, err_rs.at[t], (other, c)).start()
        return t

    def take_theirs(j):
        t = tile_at(2 * j + 1)
        wait_for(err.at[0], err_rs.at[t])
        return t

    zero = jnp.int32(0)
    add_tiles([take_own(zero), take_own(zero + 1)])

    @pl.loop(1, 8)
    def _(s):
        mine = [take_own(2 * s), take_own(2 * s + 1)]
        add_tiles([take_theirs(2 * s - 2), take_theirs(2 * s - 1)] + mine)

    add_tiles([take_theirs(zero + 14), take_theirs(zero + 15)])
    drains.append((err.at[pl.ds(0, 16)], pass_ss))

    scale = 1.0 / 256.0
    term = (gsum[...] - lane_sum(csum[...]) * rf[block].reshape(HALF, FEAT).astype(F32)) * scale
    g_send[...] = term.reshape(8, CHUNK, FEAT)
    g_recv[c] = g_send[c]

    for j in range(7, 0, -1):
        remote(g_send.at[col_peers[j][1]], g_recv.at[c], g_ss, g_rs, col_peers[j]).start()

    drains.append((g_recv.at[pl.ds(0, 7)], g_ss))
    wait_for(g_recv.at[pl.ds(0, 7)], g_rs)
    out_ref[0:CHUNK, :] = tree([g_recv[j] for j in range(8)])

    for ref, sem in drains:
        wait_for(ref, sem)


def part_outputs(joint_ref, coef_ref, grad_ref):
    coef_ref[...] = joint_ref[CHUNK:CHUNK + 15, 0:CHUNK]
    grad_ref[...] = joint_ref[0:CHUNK, :]


def body(support, support_labels, targets, target_labels):
    classes = support_labels.shape[0]
    vmem = pl.BlockSpec(memory_space=pltpu.VMEM)
    anywhere = pl.BlockSpec(memory_space=pl.ANY)
    dma = pltpu.SemaphoreType.DMA
    joint = pl.pallas_call(
        kernel,
        out_shape=jax.ShapeDtypeStruct((CHUNK + 16, FEAT), F32),
        in_specs=[vmem, vmem, anywhere, anywhere],
        out_specs=vmem,
        scratch_shapes=[
            pltpu.VMEM((TILES, TILE, FEAT), BF16),
            pltpu.VMEM((classes, TILE), F32),
            pltpu.VMEM((CHUNK, FEAT), BF16),
            pltpu.VMEM((8, 128), F32),
            pltpu.VMEM((GROUP, CHUNK, FEAT), BF16),
            pltpu.VMEM((GROUP, CHUNK, FEAT), BF16),
            pltpu.VMEM((GROUP, 8, 128), F32),
            pltpu.VMEM((GROUP, 8, 128), F32),
            pltpu.VMEM((1, WIDE), F32),
            pltpu.VMEM((HALF, 1), F32),
            pltpu.VMEM((WIDE, WIDE), BF16),
            pltpu.VMEM((WIDE, WIDE), BF16),
            pltpu.VMEM((TILES, HALF, TILE), BF16),
            pltpu.VMEM((TILES, HALF, TILE), BF16),
            pltpu.VMEM((2, GROUP, 8, 128), F32),
            pltpu.VMEM((2, GROUP, 8, 128), F32),
            pltpu.VMEM((2, 8, 128), F32),
            pltpu.VMEM((2, GROUP, 8, 128), F32),
            pltpu.VMEM((2, GROUP, 8, 128), F32),
            pltpu.VMEM((2, 1, 128), F32),
            pltpu.VMEM((GROUP, 1, 128), F32),
            pltpu.VMEM((GROUP, 1, 128), F32),
            pltpu.VMEM((GROUP, WIDE), F32),
            pltpu.VMEM((GROUP, WIDE), F32),
            pltpu.VMEM((GROUP, WIDE), F32),
            pltpu.VMEM((GROUP, WIDE), F32),
            pltpu.VMEM((GROUP, WIDE), F32),
            pltpu.VMEM((GROUP, WIDE), F32),
            pltpu.VMEM((96, HALF), BF16),
            pltpu.VMEM((48, HALF), BF16),
            pltpu.VMEM((GROUP, 32, TILE), F32),
            pltpu.VMEM((GROUP, 16, TILE), F32),
            pltpu.VMEM((GROUP, 32, TILE), F32),
            pltpu.VMEM((GROUP, 32, TILE), F32),
            pltpu.VMEM((GROUP, 16, TILE), F32),
            pltpu.VMEM((GROUP, 16, TILE), F32),
            pltpu.VMEM((2, GROUP, 16, TILE), F32),
            pltpu.VMEM((2, GROUP, 16, TILE), F32),
            pltpu.VMEM((16, TILE), BF16),
            pltpu.VMEM((TILES, 16, TILE), BF16),
            pltpu.VMEM((HALF, 32), BF16),
            pltpu.VMEM((HALF, FEAT), F32),
            pltpu.VMEM((HALF, 128), F32),
            pltpu.VMEM((8, CHUNK, FEAT), F32),
            pltpu.VMEM((8, CHUNK, FEAT), F32),
            dma((2,)),
            dma((4,)),
            dma((4,)),
            dma((4,)),
            dma((2,)),
            dma((4,)),
            dma((4,)),
            dma((3, 3)),
            dma((3, 3)),
            dma((2,)),
            dma((2, 4)),
            dma((2,)),
            dma((2,)),
            dma,
            dma((TILES,)),
            dma,
            dma,
            dma,
        ],
        compiler_params=pltpu.CompilerParams(
            collective_id=0, has_side_effects=True, vmem_limit_bytes=58 * 1024 * 1024
        ),
    )(support, support_labels, targets.reshape(TILES, TILE, FEAT), target_labels)
    return pl.pallas_call(
        part_outputs,
        out_shape=(
            jax.ShapeDtypeStruct((classes, CHUNK), F32),
            jax.ShapeDtypeStruct((CHUNK, FEAT), F32),
        ),
        in_specs=[vmem],
        out_specs=(vmem, vmem),
    )(joint)


def solution(mesh):
    in_specs = (P(("row", "col"), None), P(None, ("row", "col")), P("col", None), P(None, "col"))
    out_specs = (P(None, ("row", "col")), P(("row", "col"), None))
    return jax.shard_map(body, mesh=mesh, in_specs=in_specs, out_specs=out_specs, check_vma=False)
```

```python
import jax
import jax.numpy as jnp
from jax import lax
from jax.experimental import pallas as pl
from jax.experimental.pallas import tpu as pltpu
from jax.sharding import PartitionSpec as P

MESH = pl.DeviceIdType.MESH
F32 = jnp.float32
BF16 = jnp.bfloat16

CHUNK = 64
FEAT = 256
TILE = 256
TILES = 32
GROUP = 16
WIDE = GROUP * CHUNK
HALF = WIDE // 2
RIDGE = 0.5
FILL = (8, 4, 8)
NN = (((1,), (0,)), ((), ()))
NT = (((1,), (1,)), ((), ()))


def dot(a, b, dims=NN):
    return lax.dot_general(a, b, dims, preferred_element_type=F32)


def split3(v):
    hi = v.astype(BF16)
    rest = v - hi.astype(F32)
    mid = rest.astype(BF16)
    low = (rest - mid.astype(F32)).astype(BF16)
    return hi, mid, low


def row_norms(rows):
    square = jnp.square(rows.astype(F32))
    hi = square.astype(BF16)
    low = (square - hi.astype(F32)).astype(BF16)
    ones = jnp.ones((8, FEAT), BF16)
    return 0.5 * (dot(ones, hi, NT) + dot(ones, low, NT))[0:1, :]


def column_norms(rows):
    return 0.5 * jnp.sum(jnp.square(rows.astype(F32)), axis=1, keepdims=True)


def pack_pair(v):
    left = lax.broadcasted_iota(jnp.int32, (8, 128), 1) < CHUNK
    top, bottom = v[0:8], v[8:16]
    first = jnp.where(left, top, pltpu.roll(bottom, CHUNK, 1))
    second = jnp.where(left, pltpu.roll(top, CHUNK, 1), bottom)
    return first, second


def unpack_pair(a, b):
    left = lax.broadcasted_iota(jnp.int32, (8, 128), 1) < CHUNK
    top = jnp.where(left, a, pltpu.roll(b, CHUNK, 1))
    bottom = jnp.where(left, pltpu.roll(a, CHUNK, 1), b)
    return jnp.concatenate([top, bottom], axis=0)


def unpack(ref):
    wide = jnp.concatenate([unpack_pair(ref[2 * j], ref[2 * j + 1]) for j in range(GROUP // 2)], axis=1)
    return jnp.where(lax.broadcasted_iota(jnp.int32, wide.shape, 0) < 15, wide, 0.0)


def gray(j):
    return j + (j // 2) * (5 - 2 * j)


def to_lanes(q, shift):
    sub = lax.broadcasted_iota(jnp.int32, (16, 128), 0)
    lane = lax.broadcasted_iota(jnp.int32, (16, 128), 1)
    return jnp.sum(jnp.where(lane == sub + shift, q, 0.0), axis=0, keepdims=True)


def from_lanes(row, shift):
    sub = lax.broadcasted_iota(jnp.int32, (16, 128), 0)
    lane = lax.broadcasted_iota(jnp.int32, (16, 128), 1)
    return jnp.sum(jnp.where(lane == sub + shift, row, 0.0), axis=1, keepdims=True)


def put_scalars(message, row):
    sub = lax.broadcasted_iota(jnp.int32, (8, 128), 0)
    lane = lax.broadcasted_iota(jnp.int32, (8, 128), 1)
    return jnp.where((sub == 7) & (lane >= CHUNK), row, message)


def lane_sum(v):
    return jnp.sum(v, axis=1, keepdims=True)


def ratio(a, b):
    real = lax.broadcasted_iota(jnp.int32, (16, 1), 0) < 15
    return jnp.where(real, a, 0.0) / jnp.where(real, b, 1.0)


def tree(values):
    values = list(values)
    while len(values) > 1:
        values = [values[i] + values[i + 1] if i + 1 < len(values) else values[i] for i in range(0, len(values), 2)]
    return values[0]


def kernel(
    sup_ref, lab_ref, tgt_hbm, tlab_hbm,
    out_ref,
    tgt, tlab, sup_v, lab_v, rf, cf, lab_rows, lab_cols, rn_ref, sn_ref, tn_ref,
    kt_hi, kt_lo, kk_hi, kk_lo,
    s1_send, s1_recv, s2_send, s2_rows, s2_cols, t_send, t_rows, t_cols,
    drow, rrow, xrow, dcol, rcol, prev,
    three, one, both, own2, sib_send, sib_recv, sib_send2, sib_recv2, u_send, u_recv, w_send, w_recv, pred_send, pred_recv, err_own, err, xt, gsum, csum, g_send, g_recv,
    local_sems, f_send, z_recv, x_recv, r_recv, l_send, l_recv, v_send, v_recv,
    sib_ss, sib_rs, pred_ss, pred_rs, err_ss, err_rs, pass_ss, g_ss, g_rs,
):
    r = lax.axis_index("row")
    c = lax.axis_index("col")
    chip, core = r // 2, lax.rem(r, 2)
    z, x = chip // 4, lax.rem(chip, 4)
    zl, y = c // 4, lax.rem(c, 4)
    me = core * 8 + c
    here = x * 4 + z

    def device(pz, px):
        return (2 * (pz * 4 + px) + core, c)

    xs = [lax.rem(x + d, 4) for d in range(4)]
    zs = [lax.rem(z + d, 4) for d in range(4)]
    ys = [lax.rem(y + d, 4) for d in range(4)]
    ls = [zl, 1 - zl]
    ks = [core, 1 - core]

    def row_peer(j):
        k, p = ks[j % 2], ls[j // 8] * 4 + ys[gray((j // 2) % 4)]
        return k * 8 + p, (2 * chip + k, p)

    def col_peer(j):
        return (2 * (zs[gray(j // 4)] * 4 + xs[gray(j % 4)]) + core, c)

    def tile_at(j):
        j = jnp.int32(j)
        chip_there = lax.rem(z + gray(j // 8), 4) * 4 + lax.rem(x + gray((j // 2) % 4), 4)
        return 2 * chip_there + lax.rem(core + j % 2, 2)

    def far_first(count, act):
        for j in range(count - 1, 0, -1):
            act(j)

    tgt_copy = pltpu.make_async_copy(tgt_hbm, tgt, local_sems.at[0])
    tgt_copy.start()
    start_lane = pl.multiple_of(r * TILE, TILE)
    tlab_copy = pltpu.make_async_copy(tlab_hbm.at[:, pl.ds(start_lane, TILE)], tlab, local_sems.at[1])
    tlab_copy.start()

    barrier = pltpu.get_barrier_semaphore()
    far_first(4, lambda j: pl.semaphore_signal(barrier, inc=1, device_id=device(zs[j], x), device_id_type=MESH))
    far_first(4, lambda j: pl.semaphore_signal(barrier, inc=1, device_id=device(z, xs[j]), device_id_type=MESH))
    far_first(
        GROUP, lambda j: pl.semaphore_signal(barrier, inc=1, device_id=row_peer(j)[1], device_id_type=MESH)
    )

    lab = jnp.concatenate([lab_ref[...], jnp.zeros((1, CHUNK), F32)], axis=0)
    lab_v[...] = jnp.concatenate([lab[0:8], lab[8:16]], axis=1)
    sup = sup_ref[...]
    sup_v[...] = sup
    rf[me] = sup
    cf[here] = sup
    lab_rows[me] = lab_v[...]
    lab_cols[here] = lab_v[...]

    pl.semaphore_wait(barrier, 21)

    drains = []

    def remote(src, dst, ss, rs, to):
        return pltpu.make_async_remote_copy(
            src_ref=src, dst_ref=dst, send_sem=ss, recv_sem=rs, device_id=to, device_id_type=MESH
        )

    def wait_for(ref, sem):
        pltpu.make_async_copy(ref, ref, sem).wait()

    def to_x(dz):
        slot = xs[0] * 4 + zs[dz]
        for d in (2, 1, 3):
            remote(cf.at[slot], cf.at[slot], f_send.at[2], x_recv.at[x], device(z, xs[d])).start()

    col_peers = [(r, ls[j // 4] * 4 + ys[gray(j % 4)]) for j in range(8)]
    for d in (2, 3, 1):
        remote(sup_v, cf.at[here], f_send.at[0], z_recv.at[z], device(zs[d], x)).start()
    to_x(0)
    for j in range(7, 0, -1):
        remote(sup_v, rf.at[me], f_send.at[1], r_recv.at[0], col_peers[j]).start()
    for d in (2, 3, 1):
        remote(lab_v, lab_cols.at[here], l_send.at[0], l_recv.at[0], device(zs[d], x)).start()
    for j in range(7, 0, -1):
        remote(lab_v, lab_rows.at[me], l_send.at[1], l_recv.at[1], col_peers[j]).start()

    tgt_copy.wait()

    @pl.loop(0, TILES // 2)
    def _(i):
        tn_ref[2 * i] = row_norms(tgt[2 * i])
        tn_ref[2 * i + 1] = row_norms(tgt[2 * i + 1])

    for d in (1, 3):
        wait_for(cf.at[0], z_recv.at[zs[d]])
        to_x(d)
    wait_for(cf.at[0], z_recv.at[zs[2]])
    to_x(2)

    block = pl.ds(core * 8, 8)
    other = 2 * chip + 1 - core
    wait_for(rf.at[pl.ds(0, 7)], r_recv.at[0])
    remote(rf.at[block], rf.at[block], f_send.at[3], r_recv.at[1], (other, c)).start()
    wait_for(lab_cols.at[pl.ds(0, 3)], l_recv.at[0])
    for d in (2, 3, 1):
        four = lab_cols.at[pl.ds(x * 4, 4)]
        remote(four, four, l_send.at[2], l_recv.at[2], device(z, xs[d])).start()
    wait_for(lab_rows.at[pl.ds(0, 7)], l_recv.at[1])
    remote(lab_rows.at[block], lab_rows.at[block], l_send.at[3], l_recv.at[3], (other, c)).start()

    drains.append((cf.at[pl.ds(0, 3)], f_send.at[0]))
    drains.append((rf.at[pl.ds(0, 7)], f_send.at[1]))
    drains.append((cf.at[pl.ds(0, 12)], f_send.at[2]))
    drains.append((rf.at[pl.ds(0, 8)], f_send.at[3]))
    drains.append((lab_cols.at[pl.ds(0, 3)], l_send.at[0]))
    drains.append((lab_rows.at[pl.ds(0, 7)], l_send.at[1]))
    drains.append((lab_cols.at[pl.ds(0, 12)], l_send.at[2]))
    drains.append((lab_rows.at[pl.ds(0, 8)], l_send.at[3]))

    half = pl.ds(pl.multiple_of(core * HALF, HALF), HALF)
    sn_ref[...] = column_norms(rf[block].reshape(HALF, FEAT))

    def target_tile(i):
        rows = tgt[i]
        inner = dot(rf[block].reshape(HALF, FEAT), rows, NT)
        value = jnp.exp(inner - sn_ref[...] - tn_ref[i])
        hi = value.astype(BF16)
        kk_hi[i] = hi
        kk_lo[i] = (value - hi.astype(F32)).astype(BF16)

    done = [0]

    def fill(count):
        stop = min(TILES, done[0] + count)
        if stop > done[0]:

            @pl.loop(done[0] // 2, stop // 2)
            def _(i):
                target_tile(2 * i)
                target_tile(2 * i + 1)

        done[0] = stop

    fill(FILL[0])

    wait_for(rf.at[pl.ds(0, 8)], r_recv.at[1])
    rn_ref[...] = row_norms(rf[...].reshape(WIDE, FEAT))

    def system_block(d):
        px = xs[d]
        if d:
            wait_for(cf.at[pl.ds(0, 4)], x_recv.at[px])
        part = cf[pl.ds(px * 4, 4)].reshape(TILE, FEAT)
        inner = dot(part, rf[...].reshape(WIDE, FEAT), NT)
        value = jnp.exp(inner - column_norms(part) - rn_ref[...])
        hi = value.astype(BF16)
        where = pl.ds(pl.multiple_of(px * TILE, TILE), TILE)
        kt_hi[where, :] = hi
        kt_lo[where, :] = (value - hi.astype(F32)).astype(BF16)

    system_block(0)
    fill(FILL[1])
    for d in (1, 3, 2):
        system_block(d)

    def apply_tile(v):
        hi, mid, low = split3(v)
        big = dot(jnp.concatenate([hi, mid, low], axis=0), kt_hi[...])
        small = dot(jnp.concatenate([hi, mid], axis=0), kt_lo[...])
        return (big[0:16] + small[0:16]) + ((big[16:32] + small[16:32]) + big[32:48])

    wait_for(lab_cols.at[pl.ds(0, 12)], l_recv.at[2])
    b_cols = unpack(lab_cols)
    wait_for(lab_rows.at[pl.ds(0, 8)], l_recv.at[3])
    b_rows = unpack(lab_rows)
    drow[...] = b_rows
    rrow[...] = b_rows
    xrow[...] = jnp.zeros_like(b_rows)
    dcol[...] = b_cols
    rcol[...] = b_cols
    rr = None

    def predict_tile(t, parts, count):
        m = 16 * count
        big = dot(parts[...], kk_hi[t])
        small = dot(parts[0:2 * m, :], kk_lo[t])
        return (big[0:m] + small[0:m]) + ((big[m:2 * m] + small[m:2 * m]) + big[2 * m:3 * m])

    def predict_theirs(parts, count, send, recv, which):
        @pl.loop(0, 4)
        def _(g):
            for k in range(4):
                j = 12 - 4 * g + k
                send[j] = predict_tile(tile_at(2 * j + 1), parts, count)
            quarter = pl.ds(12 - 4 * g, 4)
            remote(send.at[quarter], recv.at[quarter], sib_ss.at[which], sib_rs.at[which, 3 - g], (other, c)).start()

        drains.append((recv, sib_ss.at[which]))

    def predict_own(parts, count, recv, which, store):
        @pl.loop(0, 4)
        def _(g):
            wait_for(recv.at[pl.ds(0, 4)], sib_rs.at[which, 3 - g])
            for k in range(4):
                j = 12 - 4 * g + k
                store[j] = predict_tile(tile_at(2 * j), parts, count) + recv[j]

    def reduce_first(value):
        for k in range(3, -1, -1):
            for q in range(4):
                u_send[k, q] = value(4 * q + k)
            if k > 0:
                remote(u_send.at[k], u_recv.at[x], pred_ss.at[0], pred_rs.at[0], device(z, xs[gray(k)])).start()
            else:
                u_recv[x] = u_send[0]
        drains.append((u_recv.at[pl.ds(0, 3)], pred_ss.at[0]))

    def pass_first():
        wait_for(u_recv.at[pl.ds(0, 3)], pred_rs.at[0])
        for q in range(3, -1, -1):
            value = (u_recv[0, q] + u_recv[1, q]) + (u_recv[2, q] + u_recv[3, q])
            if q > 0:
                w_send[q] = value
                remote(w_send.at[q], w_recv.at[z], pred_ss.at[1], pred_rs.at[1], device(zs[gray(q)], x)).start()
            else:
                w_recv[z] = value
        drains.append((w_recv.at[pl.ds(0, 3)], pred_ss.at[1]))

    def reduce_second(value):
        for j in range(GROUP - 1, 0, -1):
            pred_send[j] = value(j)
            remote(pred_send.at[j], pred_recv.at[chip], pred_ss.at[2], pred_rs.at[2], col_peer(j)).start()
        pred_recv[chip] = value(0)
        drains.append((pred_recv.at[pl.ds(0, 15)], pred_ss.at[2]))

    lane = lax.broadcasted_iota(jnp.int32, (1, 128), 1)
    left_half = lax.broadcasted_iota(jnp.int32, (8, 128), 1) < CHUNK
    for step in range(3):
        first, last = step == 0, step == 2
        norm = lane_sum(rcol[...] * rcol[...])
        applied = apply_tile(rcol[...])
        small_ridge = RIDGE / GROUP
        if first:
            d = drow[...]
            guess = applied
            scalars = to_lanes(lane_sum(d * (applied + small_ridge * d)), CHUNK) + to_lanes(norm, CHUNK + 48)
        else:
            near = ratio(norm * float(GROUP), rr)
            old = drow[...]
            d = rrow[...] + near * old
            guess = applied + near * prev[...]
            by_d = guess + small_ridge * d
            by_old = prev[...] + small_ridge * old
            scalars = to_lanes(lane_sum(d * by_d), CHUNK) + to_lanes(lane_sum(d * by_old + old * by_d), CHUNK + 16)
            scalars = scalars + to_lanes(lane_sum(old * by_old), CHUNK + 32) + to_lanes(norm, CHUNK + 48)
        if last:
            t_send[0] = scalars
            t_rows[me] = scalars
        else:
            for j in range(GROUP // 2):
                a, b = pack_pair(applied[:, 128 * j:128 * (j + 1)])
                s1_send[step, 2 * j] = put_scalars(a, scalars)
                s1_send[step, 2 * j + 1] = put_scalars(b, scalars)
            s1_recv[step, me] = s1_send[step, me]

        def send1(j):
            p, to = row_peer(j)
            src = t_send.at[0] if last else s1_send.at[step, p]
            dst = t_rows.at[me] if last else s1_recv.at[step, me]
            remote(src, dst, v_send.at[step, 0], v_recv.at[step, 0], to).start()

        far_first(GROUP, send1)
        landed = t_rows.at[pl.ds(0, 15)] if last else s1_recv.at[step, pl.ds(0, 15)]
        drains.append((landed, v_send.at[step, 0]))
        if first:
            fill(FILL[2])
        elif not last:
            hi, mid, low = split3(drow[:, half])
            hi2, mid2, low2 = split3(rrow[:, half])
            three[...] = jnp.concatenate([hi, hi2, mid, mid2, low, low2], axis=0)
            predict_theirs(three, 2, sib_send, sib_recv, 0)
        else:
            reduce_first(lambda j: (alpha0 + alpha * beta0) * both[j, 0:16, :] + alpha * both[j, 16:32, :])
            hi, mid, low = split3(rrow[:, half])
            one[...] = jnp.concatenate([hi, mid, low], axis=0)
            predict_theirs(one, 1, sib_send2, sib_recv2, 1)
            predict_own(one, 1, sib_recv2, 1, own2)
        wait_for(landed, v_recv.at[step, 0])
        if last:
            scalar_rows = [t_rows[j] for j in range(GROUP)]
        else:
            scalar_rows = [s1_recv[step, j][7:8] for j in range(GROUP)]
        sums = tree(scalar_rows)
        if first:
            rr = from_lanes(sums, CHUNK + 48)
            share = sums
        else:
            held = (lane >= CHUNK + 48) & (lane < CHUNK + 63)
            under = jnp.where(held, to_lanes(rr, CHUNK + 48), 1.0)
            senders = jnp.concatenate(scalar_rows, axis=0)
            true = jnp.where(held, sums, 0.0) / under
            off = true - jnp.where(held, senders * float(GROUP), 0.0) / under
            off = pltpu.roll(off, 80, 1)
            share = senders + off * (pltpu.roll(senders, 112, 1) + off * pltpu.roll(senders, 96, 1))
            share = jnp.sum(share, axis=0, keepdims=True)
            new = from_lanes(sums, CHUNK + 48)
            beta = ratio(new, rr)
            rr = new
        if last:
            t_send[1] = share
            t_cols[here] = share
        else:
            own = tree([s1_recv[step, j] for j in range(GROUP)])
            if not first:
                own = own + jnp.where(left_half, beta[0:8], beta[8:16]) * s2_send[step - 1]
            own = put_scalars(own, share)
            s2_send[step] = own
            s2_cols[step, here] = own

        def send2(j):
            src = t_send.at[1] if last else s2_send.at[step]
            dst = t_cols.at[here] if last else s2_cols.at[step, here]
            remote(src, dst, v_send.at[step, 1], v_recv.at[step, 1], col_peer(j)).start()

        far_first(GROUP, send2)
        landed = t_cols.at[pl.ds(0, 15)] if last else s2_cols.at[step, pl.ds(0, 15)]
        drains.append((landed, v_send.at[step, 1]))
        if not last:
            s2_rows[step, me] = own

            def send_rows(j):
                remote(
                    s2_send.at[step], s2_rows.at[step, me], v_send.at[step, 2], v_recv.at[step, 2], row_peer(j)[1]
                ).start()

            far_first(GROUP, send_rows)
            drains.append((s2_rows.at[step, pl.ds(0, 15)], v_send.at[step, 2]))
        if last:
            reduce_second(lambda j: own2[j] + beta * (both[j, 16:32, :] + beta0 * both[j, 0:16, :]))
            pass_first()
        if first:
            prev[...] = applied
        else:
            drow[...] = rrow[...] + beta * drow[...]
            if not last:
                prev[...] = applied + beta * prev[...]
                dcol[...] = rcol[...] + beta * dcol[...]
        if first:
            fill(TILES)
        elif not last:
            predict_own(three, 2, sib_recv, 0, both)
        wait_for(landed, v_recv.at[step, 1])
        if last:
            total = tree([t_cols[j] for j in range(GROUP)])
        else:
            total = tree([s2_cols[step, j][7:8] for j in range(GROUP)])
        alpha = ratio(rr, from_lanes(total, CHUNK))
        if first:
            alpha0 = alpha
        elif not last:
            beta0 = beta
        if not last:
            rcol[...] = rcol[...] - alpha * (unpack(s2_cols.at[step]) + RIDGE * dcol[...])
            xrow[...] = xrow[...] + alpha * drow[...]
            wait_for(s2_rows.at[step, pl.ds(0, 15)], v_recv.at[step, 2])
            rrow[...] = rrow[...] - alpha * (unpack(s2_rows.at[step]) + RIDGE * drow[...])

    xrow[...] = xrow[...] + alpha * drow[...]
    pair = xrow[:, pl.ds(pl.multiple_of((me // 2) * 128, 128), 128)]
    own_x = jnp.where(lax.rem(me, 2) == 0, pair, pltpu.roll(pair, CHUNK, 1))
    out_ref[CHUNK:CHUNK + 16, 0:128] = own_x
    out_ref[CHUNK:CHUNK + 16, 128:FEAT] = jnp.zeros((16, 128), F32)
    hi, mid, low = split3(xrow[:, half])
    wide = jnp.concatenate([hi.astype(F32), mid.astype(F32), jnp.zeros((96, HALF), F32)], axis=0)
    xt[...] = wide.T[:, 0:32].astype(BF16)
    gsum[...] = jnp.zeros_like(gsum)
    csum[...] = jnp.zeros_like(csum)
    tlab_copy.wait()
    labels = jnp.concatenate([tlab[...], jnp.zeros((1, TILE), F32)], axis=0)

    wait_for(w_recv.at[pl.ds(0, 3)], pred_rs.at[1])
    wait_for(pred_recv.at[pl.ds(0, 15)], pred_rs.at[2])
    predictions = tree([w_recv[j] for j in range(4)]) + alpha * tree([pred_recv[j] for j in range(GROUP)])
    own_err = (predictions - labels).astype(BF16)
    err_own[...] = own_err
    err[r] = own_err

    for j in range(1, GROUP):
        remote(err_own, err.at[r], err_ss, err_rs.at[r], col_peer(j)).start()
    drains.append((err.at[pl.ds(0, 15)], err_ss))

    def add_tiles(tiles):
        part, sums = None, None
        for t in tiles:
            e = err[t]
            mix = dot(xt[...], jnp.concatenate([e, e], axis=0))
            weights = mix.astype(BF16) * kk_hi[t]
            product = dot(weights, tgt[t])
            back = weights.astype(F32)
            back = back[:, 0:128] + back[:, 128:256]
            part = product if part is None else part + product
            sums = back if sums is None else sums + back
        gsum[...] += part
        csum[...] += sums

    def take_own(j):
        t = tile_at(2 * j)

        @pl.when(j > 0)
        def _():
            wait_for(err.at[0], err_rs.at[t])

        remote(err.at[t], err.at[t], pass_ss, err_rs.at[t], (other, c)).start()
        return t

    def take_theirs(j):
        t = tile_at(2 * j + 1)
        wait_for(err.at[0], err_rs.at[t])
        return t

    zero = jnp.int32(0)
    add_tiles([take_own(zero), take_own(zero + 1), take_own(zero + 2), take_own(zero + 3)])

    @pl.loop(1, 4)
    def _(s):
        mine = [take_own(4 * s + k) for k in range(4)]
        add_tiles([take_theirs(4 * s - 4 + k) for k in range(4)] + mine)

    add_tiles([take_theirs(zero + 12 + k) for k in range(4)])
    drains.append((err.at[pl.ds(0, 16)], pass_ss))

    scale = 1.0 / 256.0
    term = (gsum[...] - lane_sum(csum[...]) * rf[block].reshape(HALF, FEAT).astype(F32)) * scale
    g_send[...] = term.reshape(8, CHUNK, FEAT)
    g_recv[c] = g_send[c]

    for j in range(7, 0, -1):
        remote(g_send.at[col_peers[j][1]], g_recv.at[c], g_ss, g_rs, col_peers[j]).start()

    drains.append((g_recv.at[pl.ds(0, 7)], g_ss))
    wait_for(g_recv.at[pl.ds(0, 7)], g_rs)
    out_ref[0:CHUNK, :] = tree([g_recv[j] for j in range(8)])

    for ref, sem in drains:
        wait_for(ref, sem)


def part_outputs(joint_ref, coef_ref, grad_ref):
    coef_ref[...] = joint_ref[CHUNK:CHUNK + 15, 0:CHUNK]
    grad_ref[...] = joint_ref[0:CHUNK, :]


def body(support, support_labels, targets, target_labels):
    classes = support_labels.shape[0]
    vmem = pl.BlockSpec(memory_space=pltpu.VMEM)
    anywhere = pl.BlockSpec(memory_space=pl.ANY)
    dma = pltpu.SemaphoreType.DMA
    joint = pl.pallas_call(
        kernel,
        out_shape=jax.ShapeDtypeStruct((CHUNK + 16, FEAT), F32),
        in_specs=[vmem, vmem, anywhere, anywhere],
        out_specs=vmem,
        scratch_shapes=[
            pltpu.VMEM((TILES, TILE, FEAT), BF16),
            pltpu.VMEM((classes, TILE), F32),
            pltpu.VMEM((CHUNK, FEAT), BF16),
            pltpu.VMEM((8, 128), F32),
            pltpu.VMEM((GROUP, CHUNK, FEAT), BF16),
            pltpu.VMEM((GROUP, CHUNK, FEAT), BF16),
            pltpu.VMEM((GROUP, 8, 128), F32),
            pltpu.VMEM((GROUP, 8, 128), F32),
            pltpu.VMEM((1, WIDE), F32),
            pltpu.VMEM((HALF, 1), F32),
            pltpu.VMEM((TILES, 1, TILE), F32),
            pltpu.VMEM((WIDE, WIDE), BF16),
            pltpu.VMEM((WIDE, WIDE), BF16),
            pltpu.VMEM((TILES, HALF, TILE), BF16),
            pltpu.VMEM((TILES, HALF, TILE), BF16),
            pltpu.VMEM((2, GROUP, 8, 128), F32),
            pltpu.VMEM((2, GROUP, 8, 128), F32),
            pltpu.VMEM((2, 8, 128), F32),
            pltpu.VMEM((2, GROUP, 8, 128), F32),
            pltpu.VMEM((2, GROUP, 8, 128), F32),
            pltpu.VMEM((2, 1, 128), F32),
            pltpu.VMEM((GROUP, 1, 128), F32),
            pltpu.VMEM((GROUP, 1, 128), F32),
            pltpu.VMEM((GROUP, WIDE), F32),
            pltpu.VMEM((GROUP, WIDE), F32),
            pltpu.VMEM((GROUP, WIDE), F32),
            pltpu.VMEM((GROUP, WIDE), F32),
            pltpu.VMEM((GROUP, WIDE), F32),
            pltpu.VMEM((GROUP, WIDE), F32),
            pltpu.VMEM((96, HALF), BF16),
            pltpu.VMEM((48, HALF), BF16),
            pltpu.VMEM((GROUP, 32, TILE), F32),
            pltpu.VMEM((GROUP, 16, TILE), F32),
            pltpu.VMEM((GROUP, 32, TILE), F32),
            pltpu.VMEM((GROUP, 32, TILE), F32),
            pltpu.VMEM((GROUP, 16, TILE), F32),
            pltpu.VMEM((GROUP, 16, TILE), F32),
            pltpu.VMEM((4, 4, 16, TILE), F32),
            pltpu.VMEM((4, 4, 16, TILE), F32),
            pltpu.VMEM((4, 16, TILE), F32),
            pltpu.VMEM((4, 16, TILE), F32),
            pltpu.VMEM((GROUP, 16, TILE), F32),
            pltpu.VMEM((GROUP, 16, TILE), F32),
            pltpu.VMEM((16, TILE), BF16),
            pltpu.VMEM((TILES, 16, TILE), BF16),
            pltpu.VMEM((HALF, 32), BF16),
            pltpu.VMEM((HALF, FEAT), F32),
            pltpu.VMEM((HALF, 128), F32),
            pltpu.VMEM((8, CHUNK, FEAT), F32),
            pltpu.VMEM((8, CHUNK, FEAT), F32),
            dma((2,)),
            dma((4,)),
            dma((4,)),
            dma((4,)),
            dma((2,)),
            dma((4,)),
            dma((4,)),
            dma((3, 3)),
            dma((3, 3)),
            dma((2,)),
            dma((2, 4)),
            dma((3,)),
            dma((3,)),
            dma,
            dma((TILES,)),
            dma,
            dma,
            dma,
        ],
        compiler_params=pltpu.CompilerParams(
            collective_id=0, has_side_effects=True, vmem_limit_bytes=58 * 1024 * 1024
        ),
    )(support, support_labels, targets.reshape(TILES, TILE, FEAT), target_labels)
    return pl.pallas_call(
        part_outputs,
        out_shape=(
            jax.ShapeDtypeStruct((classes, CHUNK), F32),
            jax.ShapeDtypeStruct((CHUNK, FEAT), F32),
        ),
        in_specs=[vmem],
        out_specs=(vmem, vmem),
    )(joint)


def solution(mesh):
    in_specs = (P(("row", "col"), None), P(None, ("row", "col")), P("col", None), P(None, "col"))
    out_specs = (P(None, ("row", "col")), P(("row", "col"), None))
    return jax.shard_map(body, mesh=mesh, in_specs=in_specs, out_specs=out_specs, check_vma=False)
```

```python
import jax
import jax.numpy as jnp
from jax import lax
from jax.experimental import pallas as pl
from jax.experimental.pallas import tpu as pltpu
from jax.sharding import PartitionSpec as P

MESH = pl.DeviceIdType.MESH
F32 = jnp.float32
BF16 = jnp.bfloat16

CHUNK = 64
FEAT = 256
TILE = 256
TILES = 32
GROUP = 16
WIDE = GROUP * CHUNK
HALF = WIDE // 2
RIDGE = 0.5
FILL = (2, 2, 8, 16)
NN = (((1,), (0,)), ((), ()))
NT = (((1,), (1,)), ((), ()))


def dot(a, b, dims=NN):
    return lax.dot_general(a, b, dims, preferred_element_type=F32)


def split3(v):
    hi = v.astype(BF16)
    rest = v - hi.astype(F32)
    mid = rest.astype(BF16)
    low = (rest - mid.astype(F32)).astype(BF16)
    return hi, mid, low


def row_norms(rows):
    square = jnp.square(rows.astype(F32))
    hi = square.astype(BF16)
    low = (square - hi.astype(F32)).astype(BF16)
    ones = jnp.ones((8, FEAT), BF16)
    return 0.5 * (dot(ones, hi, NT) + dot(ones, low, NT))[0:1, :]


def column_norms(rows):
    return 0.5 * jnp.sum(jnp.square(rows.astype(F32)), axis=1, keepdims=True)


def pack_pair(v):
    left = lax.broadcasted_iota(jnp.int32, (8, 128), 1) < CHUNK
    top, bottom = v[0:8], v[8:16]
    first = jnp.where(left, top, pltpu.roll(bottom, CHUNK, 1))
    second = jnp.where(left, pltpu.roll(top, CHUNK, 1), bottom)
    return first, second


def unpack_pair(a, b):
    left = lax.broadcasted_iota(jnp.int32, (8, 128), 1) < CHUNK
    top = jnp.where(left, a, pltpu.roll(b, CHUNK, 1))
    bottom = jnp.where(left, pltpu.roll(a, CHUNK, 1), b)
    return jnp.concatenate([top, bottom], axis=0)


def unpack(ref):
    wide = jnp.concatenate([unpack_pair(ref[2 * j], ref[2 * j + 1]) for j in range(GROUP // 2)], axis=1)
    return jnp.where(lax.broadcasted_iota(jnp.int32, wide.shape, 0) < 15, wide, 0.0)


def gray(j):
    return j + (j // 2) * (5 - 2 * j)


def to_lanes(q, shift):
    sub = lax.broadcasted_iota(jnp.int32, (16, 128), 0)
    lane = lax.broadcasted_iota(jnp.int32, (16, 128), 1)
    return jnp.sum(jnp.where(lane == sub + shift, q, 0.0), axis=0, keepdims=True)


def from_lanes(row, shift):
    sub = lax.broadcasted_iota(jnp.int32, (16, 128), 0)
    lane = lax.broadcasted_iota(jnp.int32, (16, 128), 1)
    return jnp.sum(jnp.where(lane == sub + shift, row, 0.0), axis=1, keepdims=True)


def put_scalars(message, row):
    sub = lax.broadcasted_iota(jnp.int32, (8, 128), 0)
    lane = lax.broadcasted_iota(jnp.int32, (8, 128), 1)
    return jnp.where((sub == 7) & (lane >= CHUNK), row, message)


def lane_sum(v):
    return jnp.sum(v, axis=1, keepdims=True)


def ratio(a, b):
    real = lax.broadcasted_iota(jnp.int32, (16, 1), 0) < 15
    return jnp.where(real, a, 0.0) / jnp.where(real, b, 1.0)


def tree(values):
    values = list(values)
    while len(values) > 1:
        values = [values[i] + values[i + 1] if i + 1 < len(values) else values[i] for i in range(0, len(values), 2)]
    return values[0]


def kernel(
    sup_ref, lab_ref, tgt_hbm, tlab_hbm,
    out_ref,
    tgt, tlab, sup_v, lab_v, rf, cf, lab_rows, lab_cols, rn_ref, sn_ref, tn_ref,
    kt_hi, kt_lo, kk_hi, kk_lo,
    s1_send, s1_recv, s2_send, s2_rows, s2_cols, t_send, t_rows, t_cols,
    drow, rrow, xrow, dcol, rcol, prev,
    three, one, both, own2, sib_send, sib_recv, sib_send2, sib_recv2, u_send, u_recv, w_send, w_recv, pred_send, pred_recv, err_own, err, xt, gsum, csum, g_send, g_recv,
    local_sems, f_send, z_recv, x_recv, r_recv, l_send, l_recv, v_send, v_recv,
    sib_ss, sib_rs, pred_ss, pred_rs, err_ss, err_rs, pass_ss, g_ss, g_rs,
):
    r = lax.axis_index("row")
    c = lax.axis_index("col")
    chip, core = r // 2, lax.rem(r, 2)
    z, x = chip // 4, lax.rem(chip, 4)
    zl, y = c // 4, lax.rem(c, 4)
    me = core * 8 + c
    here = x * 4 + z

    def device(pz, px):
        return (2 * (pz * 4 + px) + core, c)

    xs = [lax.rem(x + d, 4) for d in range(4)]
    zs = [lax.rem(z + d, 4) for d in range(4)]
    ys = [lax.rem(y + d, 4) for d in range(4)]
    ls = [zl, 1 - zl]
    ks = [core, 1 - core]

    def row_peer(j):
        k, p = ks[j % 2], ls[j // 8] * 4 + ys[gray((j // 2) % 4)]
        return k * 8 + p, (2 * chip + k, p)

    def col_peer(j):
        return (2 * (zs[gray(j // 4)] * 4 + xs[gray(j % 4)]) + core, c)

    def tile_at(j):
        j = jnp.int32(j)
        chip_there = lax.rem(z + gray(j // 8), 4) * 4 + lax.rem(x + gray((j // 2) % 4), 4)
        return 2 * chip_there + lax.rem(core + j % 2, 2)

    def far_first(count, act):
        for j in range(count - 1, 0, -1):
            act(j)

    tgt_copy = pltpu.make_async_copy(tgt_hbm, tgt, local_sems.at[0])
    tgt_copy.start()
    start_lane = pl.multiple_of(r * TILE, TILE)
    tlab_copy = pltpu.make_async_copy(tlab_hbm.at[:, pl.ds(start_lane, TILE)], tlab, local_sems.at[1])
    tlab_copy.start()

    barrier = pltpu.get_barrier_semaphore()
    far_first(4, lambda j: pl.semaphore_signal(barrier, inc=1, device_id=device(zs[j], x), device_id_type=MESH))
    far_first(4, lambda j: pl.semaphore_signal(barrier, inc=1, device_id=device(z, xs[j]), device_id_type=MESH))
    far_first(
        GROUP, lambda j: pl.semaphore_signal(barrier, inc=1, device_id=row_peer(j)[1], device_id_type=MESH)
    )

    lab = jnp.concatenate([lab_ref[...], jnp.zeros((1, CHUNK), F32)], axis=0)
    lab_v[...] = jnp.concatenate([lab[0:8], lab[8:16]], axis=1)
    sup = sup_ref[...]
    sup_v[...] = sup
    rf[me] = sup
    cf[here] = sup
    lab_rows[me] = lab_v[...]
    lab_cols[here] = lab_v[...]

    pl.semaphore_wait(barrier, 21)

    drains = []

    def remote(src, dst, ss, rs, to):
        return pltpu.make_async_remote_copy(
            src_ref=src, dst_ref=dst, send_sem=ss, recv_sem=rs, device_id=to, device_id_type=MESH
        )

    def wait_for(ref, sem):
        pltpu.make_async_copy(ref, ref, sem).wait()

    def to_x(dz):
        slot = xs[0] * 4 + zs[dz]
        for d in (2, 1, 3):
            remote(cf.at[slot], cf.at[slot], f_send.at[2], x_recv.at[x], device(z, xs[d])).start()

    col_peers = [(r, ls[j // 4] * 4 + ys[gray(j % 4)]) for j in range(8)]
    for d in (2, 3, 1):
        remote(sup_v, cf.at[here], f_send.at[0], z_recv.at[z], device(zs[d], x)).start()
    to_x(0)
    for j in range(7, 0, -1):
        remote(sup_v, rf.at[me], f_send.at[1], r_recv.at[0], col_peers[j]).start()
    for d in (2, 3, 1):
        remote(lab_v, lab_cols.at[here], l_send.at[0], l_recv.at[0], device(zs[d], x)).start()
    for j in range(7, 0, -1):
        remote(lab_v, lab_rows.at[me], l_send.at[1], l_recv.at[1], col_peers[j]).start()

    tgt_copy.wait()

    @pl.loop(0, TILES // 2)
    def _(i):
        tn_ref[2 * i] = row_norms(tgt[2 * i])
        tn_ref[2 * i + 1] = row_norms(tgt[2 * i + 1])

    for d in (1, 3):
        wait_for(cf.at[0], z_recv.at[zs[d]])
        to_x(d)
    wait_for(cf.at[0], z_recv.at[zs[2]])
    to_x(2)

    block = pl.ds(core * 8, 8)
    other = 2 * chip + 1 - core
    wait_for(rf.at[pl.ds(0, 7)], r_recv.at[0])
    remote(rf.at[block], rf.at[block], f_send.at[3], r_recv.at[1], (other, c)).start()
    wait_for(lab_cols.at[pl.ds(0, 3)], l_recv.at[0])
    for d in (2, 3, 1):
        four = lab_cols.at[pl.ds(x * 4, 4)]
        remote(four, four, l_send.at[2], l_recv.at[2], device(z, xs[d])).start()
    wait_for(lab_rows.at[pl.ds(0, 7)], l_recv.at[1])
    remote(lab_rows.at[block], lab_rows.at[block], l_send.at[3], l_recv.at[3], (other, c)).start()

    drains.append((cf.at[pl.ds(0, 3)], f_send.at[0]))
    drains.append((rf.at[pl.ds(0, 7)], f_send.at[1]))
    drains.append((cf.at[pl.ds(0, 12)], f_send.at[2]))
    drains.append((rf.at[pl.ds(0, 8)], f_send.at[3]))
    drains.append((lab_cols.at[pl.ds(0, 3)], l_send.at[0]))
    drains.append((lab_rows.at[pl.ds(0, 7)], l_send.at[1]))
    drains.append((lab_cols.at[pl.ds(0, 12)], l_send.at[2]))
    drains.append((lab_rows.at[pl.ds(0, 8)], l_send.at[3]))

    half = pl.ds(pl.multiple_of(core * HALF, HALF), HALF)
    sn_ref[...] = column_norms(rf[block].reshape(HALF, FEAT))

    def target_tile(i):
        rows = tgt[i]
        inner = dot(rf[block].reshape(HALF, FEAT), rows, NT)
        value = jnp.exp(inner - sn_ref[...] - tn_ref[i])
        hi = value.astype(BF16)
        kk_hi[i] = hi
        kk_lo[i] = (value - hi.astype(F32)).astype(BF16)

    done = [0]

    def fill(count):
        stop = min(TILES, done[0] + count)
        if stop > done[0]:

            @pl.loop(done[0] // 2, stop // 2)
            def _(i):
                target_tile(2 * i)
                target_tile(2 * i + 1)

        done[0] = stop

    fill(FILL[0])

    wait_for(rf.at[pl.ds(0, 8)], r_recv.at[1])
    rn_ref[...] = row_norms(rf[...].reshape(WIDE, FEAT))

    def system_block(d):
        px = xs[d]
        if d:
            wait_for(cf.at[pl.ds(0, 4)], x_recv.at[px])
        part = cf[pl.ds(px * 4, 4)].reshape(TILE, FEAT)
        inner = dot(part, rf[...].reshape(WIDE, FEAT), NT)
        value = jnp.exp(inner - column_norms(part) - rn_ref[...])
        hi = value.astype(BF16)
        where = pl.ds(pl.multiple_of(px * TILE, TILE), TILE)
        kt_hi[where, :] = hi
        kt_lo[where, :] = (value - hi.astype(F32)).astype(BF16)

    system_block(0)
    fill(FILL[1])
    for d in (1, 3, 2):
        system_block(d)

    def apply_tile(v):
        hi, mid, low = split3(v)
        big = dot(jnp.concatenate([hi, mid, low], axis=0), kt_hi[...])
        small = dot(jnp.concatenate([hi, mid], axis=0), kt_lo[...])
        return (big[0:16] + small[0:16]) + ((big[16:32] + small[16:32]) + big[32:48])

    wait_for(lab_cols.at[pl.ds(0, 12)], l_recv.at[2])
    b_cols = unpack(lab_cols)
    wait_for(lab_rows.at[pl.ds(0, 8)], l_recv.at[3])
    b_rows = unpack(lab_rows)
    drow[...] = b_rows
    rrow[...] = b_rows
    xrow[...] = jnp.zeros_like(b_rows)
    dcol[...] = b_cols
    rcol[...] = b_cols
    rr = None

    def predict_tile(t, parts, count):
        m = 16 * count
        big = dot(parts[...], kk_hi[t])
        small = dot(parts[0:2 * m, :], kk_lo[t])
        return (big[0:m] + small[0:m]) + ((big[m:2 * m] + small[m:2 * m]) + big[2 * m:3 * m])

    def predict_theirs(parts, count, send, recv, which):
        @pl.loop(0, 4)
        def _(g):
            for k in range(4):
                j = 12 - 4 * g + k
                send[j] = predict_tile(tile_at(2 * j + 1), parts, count)
            quarter = pl.ds(12 - 4 * g, 4)
            remote(send.at[quarter], recv.at[quarter], sib_ss.at[which], sib_rs.at[which, 3 - g], (other, c)).start()

        drains.append((recv, sib_ss.at[which]))

    def predict_own(parts, count, recv, which, store):
        @pl.loop(0, 4)
        def _(g):
            wait_for(recv.at[pl.ds(0, 4)], sib_rs.at[which, 3 - g])
            for k in range(4):
                j = 12 - 4 * g + k
                store[j] = predict_tile(tile_at(2 * j), parts, count) + recv[j]

    def reduce_first(value):
        for k in range(3, -1, -1):
            for q in range(4):
                u_send[k, q] = value(4 * q + k)
            if k > 0:
                remote(u_send.at[k], u_recv.at[x], pred_ss.at[0], pred_rs.at[0], device(z, xs[gray(k)])).start()
            else:
                u_recv[x] = u_send[0]
        drains.append((u_recv.at[pl.ds(0, 3)], pred_ss.at[0]))

    def pass_first():
        wait_for(u_recv.at[pl.ds(0, 3)], pred_rs.at[0])
        for q in range(3, -1, -1):
            value = (u_recv[0, q] + u_recv[1, q]) + (u_recv[2, q] + u_recv[3, q])
            if q > 0:
                w_send[q] = value
                remote(w_send.at[q], w_recv.at[z], pred_ss.at[1], pred_rs.at[1], device(zs[gray(q)], x)).start()
            else:
                w_recv[z] = value
        drains.append((w_recv.at[pl.ds(0, 3)], pred_ss.at[1]))

    def reduce_second(value):
        for j in range(GROUP - 1, 0, -1):
            pred_send[j] = value(j)
            remote(pred_send.at[j], pred_recv.at[chip], pred_ss.at[2], pred_rs.at[2], col_peer(j)).start()
        pred_recv[chip] = value(0)
        drains.append((pred_recv.at[pl.ds(0, 15)], pred_ss.at[2]))

    lane = lax.broadcasted_iota(jnp.int32, (1, 128), 1)
    left_half = lax.broadcasted_iota(jnp.int32, (8, 128), 1) < CHUNK
    for step in range(3):
        first, last = step == 0, step == 2
        norm = lane_sum(rcol[...] * rcol[...])
        applied = apply_tile(rcol[...])
        small_ridge = RIDGE / GROUP
        if first:
            d = drow[...]
            guess = applied
            scalars = to_lanes(lane_sum(d * (applied + small_ridge * d)), CHUNK) + to_lanes(norm, CHUNK + 48)
        else:
            near = ratio(norm * float(GROUP), rr)
            old = drow[...]
            d = rrow[...] + near * old
            guess = applied + near * prev[...]
            by_d = guess + small_ridge * d
            by_old = prev[...] + small_ridge * old
            scalars = to_lanes(lane_sum(d * by_d), CHUNK) + to_lanes(lane_sum(d * by_old + old * by_d), CHUNK + 16)
            scalars = scalars + to_lanes(lane_sum(old * by_old), CHUNK + 32) + to_lanes(norm, CHUNK + 48)
        if last:
            t_send[0] = scalars
            t_rows[me] = scalars
        else:
            for j in range(GROUP // 2):
                a, b = pack_pair(applied[:, 128 * j:128 * (j + 1)])
                s1_send[step, 2 * j] = put_scalars(a, scalars)
                s1_send[step, 2 * j + 1] = put_scalars(b, scalars)
            s1_recv[step, me] = s1_send[step, me]

        def send1(j):
            p, to = row_peer(j)
            src = t_send.at[0] if last else s1_send.at[step, p]
            dst = t_rows.at[me] if last else s1_recv.at[step, me]
            remote(src, dst, v_send.at[step, 0], v_recv.at[step, 0], to).start()

        far_first(GROUP, send1)
        landed = t_rows.at[pl.ds(0, 15)] if last else s1_recv.at[step, pl.ds(0, 15)]
        drains.append((landed, v_send.at[step, 0]))
        if first:
            fill(FILL[2])
        elif not last:
            hi, mid, low = split3(drow[:, half])
            hi2, mid2, low2 = split3(rrow[:, half])
            three[...] = jnp.concatenate([hi, hi2, mid, mid2, low, low2], axis=0)
            fill(TILES)
            predict_theirs(three, 2, sib_send, sib_recv, 0)
        else:
            reduce_first(lambda j: (alpha0 + alpha * beta0) * both[j, 0:16, :] + alpha * both[j, 16:32, :])
            hi, mid, low = split3(rrow[:, half])
            one[...] = jnp.concatenate([hi, mid, low], axis=0)
            predict_theirs(one, 1, sib_send2, sib_recv2, 1)
            predict_own(one, 1, sib_recv2, 1, own2)
        wait_for(landed, v_recv.at[step, 0])
        if last:
            scalar_rows = [t_rows[j] for j in range(GROUP)]
        else:
            scalar_rows = [s1_recv[step, j][7:8] for j in range(GROUP)]
        sums = tree(scalar_rows)
        if first:
            rr = from_lanes(sums, CHUNK + 48)
            share = sums
        else:
            held = (lane >= CHUNK + 48) & (lane < CHUNK + 63)
            under = jnp.where(held, to_lanes(rr, CHUNK + 48), 1.0)
            senders = jnp.concatenate(scalar_rows, axis=0)
            true = jnp.where(held, sums, 0.0) / under
            off = true - jnp.where(held, senders * float(GROUP), 0.0) / under
            off = pltpu.roll(off, 80, 1)
            share = senders + off * (pltpu.roll(senders, 112, 1) + off * pltpu.roll(senders, 96, 1))
            share = jnp.sum(share, axis=0, keepdims=True)
            new = from_lanes(sums, CHUNK + 48)
            beta = ratio(new, rr)
            rr = new
        if last:
            t_send[1] = share
            t_cols[here] = share
        else:
            own = tree([s1_recv[step, j] for j in range(GROUP)])
            if not first:
                own = own + jnp.where(left_half, beta[0:8], beta[8:16]) * s2_send[step - 1]
            own = put_scalars(own, share)
            s2_send[step] = own
            s2_cols[step, here] = own

        def send2(j):
            src = t_send.at[1] if last else s2_send.at[step]
            dst = t_cols.at[here] if last else s2_cols.at[step, here]
            remote(src, dst, v_send.at[step, 1], v_recv.at[step, 1], col_peer(j)).start()

        far_first(GROUP, send2)
        landed = t_cols.at[pl.ds(0, 15)] if last else s2_cols.at[step, pl.ds(0, 15)]
        drains.append((landed, v_send.at[step, 1]))
        if not last:
            s2_rows[step, me] = own

            def send_rows(j):
                remote(
                    s2_send.at[step], s2_rows.at[step, me], v_send.at[step, 2], v_recv.at[step, 2], row_peer(j)[1]
                ).start()

            far_first(GROUP, send_rows)
            drains.append((s2_rows.at[step, pl.ds(0, 15)], v_send.at[step, 2]))
        if last:
            reduce_second(lambda j: own2[j] + beta * (both[j, 16:32, :] + beta0 * both[j, 0:16, :]))
            pass_first()
        if first:
            prev[...] = applied
        else:
            drow[...] = rrow[...] + beta * drow[...]
            if not last:
                prev[...] = applied + beta * prev[...]
                dcol[...] = rcol[...] + beta * dcol[...]
        if first:
            fill(FILL[3])
        elif not last:
            predict_own(three, 2, sib_recv, 0, both)
        wait_for(landed, v_recv.at[step, 1])
        if last:
            total = tree([t_cols[j] for j in range(GROUP)])
        else:
            total = tree([s2_cols[step, j][7:8] for j in range(GROUP)])
        alpha = ratio(rr, from_lanes(total, CHUNK))
        if first:
            alpha0 = alpha
        elif not last:
            beta0 = beta
        if not last:
            rcol[...] = rcol[...] - alpha * (unpack(s2_cols.at[step]) + RIDGE * dcol[...])
            xrow[...] = xrow[...] + alpha * drow[...]
            wait_for(s2_rows.at[step, pl.ds(0, 15)], v_recv.at[step, 2])
            rrow[...] = rrow[...] - alpha * (unpack(s2_rows.at[step]) + RIDGE * drow[...])

    xrow[...] = xrow[...] + alpha * drow[...]
    pair = xrow[:, pl.ds(pl.multiple_of((me // 2) * 128, 128), 128)]
    own_x = jnp.where(lax.rem(me, 2) == 0, pair, pltpu.roll(pair, CHUNK, 1))
    out_ref[CHUNK:CHUNK + 16, 0:128] = own_x
    out_ref[CHUNK:CHUNK + 16, 128:FEAT] = jnp.zeros((16, 128), F32)
    hi, mid, low = split3(xrow[:, half])
    wide = jnp.concatenate([hi.astype(F32), mid.astype(F32), jnp.zeros((96, HALF), F32)], axis=0)
    xt[...] = wide.T[:, 0:32].astype(BF16)
    gsum[...] = jnp.zeros_like(gsum)
    csum[...] = jnp.zeros_like(csum)
    tlab_copy.wait()
    labels = jnp.concatenate([tlab[...], jnp.zeros((1, TILE), F32)], axis=0)

    wait_for(w_recv.at[pl.ds(0, 3)], pred_rs.at[1])
    wait_for(pred_recv.at[pl.ds(0, 15)], pred_rs.at[2])
    predictions = tree([w_recv[j] for j in range(4)]) + alpha * tree([pred_recv[j] for j in range(GROUP)])
    own_err = (predictions - labels).astype(BF16)
    err_own[...] = own_err
    err[r] = own_err

    for j in range(1, GROUP):
        remote(err_own, err.at[r], err_ss, err_rs.at[r], col_peer(j)).start()
    drains.append((err.at[pl.ds(0, 15)], err_ss))

    def add_tiles(tiles):
        part, sums = None, None
        for t in tiles:
            e = err[t]
            mix = dot(xt[...], jnp.concatenate([e, e], axis=0))
            weights = mix.astype(BF16) * kk_hi[t]
            product = dot(weights, tgt[t])
            back = weights.astype(F32)
            back = back[:, 0:128] + back[:, 128:256]
            part = product if part is None else part + product
            sums = back if sums is None else sums + back
        gsum[...] += part
        csum[...] += sums

    def take_own(j):
        t = tile_at(2 * j)

        @pl.when(j > 0)
        def _():
            wait_for(err.at[0], err_rs.at[t])

        remote(err.at[t], err.at[t], pass_ss, err_rs.at[t], (other, c)).start()
        return t

    def take_theirs(j):
        t = tile_at(2 * j + 1)
        wait_for(err.at[0], err_rs.at[t])
        return t

    zero = jnp.int32(0)
    add_tiles([take_own(zero), take_own(zero + 1), take_own(zero + 2), take_own(zero + 3)])

    @pl.loop(1, 4)
    def _(s):
        mine = [take_own(4 * s + k) for k in range(4)]
        add_tiles([take_theirs(4 * s - 4 + k) for k in range(4)] + mine)

    add_tiles([take_theirs(zero + 12 + k) for k in range(4)])
    drains.append((err.at[pl.ds(0, 16)], pass_ss))

    scale = 1.0 / 256.0
    term = (gsum[...] - lane_sum(csum[...]) * rf[block].reshape(HALF, FEAT).astype(F32)) * scale
    g_send[...] = term.reshape(8, CHUNK, FEAT)
    g_recv[c] = g_send[c]

    for j in range(7, 0, -1):
        remote(g_send.at[col_peers[j][1]], g_recv.at[c], g_ss, g_rs, col_peers[j]).start()

    drains.append((g_recv.at[pl.ds(0, 7)], g_ss))
    wait_for(g_recv.at[pl.ds(0, 7)], g_rs)
    out_ref[0:CHUNK, :] = tree([g_recv[j] for j in range(8)])

    for ref, sem in drains:
        wait_for(ref, sem)


def part_outputs(joint_ref, coef_ref, grad_ref):
    coef_ref[...] = joint_ref[CHUNK:CHUNK + 15, 0:CHUNK]
    grad_ref[...] = joint_ref[0:CHUNK, :]


def body(support, support_labels, targets, target_labels):
    classes = support_labels.shape[0]
    vmem = pl.BlockSpec(memory_space=pltpu.VMEM)
    anywhere = pl.BlockSpec(memory_space=pl.ANY)
    dma = pltpu.SemaphoreType.DMA
    joint = pl.pallas_call(
        kernel,
        out_shape=jax.ShapeDtypeStruct((CHUNK + 16, FEAT), F32),
        in_specs=[vmem, vmem, anywhere, anywhere],
        out_specs=vmem,
        scratch_shapes=[
            pltpu.VMEM((TILES, TILE, FEAT), BF16),
            pltpu.VMEM((classes, TILE), F32),
            pltpu.VMEM((CHUNK, FEAT), BF16),
            pltpu.VMEM((8, 128), F32),
            pltpu.VMEM((GROUP, CHUNK, FEAT), BF16),
            pltpu.VMEM((GROUP, CHUNK, FEAT), BF16),
            pltpu.VMEM((GROUP, 8, 128), F32),
            pltpu.VMEM((GROUP, 8, 128), F32),
            pltpu.VMEM((1, WIDE), F32),
            pltpu.VMEM((HALF, 1), F32),
            pltpu.VMEM((TILES, 1, TILE), F32),
            pltpu.VMEM((WIDE, WIDE), BF16),
            pltpu.VMEM((WIDE, WIDE), BF16),
            pltpu.VMEM((TILES, HALF, TILE), BF16),
            pltpu.VMEM((TILES, HALF, TILE), BF16),
            pltpu.VMEM((2, GROUP, 8, 128), F32),
            pltpu.VMEM((2, GROUP, 8, 128), F32),
            pltpu.VMEM((2, 8, 128), F32),
            pltpu.VMEM((2, GROUP, 8, 128), F32),
            pltpu.VMEM((2, GROUP, 8, 128), F32),
            pltpu.VMEM((2, 1, 128), F32),
            pltpu.VMEM((GROUP, 1, 128), F32),
            pltpu.VMEM((GROUP, 1, 128), F32),
            pltpu.VMEM((GROUP, WIDE), F32),
            pltpu.VMEM((GROUP, WIDE), F32),
            pltpu.VMEM((GROUP, WIDE), F32),
            pltpu.VMEM((GROUP, WIDE), F32),
            pltpu.VMEM((GROUP, WIDE), F32),
            pltpu.VMEM((GROUP, WIDE), F32),
            pltpu.VMEM((96, HALF), BF16),
            pltpu.VMEM((48, HALF), BF16),
            pltpu.VMEM((GROUP, 32, TILE), F32),
            pltpu.VMEM((GROUP, 16, TILE), F32),
            pltpu.VMEM((GROUP, 32, TILE), F32),
            pltpu.VMEM((GROUP, 32, TILE), F32),
            pltpu.VMEM((GROUP, 16, TILE), F32),
            pltpu.VMEM((GROUP, 16, TILE), F32),
            pltpu.VMEM((4, 4, 16, TILE), F32),
            pltpu.VMEM((4, 4, 16, TILE), F32),
            pltpu.VMEM((4, 16, TILE), F32),
            pltpu.VMEM((4, 16, TILE), F32),
            pltpu.VMEM((GROUP, 16, TILE), F32),
            pltpu.VMEM((GROUP, 16, TILE), F32),
            pltpu.VMEM((16, TILE), BF16),
            pltpu.VMEM((TILES, 16, TILE), BF16),
            pltpu.VMEM((HALF, 32), BF16),
            pltpu.VMEM((HALF, FEAT), F32),
            pltpu.VMEM((HALF, 128), F32),
            pltpu.VMEM((8, CHUNK, FEAT), F32),
            pltpu.VMEM((8, CHUNK, FEAT), F32),
            dma((2,)),
            dma((4,)),
            dma((4,)),
            dma((4,)),
            dma((2,)),
            dma((4,)),
            dma((4,)),
            dma((3, 3)),
            dma((3, 3)),
            dma((2,)),
            dma((2, 4)),
            dma((3,)),
            dma((3,)),
            dma,
            dma((TILES,)),
            dma,
            dma,
            dma,
        ],
        compiler_params=pltpu.CompilerParams(
            collective_id=0, has_side_effects=True, vmem_limit_bytes=58 * 1024 * 1024
        ),
    )(support, support_labels, targets.reshape(TILES, TILE, FEAT), target_labels)
    return pl.pallas_call(
        part_outputs,
        out_shape=(
            jax.ShapeDtypeStruct((classes, CHUNK), F32),
            jax.ShapeDtypeStruct((CHUNK, FEAT), F32),
        ),
        in_specs=[vmem],
        out_specs=(vmem, vmem),
    )(joint)


def solution(mesh):
    in_specs = (P(("row", "col"), None), P(None, ("row", "col")), P("col", None), P(None, "col"))
    out_specs = (P(None, ("row", "col")), P(("row", "col"), None))
    return jax.shard_map(body, mesh=mesh, in_specs=in_specs, out_specs=out_specs, check_vma=False)
```

```python
import jax
import jax.numpy as jnp
from jax import lax
from jax.experimental import pallas as pl
from jax.experimental.pallas import tpu as pltpu
from jax.sharding import PartitionSpec as P

MESH = pl.DeviceIdType.MESH
F32 = jnp.float32
BF16 = jnp.bfloat16

CHUNK = 64
FEAT = 256
TILE = 256
TILES = 32
GROUP = 16
WIDE = GROUP * CHUNK
HALF = WIDE // 2
RIDGE = 0.5
FILL = (0, 2, 6, 14, 4)
NN = (((1,), (0,)), ((), ()))
NT = (((1,), (1,)), ((), ()))


def dot(a, b, dims=NN):
    return lax.dot_general(a, b, dims, preferred_element_type=F32)


def split3(v):
    hi = v.astype(BF16)
    rest = v - hi.astype(F32)
    mid = rest.astype(BF16)
    low = (rest - mid.astype(F32)).astype(BF16)
    return hi, mid, low


def row_norms(rows):
    square = jnp.square(rows.astype(F32))
    hi = square.astype(BF16)
    low = (square - hi.astype(F32)).astype(BF16)
    ones = jnp.ones((8, FEAT), BF16)
    return 0.5 * (dot(ones, hi, NT) + dot(ones, low, NT))[0:1, :]


def column_norms(rows):
    return 0.5 * jnp.sum(jnp.square(rows.astype(F32)), axis=1, keepdims=True)


def pack_pair(v):
    left = lax.broadcasted_iota(jnp.int32, (8, 128), 1) < CHUNK
    top, bottom = v[0:8], v[8:16]
    first = jnp.where(left, top, pltpu.roll(bottom, CHUNK, 1))
    second = jnp.where(left, pltpu.roll(top, CHUNK, 1), bottom)
    return first, second


def unpack_pair(a, b):
    left = lax.broadcasted_iota(jnp.int32, (8, 128), 1) < CHUNK
    top = jnp.where(left, a, pltpu.roll(b, CHUNK, 1))
    bottom = jnp.where(left, pltpu.roll(a, CHUNK, 1), b)
    return jnp.concatenate([top, bottom], axis=0)


def unpack(ref):
    wide = jnp.concatenate([unpack_pair(ref[2 * j], ref[2 * j + 1]) for j in range(GROUP // 2)], axis=1)
    return jnp.where(lax.broadcasted_iota(jnp.int32, wide.shape, 0) < 15, wide, 0.0)


def gray(j):
    return j + (j // 2) * (5 - 2 * j)


def to_lanes(q, shift):
    sub = lax.broadcasted_iota(jnp.int32, (16, 128), 0)
    lane = lax.broadcasted_iota(jnp.int32, (16, 128), 1)
    return jnp.sum(jnp.where(lane == sub + shift, q, 0.0), axis=0, keepdims=True)


def from_lanes(row, shift):
    sub = lax.broadcasted_iota(jnp.int32, (16, 128), 0)
    lane = lax.broadcasted_iota(jnp.int32, (16, 128), 1)
    return jnp.sum(jnp.where(lane == sub + shift, row, 0.0), axis=1, keepdims=True)


def put_scalars(message, row):
    sub = lax.broadcasted_iota(jnp.int32, (8, 128), 0)
    lane = lax.broadcasted_iota(jnp.int32, (8, 128), 1)
    return jnp.where((sub == 7) & (lane >= CHUNK), row, message)


def lane_sum(v):
    return jnp.sum(v, axis=1, keepdims=True)


def ratio(a, b):
    real = lax.broadcasted_iota(jnp.int32, (16, 1), 0) < 15
    return jnp.where(real, a, 0.0) / jnp.where(real, b, 1.0)


def tree(values):
    values = list(values)
    while len(values) > 1:
        values = [values[i] + values[i + 1] if i + 1 < len(values) else values[i] for i in range(0, len(values), 2)]
    return values[0]


def kernel(
    sup_ref, lab_ref, tgt_hbm, tlab_hbm,
    out_ref,
    tgt, tlab, sup_v, lab_v, rf, cf, lab_rows, lab_cols, rn_ref, sn_ref, tn_ref,
    kt_hi, kt_lo, kk_hi, kk_lo,
    s1_send, s1_recv, s2_send, s2_rows, s2_cols, t_send, t_rows, t_cols,
    drow, rrow, xrow, dcol, rcol, prev,
    three, one, both, own2, sib_send, sib_recv, sib_send2, sib_recv2, u_send, u_recv, w_send, w_recv, pred_send, pred_recv, err_own, err, xt, gsum, csum, g_send, g_recv,
    local_sems, f_send, z_recv, x_recv, r_recv, l_send, l_recv, v_send, v_recv,
    sib_ss, sib_rs, pred_ss, pred_rs, err_ss, err_rs, pass_ss, g_ss, g_rs,
):
    r = lax.axis_index("row")
    c = lax.axis_index("col")
    chip, core = r // 2, lax.rem(r, 2)
    z, x = chip // 4, lax.rem(chip, 4)
    zl, y = c // 4, lax.rem(c, 4)
    me = core * 8 + c
    here = x * 4 + z

    def device(pz, px):
        return (2 * (pz * 4 + px) + core, c)

    xs = [lax.rem(x + d, 4) for d in range(4)]
    zs = [lax.rem(z + d, 4) for d in range(4)]
    ys = [lax.rem(y + d, 4) for d in range(4)]
    ls = [zl, 1 - zl]
    ks = [core, 1 - core]

    def row_peer(j):
        k, p = ks[j % 2], ls[j // 8] * 4 + ys[gray((j // 2) % 4)]
        return k * 8 + p, (2 * chip + k, p)

    def col_peer(j):
        return (2 * (zs[gray(j // 4)] * 4 + xs[gray(j % 4)]) + core, c)

    def tile_at(j):
        j = jnp.int32(j)
        chip_there = lax.rem(z + gray(j // 8), 4) * 4 + lax.rem(x + gray((j // 2) % 4), 4)
        return 2 * chip_there + lax.rem(core + j % 2, 2)

    def far_first(count, act):
        for j in range(count - 1, 0, -1):
            act(j)

    tgt_copy = pltpu.make_async_copy(tgt_hbm, tgt, local_sems.at[0])
    tgt_copy.start()
    start_lane = pl.multiple_of(r * TILE, TILE)
    tlab_copy = pltpu.make_async_copy(tlab_hbm.at[:, pl.ds(start_lane, TILE)], tlab, local_sems.at[1])
    tlab_copy.start()

    barrier = pltpu.get_barrier_semaphore()
    far_first(4, lambda j: pl.semaphore_signal(barrier, inc=1, device_id=device(zs[j], x), device_id_type=MESH))
    far_first(4, lambda j: pl.semaphore_signal(barrier, inc=1, device_id=device(z, xs[j]), device_id_type=MESH))
    far_first(
        GROUP, lambda j: pl.semaphore_signal(barrier, inc=1, device_id=row_peer(j)[1], device_id_type=MESH)
    )

    lab = jnp.concatenate([lab_ref[...], jnp.zeros((1, CHUNK), F32)], axis=0)
    lab_v[...] = jnp.concatenate([lab[0:8], lab[8:16]], axis=1)
    sup = sup_ref[...]
    sup_v[...] = sup
    rf[me] = sup
    cf[here] = sup
    lab_rows[me] = lab_v[...]
    lab_cols[here] = lab_v[...]

    pl.semaphore_wait(barrier, 21)

    drains = []

    def remote(src, dst, ss, rs, to):
        return pltpu.make_async_remote_copy(
            src_ref=src, dst_ref=dst, send_sem=ss, recv_sem=rs, device_id=to, device_id_type=MESH
        )

    def wait_for(ref, sem):
        pltpu.make_async_copy(ref, ref, sem).wait()

    def to_x(dz):
        slot = xs[0] * 4 + zs[dz]
        for d in (2, 1, 3):
            remote(cf.at[slot], cf.at[slot], f_send.at[2], x_recv.at[x], device(z, xs[d])).start()

    col_peers = [(r, ls[j // 4] * 4 + ys[gray(j % 4)]) for j in range(8)]
    for d in (2, 3, 1):
        remote(sup_v, cf.at[here], f_send.at[0], z_recv.at[z], device(zs[d], x)).start()
    to_x(0)
    for j in range(7, 0, -1):
        remote(sup_v, rf.at[me], f_send.at[1], r_recv.at[0], col_peers[j]).start()
    for d in (2, 3, 1):
        remote(lab_v, lab_cols.at[here], l_send.at[0], l_recv.at[0], device(zs[d], x)).start()
    for j in range(7, 0, -1):
        remote(lab_v, lab_rows.at[me], l_send.at[1], l_recv.at[1], col_peers[j]).start()

    tgt_copy.wait()

    @pl.loop(0, TILES // 2)
    def _(i):
        tn_ref[2 * i] = row_norms(tgt[2 * i])
        tn_ref[2 * i + 1] = row_norms(tgt[2 * i + 1])

    for d in (1, 3):
        wait_for(cf.at[0], z_recv.at[zs[d]])
        to_x(d)
    wait_for(cf.at[0], z_recv.at[zs[2]])
    to_x(2)

    block = pl.ds(core * 8, 8)
    other = 2 * chip + 1 - core
    wait_for(rf.at[pl.ds(0, 7)], r_recv.at[0])
    remote(rf.at[block], rf.at[block], f_send.at[3], r_recv.at[1], (other, c)).start()
    wait_for(lab_cols.at[pl.ds(0, 3)], l_recv.at[0])
    for d in (2, 3, 1):
        four = lab_cols.at[pl.ds(x * 4, 4)]
        remote(four, four, l_send.at[2], l_recv.at[2], device(z, xs[d])).start()
    wait_for(lab_rows.at[pl.ds(0, 7)], l_recv.at[1])
    remote(lab_rows.at[block], lab_rows.at[block], l_send.at[3], l_recv.at[3], (other, c)).start()

    drains.append((cf.at[pl.ds(0, 3)], f_send.at[0]))
    drains.append((rf.at[pl.ds(0, 7)], f_send.at[1]))
    drains.append((cf.at[pl.ds(0, 12)], f_send.at[2]))
    drains.append((rf.at[pl.ds(0, 8)], f_send.at[3]))
    drains.append((lab_cols.at[pl.ds(0, 3)], l_send.at[0]))
    drains.append((lab_rows.at[pl.ds(0, 7)], l_send.at[1]))
    drains.append((lab_cols.at[pl.ds(0, 12)], l_send.at[2]))
    drains.append((lab_rows.at[pl.ds(0, 8)], l_send.at[3]))

    half = pl.ds(pl.multiple_of(core * HALF, HALF), HALF)
    sn_ref[...] = column_norms(rf[block].reshape(HALF, FEAT))

    def target_tile(n):
        own = n // GROUP
        i = 2 * (n - GROUP * own) + (1 - core) + own * (2 * core - 1)
        rows = tgt[i]
        inner = dot(rf[block].reshape(HALF, FEAT), rows, NT)
        value = jnp.exp(inner - sn_ref[...] - tn_ref[i])
        hi = value.astype(BF16)
        kk_hi[i] = hi
        kk_lo[i] = (value - hi.astype(F32)).astype(BF16)

    done = [0]

    def fill(count):
        stop = min(TILES, done[0] + count)
        if stop > done[0]:

            @pl.loop(done[0] // 2, stop // 2)
            def _(i):
                target_tile(2 * i)
                target_tile(2 * i + 1)

        done[0] = stop

    fill(FILL[0])

    wait_for(rf.at[pl.ds(0, 8)], r_recv.at[1])
    rn_ref[...] = row_norms(rf[...].reshape(WIDE, FEAT))

    def system_block(d):
        px = xs[d]
        if d:
            wait_for(cf.at[pl.ds(0, 4)], x_recv.at[px])
        part = cf[pl.ds(px * 4, 4)].reshape(TILE, FEAT)
        inner = dot(part, rf[...].reshape(WIDE, FEAT), NT)
        value = jnp.exp(inner - column_norms(part) - rn_ref[...])
        hi = value.astype(BF16)
        where = pl.ds(pl.multiple_of(px * TILE, TILE), TILE)
        kt_hi[where, :] = hi
        kt_lo[where, :] = (value - hi.astype(F32)).astype(BF16)

    system_block(0)
    fill(FILL[1])
    for d in (1, 3, 2):
        system_block(d)

    def apply_tile(v):
        hi, mid, low = split3(v)
        big = dot(jnp.concatenate([hi, mid, low], axis=0), kt_hi[...])
        small = dot(jnp.concatenate([hi, mid], axis=0), kt_lo[...])
        return (big[0:16] + small[0:16]) + ((big[16:32] + small[16:32]) + big[32:48])

    wait_for(lab_cols.at[pl.ds(0, 12)], l_recv.at[2])
    b_cols = unpack(lab_cols)
    wait_for(lab_rows.at[pl.ds(0, 8)], l_recv.at[3])
    b_rows = unpack(lab_rows)
    drow[...] = b_rows
    rrow[...] = b_rows
    xrow[...] = jnp.zeros_like(b_rows)
    dcol[...] = b_cols
    rcol[...] = b_cols
    rr = None

    def predict_tile(t, parts, count):
        m = 16 * count
        big = dot(parts[...], kk_hi[t])
        small = dot(parts[0:2 * m, :], kk_lo[t])
        return (big[0:m] + small[0:m]) + ((big[m:2 * m] + small[m:2 * m]) + big[2 * m:3 * m])

    def predict_theirs(parts, count, send, recv, which):
        @pl.loop(0, 4)
        def _(g):
            for k in range(4):
                j = 12 - 4 * g + k
                send[j] = predict_tile(tile_at(2 * j + 1), parts, count)
            quarter = pl.ds(12 - 4 * g, 4)
            remote(send.at[quarter], recv.at[quarter], sib_ss.at[which], sib_rs.at[which, 3 - g], (other, c)).start()

        drains.append((recv, sib_ss.at[which]))

    def predict_own(parts, count, recv, which, store):
        @pl.loop(0, 4)
        def _(g):
            wait_for(recv.at[pl.ds(0, 4)], sib_rs.at[which, 3 - g])
            for k in range(4):
                j = 12 - 4 * g + k
                store[j] = predict_tile(tile_at(2 * j), parts, count) + recv[j]

    def reduce_first(value):
        for k in range(3, -1, -1):
            for q in range(4):
                u_send[k, q] = value(4 * q + k)
            if k > 0:
                remote(u_send.at[k], u_recv.at[x], pred_ss.at[0], pred_rs.at[0], device(z, xs[gray(k)])).start()
            else:
                u_recv[x] = u_send[0]
        drains.append((u_recv.at[pl.ds(0, 3)], pred_ss.at[0]))

    def pass_first():
        wait_for(u_recv.at[pl.ds(0, 3)], pred_rs.at[0])
        for q in range(3, -1, -1):
            value = (u_recv[0, q] + u_recv[1, q]) + (u_recv[2, q] + u_recv[3, q])
            if q > 0:
                w_send[q] = value
                remote(w_send.at[q], w_recv.at[z], pred_ss.at[1], pred_rs.at[1], device(zs[gray(q)], x)).start()
            else:
                w_recv[z] = value
        drains.append((w_recv.at[pl.ds(0, 3)], pred_ss.at[1]))

    def reduce_second(value):
        for j in range(GROUP - 1, 0, -1):
            pred_send[j] = value(j)
            remote(pred_send.at[j], pred_recv.at[chip], pred_ss.at[2], pred_rs.at[2], col_peer(j)).start()
        pred_recv[chip] = value(0)
        drains.append((pred_recv.at[pl.ds(0, 15)], pred_ss.at[2]))

    lane = lax.broadcasted_iota(jnp.int32, (1, 128), 1)
    left_half = lax.broadcasted_iota(jnp.int32, (8, 128), 1) < CHUNK
    for step in range(3):
        first, last = step == 0, step == 2
        norm = lane_sum(rcol[...] * rcol[...])
        applied = apply_tile(rcol[...])
        small_ridge = RIDGE / GROUP
        if first:
            d = drow[...]
            guess = applied
            scalars = to_lanes(lane_sum(d * (applied + small_ridge * d)), CHUNK) + to_lanes(norm, CHUNK + 48)
        else:
            near = ratio(norm * float(GROUP), rr)
            old = drow[...]
            d = rrow[...] + near * old
            guess = applied + near * prev[...]
            by_d = guess + small_ridge * d
            by_old = prev[...] + small_ridge * old
            scalars = to_lanes(lane_sum(d * by_d), CHUNK) + to_lanes(lane_sum(d * by_old + old * by_d), CHUNK + 16)
            scalars = scalars + to_lanes(lane_sum(old * by_old), CHUNK + 32) + to_lanes(norm, CHUNK + 48)
        if last:
            t_send[0] = scalars
            t_rows[me] = scalars
        else:
            for j in range(GROUP // 2):
                a, b = pack_pair(applied[:, 128 * j:128 * (j + 1)])
                s1_send[step, 2 * j] = put_scalars(a, scalars)
                s1_send[step, 2 * j + 1] = put_scalars(b, scalars)
            s1_recv[step, me] = s1_send[step, me]

        def send1(j):
            p, to = row_peer(j)
            src = t_send.at[0] if last else s1_send.at[step, p]
            dst = t_rows.at[me] if last else s1_recv.at[step, me]
            remote(src, dst, v_send.at[step, 0], v_recv.at[step, 0], to).start()

        far_first(GROUP, send1)
        landed = t_rows.at[pl.ds(0, 15)] if last else s1_recv.at[step, pl.ds(0, 15)]
        drains.append((landed, v_send.at[step, 0]))
        if first:
            fill(FILL[2])
        elif not last:
            hi, mid, low = split3(drow[:, half])
            hi2, mid2, low2 = split3(rrow[:, half])
            three[...] = jnp.concatenate([hi, hi2, mid, mid2, low, low2], axis=0)
            fill(FILL[4])
            predict_theirs(three, 2, sib_send, sib_recv, 0)
        else:
            reduce_first(lambda j: (alpha0 + alpha * beta0) * both[j, 0:16, :] + alpha * both[j, 16:32, :])
            hi, mid, low = split3(rrow[:, half])
            one[...] = jnp.concatenate([hi, mid, low], axis=0)
            predict_theirs(one, 1, sib_send2, sib_recv2, 1)
            predict_own(one, 1, sib_recv2, 1, own2)
        wait_for(landed, v_recv.at[step, 0])
        if last:
            scalar_rows = [t_rows[j] for j in range(GROUP)]
        else:
            scalar_rows = [s1_recv[step, j][7:8] for j in range(GROUP)]
        sums = tree(scalar_rows)
        if first:
            rr = from_lanes(sums, CHUNK + 48)
            share = sums
        else:
            held = (lane >= CHUNK + 48) & (lane < CHUNK + 63)
            under = jnp.where(held, to_lanes(rr, CHUNK + 48), 1.0)
            senders = jnp.concatenate(scalar_rows, axis=0)
            true = jnp.where(held, sums, 0.0) / under
            off = true - jnp.where(held, senders * float(GROUP), 0.0) / under
            off = pltpu.roll(off, 80, 1)
            share = senders + off * (pltpu.roll(senders, 112, 1) + off * pltpu.roll(senders, 96, 1))
            share = jnp.sum(share, axis=0, keepdims=True)
            new = from_lanes(sums, CHUNK + 48)
            beta = ratio(new, rr)
            rr = new
        if last:
            t_send[1] = share
            t_cols[here] = share
        else:
            own = tree([s1_recv[step, j] for j in range(GROUP)])
            if not first:
                own = own + jnp.where(left_half, beta[0:8], beta[8:16]) * s2_send[step - 1]
            own = put_scalars(own, share)
            s2_send[step] = own
            s2_cols[step, here] = own

        def send2(j):
            src = t_send.at[1] if last else s2_send.at[step]
            dst = t_cols.at[here] if last else s2_cols.at[step, here]
            remote(src, dst, v_send.at[step, 1], v_recv.at[step, 1], col_peer(j)).start()

        far_first(GROUP, send2)
        landed = t_cols.at[pl.ds(0, 15)] if last else s2_cols.at[step, pl.ds(0, 15)]
        drains.append((landed, v_send.at[step, 1]))
        if not last:
            s2_rows[step, me] = own

            def send_rows(j):
                remote(
                    s2_send.at[step], s2_rows.at[step, me], v_send.at[step, 2], v_recv.at[step, 2], row_peer(j)[1]
                ).start()

            far_first(GROUP, send_rows)
            drains.append((s2_rows.at[step, pl.ds(0, 15)], v_send.at[step, 2]))
        if last:
            reduce_second(lambda j: own2[j] + beta * (both[j, 16:32, :] + beta0 * both[j, 0:16, :]))
            pass_first()
        if first:
            prev[...] = applied
        else:
            drow[...] = rrow[...] + beta * drow[...]
            if not last:
                prev[...] = applied + beta * prev[...]
                dcol[...] = rcol[...] + beta * dcol[...]
        if first:
            fill(FILL[3])
        elif not last:
            fill(TILES)
            predict_own(three, 2, sib_recv, 0, both)
        wait_for(landed, v_recv.at[step, 1])
        if last:
            total = tree([t_cols[j] for j in range(GROUP)])
        else:
            total = tree([s2_cols[step, j][7:8] for j in range(GROUP)])
        alpha = ratio(rr, from_lanes(total, CHUNK))
        if first:
            alpha0 = alpha
        elif not last:
            beta0 = beta
        if not last:
            rcol[...] = rcol[...] - alpha * (unpack(s2_cols.at[step]) + RIDGE * dcol[...])
            xrow[...] = xrow[...] + alpha * drow[...]
            wait_for(s2_rows.at[step, pl.ds(0, 15)], v_recv.at[step, 2])
            rrow[...] = rrow[...] - alpha * (unpack(s2_rows.at[step]) + RIDGE * drow[...])

    xrow[...] = xrow[...] + alpha * drow[...]
    pair = xrow[:, pl.ds(pl.multiple_of((me // 2) * 128, 128), 128)]
    own_x = jnp.where(lax.rem(me, 2) == 0, pair, pltpu.roll(pair, CHUNK, 1))
    out_ref[CHUNK:CHUNK + 16, 0:128] = own_x
    out_ref[CHUNK:CHUNK + 16, 128:FEAT] = jnp.zeros((16, 128), F32)
    hi, mid, low = split3(xrow[:, half])
    wide = jnp.concatenate([hi.astype(F32), mid.astype(F32), jnp.zeros((96, HALF), F32)], axis=0)
    xt[...] = wide.T[:, 0:32].astype(BF16)
    gsum[...] = jnp.zeros_like(gsum)
    csum[...] = jnp.zeros_like(csum)
    tlab_copy.wait()
    labels = jnp.concatenate([tlab[...], jnp.zeros((1, TILE), F32)], axis=0)

    wait_for(w_recv.at[pl.ds(0, 3)], pred_rs.at[1])
    wait_for(pred_recv.at[pl.ds(0, 15)], pred_rs.at[2])
    predictions = tree([w_recv[j] for j in range(4)]) + alpha * tree([pred_recv[j] for j in range(GROUP)])
    own_err = (predictions - labels).astype(BF16)
    err_own[...] = own_err
    err[r] = own_err

    for j in range(1, GROUP):
        remote(err_own, err.at[r], err_ss, err_rs.at[r], col_peer(j)).start()
    drains.append((err.at[pl.ds(0, 15)], err_ss))

    def add_tiles(tiles):
        part, sums = None, None
        for t in tiles:
            e = err[t]
            mix = dot(xt[...], jnp.concatenate([e, e], axis=0))
            weights = mix.astype(BF16) * kk_hi[t]
            product = dot(weights, tgt[t])
            back = weights.astype(F32)
            back = back[:, 0:128] + back[:, 128:256]
            part = product if part is None else part + product
            sums = back if sums is None else sums + back
        gsum[...] += part
        csum[...] += sums

    def take_own(j):
        t = tile_at(2 * j)

        @pl.when(j > 0)
        def _():
            wait_for(err.at[0], err_rs.at[t])

        remote(err.at[t], err.at[t], pass_ss, err_rs.at[t], (other, c)).start()
        return t

    def take_theirs(j):
        t = tile_at(2 * j + 1)
        wait_for(err.at[0], err_rs.at[t])
        return t

    zero = jnp.int32(0)
    add_tiles([take_own(zero), take_own(zero + 1), take_own(zero + 2), take_own(zero + 3)])

    @pl.loop(1, 4)
    def _(s):
        mine = [take_own(4 * s + k) for k in range(4)]
        add_tiles([take_theirs(4 * s - 4 + k) for k in range(4)] + mine)

    add_tiles([take_theirs(zero + 12 + k) for k in range(4)])
    drains.append((err.at[pl.ds(0, 16)], pass_ss))

    scale = 1.0 / 256.0
    term = (gsum[...] - lane_sum(csum[...]) * rf[block].reshape(HALF, FEAT).astype(F32)) * scale
    g_send[...] = term.reshape(8, CHUNK, FEAT)
    g_recv[c] = g_send[c]

    for j in range(7, 0, -1):
        remote(g_send.at[col_peers[j][1]], g_recv.at[c], g_ss, g_rs, col_peers[j]).start()

    drains.append((g_recv.at[pl.ds(0, 7)], g_ss))
    wait_for(g_recv.at[pl.ds(0, 7)], g_rs)
    out_ref[0:CHUNK, :] = tree([g_recv[j] for j in range(8)])

    for ref, sem in drains:
        wait_for(ref, sem)


def part_outputs(joint_ref, coef_ref, grad_ref):
    coef_ref[...] = joint_ref[CHUNK:CHUNK + 15, 0:CHUNK]
    grad_ref[...] = joint_ref[0:CHUNK, :]


def body(support, support_labels, targets, target_labels):
    classes = support_labels.shape[0]
    vmem = pl.BlockSpec(memory_space=pltpu.VMEM)
    anywhere = pl.BlockSpec(memory_space=pl.ANY)
    dma = pltpu.SemaphoreType.DMA
    joint = pl.pallas_call(
        kernel,
        out_shape=jax.ShapeDtypeStruct((CHUNK + 16, FEAT), F32),
        in_specs=[vmem, vmem, anywhere, anywhere],
        out_specs=vmem,
        scratch_shapes=[
            pltpu.VMEM((TILES, TILE, FEAT), BF16),
            pltpu.VMEM((classes, TILE), F32),
            pltpu.VMEM((CHUNK, FEAT), BF16),
            pltpu.VMEM((8, 128), F32),
            pltpu.VMEM((GROUP, CHUNK, FEAT), BF16),
            pltpu.VMEM((GROUP, CHUNK, FEAT), BF16),
            pltpu.VMEM((GROUP, 8, 128), F32),
            pltpu.VMEM((GROUP, 8, 128), F32),
            pltpu.VMEM((1, WIDE), F32),
            pltpu.VMEM((HALF, 1), F32),
            pltpu.VMEM((TILES, 1, TILE), F32),
            pltpu.VMEM((WIDE, WIDE), BF16),
            pltpu.VMEM((WIDE, WIDE), BF16),
            pltpu.VMEM((TILES, HALF, TILE), BF16),
            pltpu.VMEM((TILES, HALF, TILE), BF16),
            pltpu.VMEM((2, GROUP, 8, 128), F32),
            pltpu.VMEM((2, GROUP, 8, 128), F32),
            pltpu.VMEM((2, 8, 128), F32),
            pltpu.VMEM((2, GROUP, 8, 128), F32),
            pltpu.VMEM((2, GROUP, 8, 128), F32),
            pltpu.VMEM((2, 1, 128), F32),
            pltpu.VMEM((GROUP, 1, 128), F32),
            pltpu.VMEM((GROUP, 1, 128), F32),
            pltpu.VMEM((GROUP, WIDE), F32),
            pltpu.VMEM((GROUP, WIDE), F32),
            pltpu.VMEM((GROUP, WIDE), F32),
            pltpu.VMEM((GROUP, WIDE), F32),
            pltpu.VMEM((GROUP, WIDE), F32),
            pltpu.VMEM((GROUP, WIDE), F32),
            pltpu.VMEM((96, HALF), BF16),
            pltpu.VMEM((48, HALF), BF16),
            pltpu.VMEM((GROUP, 32, TILE), F32),
            pltpu.VMEM((GROUP, 16, TILE), F32),
            pltpu.VMEM((GROUP, 32, TILE), F32),
            pltpu.VMEM((GROUP, 32, TILE), F32),
            pltpu.VMEM((GROUP, 16, TILE), F32),
            pltpu.VMEM((GROUP, 16, TILE), F32),
            pltpu.VMEM((4, 4, 16, TILE), F32),
            pltpu.VMEM((4, 4, 16, TILE), F32),
            pltpu.VMEM((4, 16, TILE), F32),
            pltpu.VMEM((4, 16, TILE), F32),
            pltpu.VMEM((GROUP, 16, TILE), F32),
            pltpu.VMEM((GROUP, 16, TILE), F32),
            pltpu.VMEM((16, TILE), BF16),
            pltpu.VMEM((TILES, 16, TILE), BF16),
            pltpu.VMEM((HALF, 32), BF16),
            pltpu.VMEM((HALF, FEAT), F32),
            pltpu.VMEM((HALF, 128), F32),
            pltpu.VMEM((8, CHUNK, FEAT), F32),
            pltpu.VMEM((8, CHUNK, FEAT), F32),
            dma((2,)),
            dma((4,)),
            dma((4,)),
            dma((4,)),
            dma((2,)),
            dma((4,)),
            dma((4,)),
            dma((3, 3)),
            dma((3, 3)),
            dma((2,)),
            dma((2, 4)),
            dma((3,)),
            dma((3,)),
            dma,
            dma((TILES,)),
            dma,
            dma,
            dma,
        ],
        compiler_params=pltpu.CompilerParams(
            collective_id=0, has_side_effects=True, vmem_limit_bytes=58 * 1024 * 1024
        ),
    )(support, support_labels, targets.reshape(TILES, TILE, FEAT), target_labels)
    return pl.pallas_call(
        part_outputs,
        out_shape=(
            jax.ShapeDtypeStruct((classes, CHUNK), F32),
            jax.ShapeDtypeStruct((CHUNK, FEAT), F32),
        ),
        in_specs=[vmem],
        out_specs=(vmem, vmem),
    )(joint)


def solution(mesh):
    in_specs = (P(("row", "col"), None), P(None, ("row", "col")), P("col", None), P(None, "col"))
    out_specs = (P(None, ("row", "col")), P(("row", "col"), None))
    return jax.shard_map(body, mesh=mesh, in_specs=in_specs, out_specs=out_specs, check_vma=False)
```
